32 devices in a mesh: batch: 8 (over y, x, core), fsdp: 4 (over z).
Axes of the slice: x: 2, y: 2, z: 4, core: 2. Of those that a mesh axis runs over, the one named last changes fastest.
Arguments:
- text: bfloat16 [128, 144, 1024], P(('batch', 'fsdp')), may hold values from -6 to 6
- memory: bfloat16 [128, 256, 1024], P(('batch', 'fsdp')), may hold values from -6 to 6
- text_lengths: int32 [128], P(('batch', 'fsdp')), may hold values from 1 to 144, 9216 in all
- memory_mask: int32 [128, 256], P(('batch', 'fsdp')), may hold values 0 or 1
- grad_out: bfloat16 [128, 144, 1024], P(('batch', 'fsdp')), may hold values from -6 to 6
- self_gain: bfloat16 [1024], P('fsdp'), may hold values from 0.5 to 1.5
- self_query: bfloat16 [1024, 1024], P('fsdp'), may hold values from -0.25 to 0.25
- self_key: bfloat16 [1024, 1024], P('fsdp'), may hold values from -0.25 to 0.25
- self_value: bfloat16 [1024, 1024], P('fsdp'), may hold values from -0.1875 to 0.1875
- self_output: bfloat16 [1024, 1024], P('fsdp'), may hold values from -0.5 to 0.5
- cross_gain: bfloat16 [1024], P('fsdp'), may hold values from 0.5 to 1.5
- cross_query: bfloat16 [1024, 1024], P('fsdp'), may hold values from -0.25 to 0.25
- cross_key: bfloat16 [1024, 1024], P('fsdp'), may hold values from -0.25 to 0.25
- cross_value: bfloat16 [1024, 1024], P('fsdp'), may hold values from -0.1875 to 0.1875
- cross_output: bfloat16 [1024, 1024], P('fsdp'), may hold values from -0.5 to 0.5
- mlp_gain: bfloat16 [1024], P('fsdp'), may hold values from 0.5 to 1.5
- mlp_gate: bfloat16 [1024, 2816], P('fsdp'), may hold values from -0.1875 to 0.1875
- mlp_up: bfloat16 [1024, 2816], P('fsdp'), may hold values from -0.1875 to 0.1875
- mlp_down: bfloat16 [2816, 1024], P('fsdp'), may hold values from -0.15625 to 0.15625
Outputs:
- block_out: bfloat16 [128, 144, 1024], P(('batch', 'fsdp'))
- grad_text: float32 [128, 144, 1024], P(('batch', 'fsdp'))
- grad_memory: float32 [128, 256, 1024], P(('batch', 'fsdp'))
- grad_self_gain: float32 [1024], P('fsdp')
- grad_self_query: float32 [1024, 1024], P('fsdp')
- grad_self_key: float32 [1024, 1024], P('fsdp')
- grad_self_value: float32 [1024, 1024], P('fsdp')
- grad_self_output: float32 [1024, 1024], P('fsdp')
- grad_cross_gain: float32 [1024], P('fsdp')
- grad_cross_query: float32 [1024, 1024], P('fsdp')
- grad_cross_key: float32 [1024, 1024], P('fsdp')
- grad_cross_value: float32 [1024, 1024], P('fsdp')
- grad_cross_output: float32 [1024, 1024], P('fsdp')
- grad_mlp_gain: float32 [1024], P('fsdp')
- grad_mlp_gate: float32 [1024, 2816], P('fsdp')
- grad_mlp_up: float32 [1024, 2816], P('fsdp')
- grad_mlp_down: float32 [2816, 1024], P('fsdp')
The draws below stay inside these ranges and needn't reach their ends.
Inputs may be any that keep to these rules, and one draw needn't show every extreme that they name: `text_lengths`: text slots at or past an item's length are padding; they are still computed.
All inputs are finite; a program needn't handle non-finite values. No bound on the sum of `text_lengths` or of `memory_mask` on one device may be relied on, other than what follows from the above.
Results may differ from the reference program's by a relative error of at most 0.028.
Values may be sent and summed in bfloat16 or wider, within the bound.
No kernel may reach another device: no remote copies, remote signals or barrier semaphores. Data moves between devices by JAX's collectives and lax.ppermute only.
A program may use at most 384 MiB of HBM per device.

```python
import math
import jax
import jax.numpy as jnp
import numpy as np
from jax import lax

D = 1024
HEADS = 16
HEAD_DIM = 64
FF = 2816
TEXT = 144
MEM = 256
ITEMS = 128


def with_ends(array, rng, least, high):
    longest = array.shape.index(max(array.shape))
    spots = []
    for shift in (0, 1):
        where = [jax.random.randint(jax.random.fold_in(rng, axis), (), 0, length) for axis, length in enumerate(array.shape)]
        where[longest] = (where[longest] + shift) % array.shape[longest]
        spots.append(tuple(where))
    return array.at[spots[0]].set(least).at[spots[1]].set(high)


def levels(key, dims, pieces, low, high):
    def one(axis_at, shards_of):
        steps = jax.random.uniform(jax.random.fold_in(jax.random.fold_in(key, 6), axis_at), (shards_of,), jnp.float32, low / len(pieces), high / len(pieces))
        return jnp.repeat(jnp.exp(steps), dims[axis_at] // shards_of).reshape((-1,) + (1,) * (len(dims) - axis_at - 1))

    loudness = one(*pieces[0])
    for cut in pieces[1:]:
        loudness = loudness * one(*cut)
    return loudness


def length_profile(amount, total, limit, lean):
    loads = [(1 << 20) // math.isqrt(grade ** lean) + 1 for grade in range(2, amount + 1)]
    rest, counts = total - limit - (amount - 1), [1] * (amount - 1)
    while rest > 0:
        free = [i for i in range(amount - 1) if counts[i] < limit]
        pool, remaining = sum([loads[i] for i in free]), rest
        for i in free:
            extra = min(limit - counts[i], max(1, remaining * loads[i] // pool), rest)
            counts[i] = counts[i] + extra
            rest = rest - extra
    return np.array([limit] + counts)


def ragged_sizes(own_key, number_of, total, most, skew):
    if number_of == 2:
        one = jax.random.randint(own_key, (), max(1, total - most), min(most, total - 1) + 1)
        return jnp.stack([one, total - one])
    sizes = jnp.asarray(length_profile(number_of, total, most, skew), jnp.int32)
    twos = (number_of - 1) // 2
    source_of, sink = sizes[1:1 + 2 * twos:2], sizes[2:2 + 2 * twos:2]
    room = jnp.minimum(source_of - 1, most - sink)
    shifted = jax.random.randint(jax.random.fold_in(own_key, 1), (twos,), 0, 1 << 20) % (room + 1)
    sizes = sizes.at[1:1 + 2 * twos:2].set(source_of - shifted).at[2:2 + 2 * twos:2].set(sink + shifted)
    return sizes[jax.random.permutation(jax.random.fold_in(own_key, 2), number_of)]


def bell_draw(key, shape, width, most, shards=(), kind=jnp.bfloat16):
    values = jax.random.normal(key, shape, jnp.float32) * width
    if len(shards) > 0:
        values = levels(key, shape, shards, -0.22, 0.18) * values
    return jnp.clip(values, min=-most, max=most).astype(kind)


def setup_inputs(seed: int = 0) -> dict:
    seeds = jax.random.split(jax.random.key(seed), 20)
    text = bell_draw(seeds[0], (ITEMS, TEXT, D), 1.0, 6.0, ((0, 32),))
    memory = bell_draw(seeds[1], (ITEMS, MEM, D), 1.0, 6.0, ((0, 32),))
    text_lengths = ragged_sizes(seeds[2], ITEMS, ITEMS * TEXT // 2, TEXT, 2).astype(jnp.int32)
    memory_mask = with_ends((jax.random.randint(seeds[3], (ITEMS, MEM), 0, 4) < 3).astype(jnp.int32), jax.random.fold_in(seeds[3], 1), 0, 1)
    grad_out = bell_draw(seeds[4], (ITEMS, TEXT, D), 1.0, 6.0, ((0, 32),))
    self_gain = jnp.clip(1.0 + 0.1 * jax.random.normal(seeds[5], (D,), jnp.float32), 0.5, 1.5).astype(jnp.bfloat16)
    self_query = bell_draw(seeds[6], (D, D), (D // 2) ** -0.5, 0.25, ((0, 4),))
    self_key = bell_draw(seeds[7], (D, D), (D // 2) ** -0.5, 0.25, ((0, 4),))
    self_value = bell_draw(seeds[8], (D, D), D ** -0.5, 0.1875, ((0, 4),))
    self_output = bell_draw(seeds[9], (D, D), (D // 8) ** -0.5, 0.5, ((0, 4),))
    cross_gain = jnp.clip(1.0 + 0.1 * jax.random.normal(seeds[10], (D,), jnp.float32), 0.5, 1.5).astype(jnp.bfloat16)
    cross_query = bell_draw(seeds[11], (D, D), (D // 2) ** -0.5, 0.25, ((0, 4),))
    cross_key = bell_draw(seeds[12], (D, D), (D // 2) ** -0.5, 0.25, ((0, 4),))
    cross_value = bell_draw(seeds[13], (D, D), D ** -0.5, 0.1875, ((0, 4),))
    cross_output = bell_draw(seeds[14], (D, D), (D // 8) ** -0.5, 0.5, ((0, 4),))
    mlp_gain = jnp.clip(1.0 + 0.1 * jax.random.normal(seeds[15], (D,), jnp.float32), 0.5, 1.5).astype(jnp.bfloat16)
    mlp_gate = bell_draw(seeds[16], (D, FF), D ** -0.5, 0.1875, ((0, 4),))
    mlp_up = bell_draw(seeds[17], (D, FF), D ** -0.5, 0.1875, ((0, 4),))
    mlp_down = bell_draw(seeds[18], (FF, D), (FF // 2) ** -0.5, 0.15625, ((0, 4),))
    return dict(text=text, memory=memory, text_lengths=text_lengths, memory_mask=memory_mask, grad_out=grad_out, self_gain=self_gain, self_query=self_query, self_key=self_key, self_value=self_value, self_output=self_output, cross_gain=cross_gain, cross_query=cross_query, cross_key=cross_key, cross_value=cross_value, cross_output=cross_output, mlp_gain=mlp_gain, mlp_gate=mlp_gate, mlp_up=mlp_up, mlp_down=mlp_down)


highest = lax.Precision.HIGHEST
epsilon = 1e-06

@jax.custom_vjp
def low(v):
    return lax.optimization_barrier(v.astype(jnp.bfloat16)).astype(jnp.float32)

@jax.custom_vjp
def low_back(v):
    return v

def low_keep(v):
    return (low(v), None)

def low_pass(kept, grad):
    return (grad,)

def back_keep(v):
    return (v, None)

def back_low(kept, grad):
    return (low(grad),)
low.defvjp(low_keep, low_pass)
low_back.defvjp(back_keep, back_low)

def normalize(value, gain):
    return value * lax.rsqrt(lax.optimization_barrier(jnp.mean(value * value, axis=-1, keepdims=True)) + epsilon) * gain

def product(left, right):
    return jnp.matmul(left, right, precision=highest)

def rounded(value):
    return low(low_back(value))

def attend(query, keys, values, allowed):
    item_count, query_rows, features = query.shape
    key_rows = keys.shape[1]
    query_heads = query.reshape(item_count, query_rows, HEADS, HEAD_DIM)
    key_heads = keys.reshape(item_count, key_rows, HEADS, HEAD_DIM)
    value_heads = values.reshape(item_count, key_rows, HEADS, HEAD_DIM)
    scores = low_back(jnp.einsum('iqhd,ikhd->ihqk', query_heads, key_heads, precision=highest) * 0.125)
    scores = jnp.where(allowed[:, None], scores, -1e+30)
    row_max = lax.optimization_barrier(jnp.max(scores, axis=-1, keepdims=True))
    lifted = jnp.exp(scores - row_max)
    weights = low(lifted / lax.optimization_barrier(jnp.sum(lifted, axis=-1, keepdims=True)))
    mixed = jnp.einsum('ihqk,ikhd->iqhd', weights, value_heads, precision=highest)
    return rounded(mixed.reshape(item_count, query_rows, features))

def block(text_value, memory_value, lengths, masks, params):
    self_gain, self_query, self_key, self_value, self_output, cross_gain, cross_query, cross_key, cross_value, cross_output, mlp_gain, mlp_gate, mlp_up, mlp_down = params
    text_rows = text_value.shape[1]
    positions = jnp.arange(text_rows, dtype=jnp.int32)
    causal = positions[:, None] >= positions[None, :]
    allowed_self = causal[None] & (positions[None, None, :] < lengths[:, None, None])
    allowed_cross = (masks > 0)[:, None, :]
    normed = low(normalize(text_value, self_gain))
    query = rounded(product(normed, self_query))
    keys = rounded(product(normed, self_key))
    values = rounded(product(normed, self_value))
    mixed = attend(query, keys, values, allowed_self)
    hidden_one = text_value + low_back(product(mixed, self_output))
    normed = low(normalize(hidden_one, cross_gain))
    query = rounded(product(normed, cross_query))
    keys = rounded(product(memory_value, cross_key))
    values = rounded(product(memory_value, cross_value))
    mixed = attend(query, keys, values, allowed_cross)
    hidden_two = hidden_one + low_back(product(mixed, cross_output))
    normed = low(normalize(hidden_two, mlp_gain))
    gate = low_back(product(normed, mlp_gate))
    up_value = low_back(product(normed, mlp_up))
    inner = low(jax.nn.gelu(gate, approximate=True) * up_value)
    return hidden_two + low_back(product(inner, mlp_down))

def reference(text, memory, text_lengths, memory_mask, grad_out, self_gain, self_query, self_key, self_value, self_output, cross_gain, cross_query, cross_key, cross_value, cross_output, mlp_gain, mlp_gate, mlp_up, mlp_down):
    params = tuple((item.astype(jnp.float32) for item in (self_gain, self_query, self_key, self_value, self_output, cross_gain, cross_query, cross_key, cross_value, cross_output, mlp_gain, mlp_gate, mlp_up, mlp_down)))
    group_size = math.gcd(ITEMS, 16)
    group_count = ITEMS // group_size
    lengths = text_lengths.reshape(group_count, group_size)
    masks = memory_mask.reshape(group_count, group_size, MEM)

    def forward(text_value, memory_value, weights):

        def one_group(batch):
            return jax.checkpoint(block)(batch[0], batch[1], batch[2], batch[3], weights)
        outputs = lax.map(one_group, (text_value.reshape(group_count, group_size, TEXT, D), memory_value.reshape(group_count, group_size, MEM, D), lengths, masks))
        return outputs.reshape(ITEMS, TEXT, D)
    result, pullback = jax.vjp(forward, text.astype(jnp.float32), memory.astype(jnp.float32), params)
    grad_text, grad_memory, grads = pullback(grad_out.astype(jnp.float32))
    return (result.astype(jnp.bfloat16), grad_text, grad_memory, grads[0], grads[1], grads[2], grads[3], grads[4], grads[5], grads[6], grads[7], grads[8], grads[9], grads[10], grads[11], grads[12], grads[13])
```

```python
import functools

import jax
import jax.numpy as jnp
from jax import lax
from jax.experimental import pallas as pl
from jax.experimental.pallas import tpu as pltpu
from jax.sharding import PartitionSpec as P

HEAD_DIM = 64
QUAD = 4
WIDE = HEAD_DIM * QUAD
EPSILON = 1e-06
MASKED = -1e30
SCALE = 0.125
VMEM_LIMIT = 56 * 1024 * 1024

BF16 = jnp.bfloat16
F32 = jnp.float32


def params():
    return pltpu.CompilerParams(vmem_limit_bytes=VMEM_LIMIT)


def dot(a, b, dims):
    return lax.dot_general(a, b, (dims, ((), ())), preferred_element_type=F32)


def stack_heads(value):
    lane = lax.broadcasted_iota(jnp.int32, value.shape, 1) // HEAD_DIM
    zero = jnp.zeros_like(value)
    return jnp.concatenate([jnp.where(lane == j, value, zero) for j in range(QUAD)], axis=0)


def join_heads(stacked):
    rows = stacked.shape[0] // QUAD
    lane = lax.broadcasted_iota(jnp.int32, (rows, WIDE), 1) // HEAD_DIM
    out = stacked[:rows]
    for j in range(1, QUAD):
        out = jnp.where(lane == j, stacked[j * rows : (j + 1) * rows], out)
    return out


def causal_mask(rows, keys, length):
    t = lax.broadcasted_iota(jnp.int32, (rows, keys), 0)
    u = lax.broadcasted_iota(jnp.int32, (rows, keys), 1)
    one = (u <= t) & (u < length)
    return jnp.concatenate([one] * QUAD, axis=0)


def forward_quad(q, k, v, allowed):
    stacked = stack_heads(q)
    scores = dot(stacked, k, ((1,), (1,))) * SCALE
    scores = jnp.where(allowed, scores, MASKED)
    top = jnp.max(scores, axis=-1, keepdims=True)
    lifted = jnp.exp(scores - top)
    total = jnp.sum(lifted, axis=-1, keepdims=True)
    probs = (lifted / total).astype(BF16)
    mixed = join_heads(dot(probs, v, ((1,), (0,))))
    return probs, mixed.astype(BF16)


def backward_quad(q, k, v, probs, grad, allowed):
    q_stack = stack_heads(q)
    g_stack = stack_heads(grad)
    grad_v = dot(probs, g_stack, ((0,), (0,)))
    grad_p = dot(g_stack, v, ((1,), (1,)))
    p = probs.astype(F32)
    inner = jnp.sum(grad_p * p, axis=-1, keepdims=True)
    grad_s = p * (grad_p - inner)
    if allowed is not None:
        grad_s = jnp.where(allowed, grad_s, 0.0)
    grad_s = grad_s.astype(BF16)
    grad_q = join_heads(dot(grad_s, k, ((1,), (0,)))) * SCALE
    grad_k = dot(grad_s, q_stack, ((0,), (0,))) * SCALE
    return grad_q.astype(BF16), grad_k.astype(BF16), grad_v.astype(BF16)


def self_forward_kernel(lengths, qkv_ref, o_ref, p_ref):
    rows, width = o_ref.shape[1], o_ref.shape[2]
    allowed = causal_mask(rows, rows, lengths[pl.program_id(0)])
    for h in range(width // WIDE):
        c = h * WIDE
        probs, mixed = forward_quad(
            qkv_ref[0, :, c : c + WIDE],
            qkv_ref[0, :, width + c : width + c + WIDE],
            qkv_ref[0, :, 2 * width + c : 2 * width + c + WIDE],
            allowed,
        )
        o_ref[0, :, c : c + WIDE] = mixed
        p_ref[0, h] = probs


def self_forward(qkv, lengths):
    items, rows, width3 = qkv.shape
    width = width3 // 3
    quads = width // WIDE
    return pl.pallas_call(
        self_forward_kernel,
        grid_spec=pltpu.PrefetchScalarGridSpec(
            num_scalar_prefetch=1,
            grid=(items,),
            in_specs=[pl.BlockSpec((1, rows, width3), lambda i, s: (i, 0, 0))],
            out_specs=[
                pl.BlockSpec((1, rows, width), lambda i, s: (i, 0, 0)),
                pl.BlockSpec((1, quads, QUAD * rows, rows), lambda i, s: (i, 0, 0, 0)),
            ],
        ),
        out_shape=[
            jax.ShapeDtypeStruct((items, rows, width), BF16),
            jax.ShapeDtypeStruct((items, quads, QUAD * rows, rows), BF16),
        ],
        compiler_params=params(),
        cost_estimate=pl.CostEstimate(
            flops=8 * items * quads * QUAD * rows * 256 * 256,
            bytes_accessed=2 * items * rows * (4 * width + 16 * rows),
            transcendentals=0,
        ),
    )(lengths, qkv)


def self_backward_kernel(qkv_ref, p_ref, g_ref, d_ref):
    width = g_ref.shape[2]
    for h in range(width // WIDE):
        c = h * WIDE
        grad_q, grad_k, grad_v = backward_quad(
            qkv_ref[0, :, c : c + WIDE],
            qkv_ref[0, :, width + c : width + c + WIDE],
            qkv_ref[0, :, 2 * width + c : 2 * width + c + WIDE],
            p_ref[0, h],
            g_ref[0, :, c : c + WIDE],
            None,
        )
        d_ref[0, :, c : c + WIDE] = grad_q
        d_ref[0, :, width + c : width + c + WIDE] = grad_k
        d_ref[0, :, 2 * width + c : 2 * width + c + WIDE] = grad_v


def self_backward(qkv, probs, grad):
    items, rows, width3 = qkv.shape
    width = width3 // 3
    quads = width // WIDE
    return pl.pallas_call(
        self_backward_kernel,
        grid=(items,),
        in_specs=[
            pl.BlockSpec((1, rows, width3), lambda i: (i, 0, 0)),
            pl.BlockSpec((1, quads, QUAD * rows, rows), lambda i: (i, 0, 0, 0)),
            pl.BlockSpec((1, rows, width), lambda i: (i, 0, 0)),
        ],
        out_specs=pl.BlockSpec((1, rows, width3), lambda i: (i, 0, 0)),
        out_shape=jax.ShapeDtypeStruct((items, rows, width3), BF16),
        compiler_params=params(),
        cost_estimate=pl.CostEstimate(
            flops=20 * items * quads * QUAD * rows * 256 * 256,
            bytes_accessed=2 * items * rows * (7 * width + 16 * rows),
            transcendentals=0,
        ),
    )(qkv, probs, grad)


def cross_forward_kernel(q_ref, kv_ref, m_ref, o_ref, p_ref):
    rows, width = o_ref.shape[1], o_ref.shape[2]
    allowed = m_ref[0] > 0
    for h in range(width // WIDE):
        c = h * WIDE
        probs, mixed = forward_quad(
            q_ref[0, :, c : c + WIDE],
            kv_ref[0, :, c : c + WIDE],
            kv_ref[0, :, width + c : width + c + WIDE],
            allowed,
        )
        o_ref[0, :, c : c + WIDE] = mixed
        p_ref[0, h] = probs


def cross_forward(q, kv, mask):
    items, rows, width = q.shape
    keys = kv.shape[1]
    quads = width // WIDE
    return pl.pallas_call(
        cross_forward_kernel,
        grid=(items,),
        in_specs=[
            pl.BlockSpec((1, rows, width), lambda i: (i, 0, 0)),
            pl.BlockSpec((1, keys, 2 * width), lambda i: (i, 0, 0)),
            pl.BlockSpec((1, 1, keys), lambda i: (i, 0, 0)),
        ],
        out_specs=[
            pl.BlockSpec((1, rows, width), lambda i: (i, 0, 0)),
            pl.BlockSpec((1, quads, QUAD * rows, keys), lambda i: (i, 0, 0, 0)),
        ],
        out_shape=[
            jax.ShapeDtypeStruct((items, rows, width), BF16),
            jax.ShapeDtypeStruct((items, quads, QUAD * rows, keys), BF16),
        ],
        compiler_params=params(),
        cost_estimate=pl.CostEstimate(
            flops=8 * items * quads * QUAD * rows * 256 * 256,
            bytes_accessed=2 * items * rows * (6 * width + 16 * keys),
            transcendentals=0,
        ),
    )(q, kv, mask)


def cross_backward_kernel(q_ref, kv_ref, p_ref, g_ref, m_ref, dq_ref, dkv_ref):
    width = g_ref.shape[2]
    allowed = m_ref[0] > 0
    for h in range(width // WIDE):
        c = h * WIDE
        grad_q, grad_k, grad_v = backward_quad(
            q_ref[0, :, c : c + WIDE],
            kv_ref[0, :, c : c + WIDE],
            kv_ref[0, :, width + c : width + c + WIDE],
            p_ref[0, h],
            g_ref[0, :, c : c + WIDE],
            allowed,
        )
        dq_ref[0, :, c : c + WIDE] = grad_q
        dkv_ref[0, :, c : c + WIDE] = grad_k
        dkv_ref[0, :, width + c : width + c + WIDE] = grad_v


def cross_backward(q, kv, probs, grad, mask):
    items, rows, width = q.shape
    keys = kv.shape[1]
    quads = width // WIDE
    return pl.pallas_call(
        cross_backward_kernel,
        grid=(items,),
        in_specs=[
            pl.BlockSpec((1, rows, width), lambda i: (i, 0, 0)),
            pl.BlockSpec((1, keys, 2 * width), lambda i: (i, 0, 0)),
            pl.BlockSpec((1, quads, QUAD * rows, keys), lambda i: (i, 0, 0, 0)),
            pl.BlockSpec((1, rows, width), lambda i: (i, 0, 0)),
            pl.BlockSpec((1, 1, keys), lambda i: (i, 0, 0)),
        ],
        out_specs=[
            pl.BlockSpec((1, rows, width), lambda i: (i, 0, 0)),
            pl.BlockSpec((1, keys, 2 * width), lambda i: (i, 0, 0)),
        ],
        out_shape=[
            jax.ShapeDtypeStruct((items, rows, width), BF16),
            jax.ShapeDtypeStruct((items, keys, 2 * width), BF16),
        ],
        compiler_params=params(),
        cost_estimate=pl.CostEstimate(
            flops=20 * items * quads * QUAD * rows * 256 * 256,
            bytes_accessed=2 * items * rows * (10 * width + 16 * keys),
            transcendentals=0,
        ),
    )(q, kv, probs, grad, mask)


def factor_of(value):
    return lax.rsqrt(jnp.mean(value * value, axis=-1, keepdims=True) + EPSILON)


def norm_back(value, factor, gain, grad):
    scaled = gain * grad
    along = jnp.mean(scaled * value, axis=-1, keepdims=True)
    grad_value = factor * scaled - value * (factor * factor * factor * along)
    return grad_value, jnp.sum(grad * value * factor, axis=0)


def matmul(left, right):
    return jnp.dot(left, right, preferred_element_type=F32)


def matmul_t(left, right):
    return jnp.einsum("re,de->rd", left, right, preferred_element_type=F32)


def weight_grad(left, right):
    return jnp.einsum("rd,re->de", left, right, preferred_element_type=F32).astype(BF16)


def gather(shard, spot):
    rows = shard.shape[0] // 8
    piece = lax.dynamic_slice_in_dim(shard, (spot % 8) * rows, rows, 0)
    groups = lax.axis_size("batch") // 8
    if groups > 1:
        inner = lax.all_gather(
            piece,
            "batch",
            axis=0,
            tiled=True,
            axis_index_groups=[[8 * g + j for j in range(8)] for g in range(groups)],
        )
        return lax.all_gather(inner, "fsdp", axis=0, tiled=True)
    return lax.all_gather(piece, ("fsdp", "batch"), axis=0, tiled=True)


def scatter(grad):
    batch = lax.axis_size("batch")
    if batch > 8:
        part = lax.psum_scatter(grad, "fsdp", scatter_dimension=0, tiled=True)
        return lax.psum(part, "batch").astype(F32)
    part = lax.psum_scatter(grad, ("fsdp", "batch"), scatter_dimension=0, tiled=True)
    return lax.all_gather(part, "batch", axis=0, tiled=True).astype(F32)


def on_device(
    text,
    memory,
    text_lengths,
    memory_mask,
    grad_out,
    self_gain,
    self_query,
    self_key,
    self_value,
    self_output,
    cross_gain,
    cross_query,
    cross_key,
    cross_value,
    cross_output,
    mlp_gain,
    mlp_gate,
    mlp_up,
    mlp_down,
):
    items, rows, width = text.shape
    keys = memory.shape[1]
    spot = lax.axis_index("batch")

    gains = lax.all_gather(jnp.stack([self_gain, cross_gain, mlp_gain]), "fsdp", axis=1, tiled=True)
    gains = gains.astype(F32)
    w_self = gather(
        jnp.concatenate([self_query, self_key, self_value, self_output], axis=1), spot
    )
    w_cross = gather(
        jnp.concatenate([cross_key, cross_value, cross_query, cross_output], axis=1), spot
    )
    w_down = gather(mlp_down, spot)
    w_wide = gather(jnp.concatenate([mlp_gate, mlp_up], axis=1), spot)
    w_qkv, w_so = w_self[:, : 3 * width], w_self[:, 3 * width :]
    w_kv = w_cross[:, : 2 * width]
    w_cq, w_co = w_cross[:, 2 * width : 3 * width], w_cross[:, 3 * width :]
    hidden = w_down.shape[0]

    x = text.reshape(-1, width).astype(F32)
    flat_memory = memory.reshape(-1, width)
    e3 = grad_out.reshape(-1, width)
    mask = memory_mask[:, None, :]

    c1 = factor_of(x)
    a1 = (x * c1 * gains[0]).astype(BF16)
    qkv = matmul(a1, w_qkv).astype(BF16).reshape(items, rows, 3 * width)
    o1, p1 = self_forward(qkv, text_lengths)
    o1 = o1.reshape(-1, width)
    h1 = x + matmul(o1, w_so)
    c2 = factor_of(h1)
    a2 = (h1 * c2 * gains[1]).astype(BF16)
    kv = matmul(flat_memory, w_kv).astype(BF16).reshape(items, keys, 2 * width)
    q2 = matmul(a2, w_cq).astype(BF16).reshape(items, rows, width)
    o2, p2 = cross_forward(q2, kv, mask)
    o2 = o2.reshape(-1, width)
    h2 = h1 + matmul(o2, w_co)
    c3 = factor_of(h2)
    a3 = (h2 * c3 * gains[2]).astype(BF16)
    d_inner = matmul_t(e3, w_down)
    gate = matmul(a3, w_wide[:, :hidden])
    up = matmul(a3, w_wide[:, hidden:])
    act, pull = jax.vjp(lambda g, u: jax.nn.gelu(g, approximate=True) * u, gate, up)
    inner = act.astype(BF16)
    d_gate, d_up = pull(d_inner)
    d_gate, d_up = d_gate.astype(BF16), d_up.astype(BF16)
    g_down = scatter(weight_grad(inner, e3))
    g_gate = scatter(weight_grad(a3, d_gate))
    g_up = scatter(weight_grad(a3, d_up))
    block_out = (h2 + matmul(inner, w_down)).astype(BF16)

    d_a3 = matmul_t(d_gate, w_wide[:, :hidden]) + matmul_t(d_up, w_wide[:, hidden:])
    back, gg3 = norm_back(h2, c3, gains[2], d_a3)
    d_h2 = e3.astype(F32) + back
    e2 = d_h2.astype(BF16)
    g_co = weight_grad(o2, e2)
    d_o2 = matmul_t(e2, w_co).astype(BF16).reshape(items, rows, width)
    d_q2, d_kv = cross_backward(q2, kv, p2, d_o2, mask)
    d_q2 = d_q2.reshape(-1, width)
    d_kv = d_kv.reshape(-1, 2 * width)
    g_cq = weight_grad(a2, d_q2)
    g_kv = weight_grad(flat_memory, d_kv)
    g_cross = scatter(jnp.concatenate([g_kv, g_cq, g_co], axis=1))
    grad_memory = matmul_t(d_kv, w_kv)
    d_a2 = matmul_t(d_q2, w_cq)
    back, gg2 = norm_back(h1, c2, gains[1], d_a2)
    d_h1 = d_h2 + back
    e1 = d_h1.astype(BF16)
    g_so = weight_grad(o1, e1)
    d_o1 = matmul_t(e1, w_so).astype(BF16).reshape(items, rows, width)
    d_qkv = self_backward(qkv, p1, d_o1).reshape(-1, 3 * width)
    g_qkv = weight_grad(a1, d_qkv)
    g_self = scatter(jnp.concatenate([g_qkv, g_so], axis=1))
    d_a1 = matmul_t(d_qkv, w_qkv)
    back, gg1 = norm_back(x, c1, gains[0], d_a1)
    grad_text = d_h1 + back

    gg = lax.psum(jnp.stack([gg1, gg2, gg3]), ("batch", "fsdp"))
    own = lax.axis_index("fsdp") * self_gain.shape[0]
    gg = lax.dynamic_slice_in_dim(gg, own, self_gain.shape[0], 1)
    cut = lambda g, j: g[:, j * width : (j + 1) * width]
    return (
        block_out.reshape(text.shape),
        grad_text.reshape(text.shape),
        grad_memory.reshape(memory.shape),
        gg[0],
        cut(g_self, 0),
        cut(g_self, 1),
        cut(g_self, 2),
        cut(g_self, 3),
        gg[1],
        cut(g_cross, 2),
        cut(g_cross, 0),
        cut(g_cross, 1),
        cut(g_cross, 3),
        gg[2],
        g_gate,
        g_up,
        g_down,
    )


def solution(mesh):
    rows = P(("batch", "fsdp"), None, None)
    gain, weight = P("fsdp"), P("fsdp", None)
    weights = (gain, weight, weight, weight, weight) * 2 + (gain, weight, weight, weight)
    return jax.shard_map(
        on_device,
        mesh=mesh,
        in_specs=(rows, rows, P(("batch", "fsdp")), P(("batch", "fsdp"), None), rows) + weights,
        out_specs=(rows, rows, rows) + weights,
        check_vma=False,
    )
```

```python
import functools

import jax
import jax.numpy as jnp
from jax import lax
from jax.experimental import pallas as pl
from jax.experimental.pallas import tpu as pltpu
from jax.sharding import PartitionSpec as P

HEAD_DIM = 64
QUAD = 4
WIDE = HEAD_DIM * QUAD
EPSILON = 1e-06
MASKED = -1e30
SCALE = 0.125
VMEM_LIMIT = 56 * 1024 * 1024

BF16 = jnp.bfloat16
F32 = jnp.float32


def params():
    return pltpu.CompilerParams(vmem_limit_bytes=VMEM_LIMIT)


def dot(a, b, dims):
    return lax.dot_general(a, b, (dims, ((), ())), preferred_element_type=F32)


def stack_heads(value):
    lane = lax.broadcasted_iota(jnp.int32, value.shape, 1) // HEAD_DIM
    zero = jnp.zeros_like(value)
    return jnp.concatenate([jnp.where(lane == j, value, zero) for j in range(QUAD)], axis=0)


def join_heads(stacked):
    rows = stacked.shape[0] // QUAD
    lane = lax.broadcasted_iota(jnp.int32, (rows, WIDE), 1) // HEAD_DIM
    out = stacked[:rows]
    for j in range(1, QUAD):
        out = jnp.where(lane == j, stacked[j * rows : (j + 1) * rows], out)
    return out


def causal_mask(rows, keys, length):
    t = lax.broadcasted_iota(jnp.int32, (rows, keys), 0)
    u = lax.broadcasted_iota(jnp.int32, (rows, keys), 1)
    one = (u <= t) & (u < length)
    return jnp.concatenate([one] * QUAD, axis=0)


def forward_quad(q, k, v, allowed):
    stacked = stack_heads(q)
    scores = dot(stacked, k, ((1,), (1,))) * SCALE
    scores = jnp.where(allowed, scores, MASKED)
    top = jnp.max(scores, axis=-1, keepdims=True)
    lifted = jnp.exp(scores - top)
    total = jnp.sum(lifted, axis=-1, keepdims=True)
    probs = (lifted / total).astype(BF16)
    mixed = join_heads(dot(probs, v, ((1,), (0,))))
    return probs, mixed.astype(BF16)


def backward_quad(q, k, v, probs, grad, allowed):
    q_stack = stack_heads(q)
    g_stack = stack_heads(grad)
    grad_v = dot(probs, g_stack, ((0,), (0,)))
    grad_p = dot(g_stack, v, ((1,), (1,)))
    p = probs.astype(F32)
    inner = jnp.sum(grad_p * p, axis=-1, keepdims=True)
    grad_s = p * (grad_p - inner)
    if allowed is not None:
        grad_s = jnp.where(allowed, grad_s, 0.0)
    grad_s = grad_s.astype(BF16)
    grad_q = join_heads(dot(grad_s, k, ((1,), (0,)))) * SCALE
    grad_k = dot(grad_s, q_stack, ((0,), (0,))) * SCALE
    return grad_q.astype(BF16), grad_k.astype(BF16), grad_v.astype(BF16)


def self_forward_kernel(lengths, qkv_ref, o_ref, p_ref):
    rows, width = o_ref.shape[1], o_ref.shape[2]
    allowed = causal_mask(rows, rows, lengths[pl.program_id(0)])
    for h in range(width // WIDE):
        c = h * WIDE
        probs, mixed = forward_quad(
            qkv_ref[0, :, c : c + WIDE],
            qkv_ref[0, :, width + c : width + c + WIDE],
            qkv_ref[0, :, 2 * width + c : 2 * width + c + WIDE],
            allowed,
        )
        o_ref[0, :, c : c + WIDE] = mixed
        p_ref[0, h] = probs


def self_forward(qkv, lengths):
    items, rows, width3 = qkv.shape
    width = width3 // 3
    quads = width // WIDE
    return pl.pallas_call(
        self_forward_kernel,
        grid_spec=pltpu.PrefetchScalarGridSpec(
            num_scalar_prefetch=1,
            grid=(items,),
            in_specs=[pl.BlockSpec((1, rows, width3), lambda i, s: (i, 0, 0))],
            out_specs=[
                pl.BlockSpec((1, rows, width), lambda i, s: (i, 0, 0)),
                pl.BlockSpec((1, quads, QUAD * rows, rows), lambda i, s: (i, 0, 0, 0)),
            ],
        ),
        out_shape=[
            jax.ShapeDtypeStruct((items, rows, width), BF16),
            jax.ShapeDtypeStruct((items, quads, QUAD * rows, rows), BF16),
        ],
        compiler_params=params(),
        cost_estimate=pl.CostEstimate(
            flops=8 * items * quads * QUAD * rows * 256 * 256,
            bytes_accessed=2 * items * rows * (4 * width + 16 * rows),
            transcendentals=0,
        ),
    )(lengths, qkv)


def self_backward_kernel(qkv_ref, p_ref, g_ref, *refs):
    d_ref = refs[-1]
    width = g_ref.shape[2]
    for h in range(width // WIDE):
        c = h * WIDE
        grad_q, grad_k, grad_v = backward_quad(
            qkv_ref[0, :, c : c + WIDE],
            qkv_ref[0, :, width + c : width + c + WIDE],
            qkv_ref[0, :, 2 * width + c : 2 * width + c + WIDE],
            p_ref[0, h],
            g_ref[0, :, c : c + WIDE],
            None,
        )
        d_ref[0, :, c : c + WIDE] = grad_q
        d_ref[0, :, width + c : width + c + WIDE] = grad_k
        d_ref[0, :, 2 * width + c : 2 * width + c + WIDE] = grad_v


def self_backward(order, qkv, probs, grad):
    items, rows, width3 = qkv.shape
    width = width3 // 3
    quads = width // WIDE
    waits = order.take()
    out = pl.pallas_call(
        self_backward_kernel,
        grid=(items,),
        in_specs=[
            pl.BlockSpec((1, rows, width3), lambda i: (i, 0, 0)),
            pl.BlockSpec((1, quads, QUAD * rows, rows), lambda i: (i, 0, 0, 0)),
            pl.BlockSpec((1, rows, width), lambda i: (i, 0, 0)),
        ]
        + [pl.BlockSpec(memory_space=pl.ANY)] * len(waits),
        out_specs=pl.BlockSpec((1, rows, width3), lambda i: (i, 0, 0)),
        out_shape=jax.ShapeDtypeStruct((items, rows, width3), BF16),
        compiler_params=params(),
        cost_estimate=cost(11.5),
    )(qkv, probs, grad, *waits)
    return order.after(out)


def cross_forward_kernel(q_ref, kv_ref, m_ref, o_ref, p_ref):
    rows, width = o_ref.shape[1], o_ref.shape[2]
    allowed = m_ref[0] > 0
    for h in range(width // WIDE):
        c = h * WIDE
        probs, mixed = forward_quad(
            q_ref[0, :, c : c + WIDE],
            kv_ref[0, :, c : c + WIDE],
            kv_ref[0, :, width + c : width + c + WIDE],
            allowed,
        )
        o_ref[0, :, c : c + WIDE] = mixed
        p_ref[0, h] = probs


def cross_forward(q, kv, mask):
    items, rows, width = q.shape
    keys = kv.shape[1]
    quads = width // WIDE
    return pl.pallas_call(
        cross_forward_kernel,
        grid=(items,),
        in_specs=[
            pl.BlockSpec((1, rows, width), lambda i: (i, 0, 0)),
            pl.BlockSpec((1, keys, 2 * width), lambda i: (i, 0, 0)),
            pl.BlockSpec((1, 1, keys), lambda i: (i, 0, 0)),
        ],
        out_specs=[
            pl.BlockSpec((1, rows, width), lambda i: (i, 0, 0)),
            pl.BlockSpec((1, quads, QUAD * rows, keys), lambda i: (i, 0, 0, 0)),
        ],
        out_shape=[
            jax.ShapeDtypeStruct((items, rows, width), BF16),
            jax.ShapeDtypeStruct((items, quads, QUAD * rows, keys), BF16),
        ],
        compiler_params=params(),
        cost_estimate=pl.CostEstimate(
            flops=8 * items * quads * QUAD * rows * 256 * 256,
            bytes_accessed=2 * items * rows * (6 * width + 16 * keys),
            transcendentals=0,
        ),
    )(q, kv, mask)


def cross_backward_kernel(q_ref, kv_ref, p_ref, g_ref, m_ref, *refs):
    dq_ref, dkv_ref = refs[-2:]
    width = g_ref.shape[2]
    allowed = m_ref[0] > 0
    for h in range(width // WIDE):
        c = h * WIDE
        grad_q, grad_k, grad_v = backward_quad(
            q_ref[0, :, c : c + WIDE],
            kv_ref[0, :, c : c + WIDE],
            kv_ref[0, :, width + c : width + c + WIDE],
            p_ref[0, h],
            g_ref[0, :, c : c + WIDE],
            allowed,
        )
        dq_ref[0, :, c : c + WIDE] = grad_q
        dkv_ref[0, :, c : c + WIDE] = grad_k
        dkv_ref[0, :, width + c : width + c + WIDE] = grad_v


def cross_backward(order, q, kv, probs, grad, mask):
    items, rows, width = q.shape
    keys = kv.shape[1]
    quads = width // WIDE
    waits = order.take()
    out = pl.pallas_call(
        cross_backward_kernel,
        grid=(items,),
        in_specs=[
            pl.BlockSpec((1, rows, width), lambda i: (i, 0, 0)),
            pl.BlockSpec((1, keys, 2 * width), lambda i: (i, 0, 0)),
            pl.BlockSpec((1, quads, QUAD * rows, keys), lambda i: (i, 0, 0, 0)),
            pl.BlockSpec((1, rows, width), lambda i: (i, 0, 0)),
            pl.BlockSpec((1, 1, keys), lambda i: (i, 0, 0)),
        ]
        + [pl.BlockSpec(memory_space=pl.ANY)] * len(waits),
        out_specs=[
            pl.BlockSpec((1, rows, width), lambda i: (i, 0, 0)),
            pl.BlockSpec((1, keys, 2 * width), lambda i: (i, 0, 0)),
        ],
        out_shape=[
            jax.ShapeDtypeStruct((items, rows, width), BF16),
            jax.ShapeDtypeStruct((items, keys, 2 * width), BF16),
        ],
        compiler_params=params(),
        cost_estimate=cost(13.5),
    )(q, kv, probs, grad, mask, *waits)
    order.after(out[0])
    return out


def factor_of(value):
    return lax.rsqrt(jnp.mean(value * value, axis=-1, keepdims=True) + EPSILON)


def matmul(left, right):
    return jnp.dot(left, right, preferred_element_type=F32)


AXES = {1: "core", 2: "x", 4: "y"}


def swap(value, bit):
    return lax.ppermute(value, AXES[bit], [(0, 1), (1, 0)])


class Order:
    def __init__(self):
        self.waits = []

    def take(self):
        waits, self.waits = self.waits, []
        return waits

    def after(self, array):
        self.waits.append(array)
        return array


def hold_kernel(*refs):
    pass


def hold(order, array):
    whole = pl.BlockSpec(memory_space=pl.ANY)
    waits = order.take()
    out = pl.pallas_call(
        hold_kernel,
        in_specs=[whole] * (1 + len(waits)),
        out_specs=whole,
        out_shape=jax.ShapeDtypeStruct(array.shape, array.dtype),
        input_output_aliases={0: 0},
        compiler_params=pltpu.CompilerParams(vmem_limit_bytes=1024 * 1024),
        cost_estimate=cost(0.5),
    )(array, *waits)
    return order.after(out)


SHARE = 0.5


def cost(micros):
    return pl.CostEstimate(
        flops=int(SHARE * micros * 1.15e9),
        bytes_accessed=int(SHARE * micros * 3.6e6),
        transcendentals=0,
    )


def put_split(value, flag, axis, give_ref, keep_ref):
    half = value.shape[axis] // 2
    low, high = (value[:half], value[half:]) if axis == 0 else (value[:, :half], value[:, half:])

    @pl.when(flag == 0)
    def _():
        keep_ref[...] = low
        give_ref[...] = high

    @pl.when(flag > 0)
    def _():
        keep_ref[...] = high
        give_ref[...] = low


def product_kernel(jobs, has_add, axis, halves, flags, *refs):
    outs = refs[-halves * 2 :] if has_add else refs[-1:]
    add_ref = refs[sum(count + 1 for count, _, _ in jobs)]
    at = 0
    total = sum(steps for _, _, steps in jobs)
    for count, start, steps in jobs:
        lefts, right = refs[at : at + count], refs[at + count]
        at += count + 1

        def work(lefts=lefts, right=right, start=start):
            left = jnp.concatenate([r[...] for r in lefts], axis=1)
            value = right[0] if len(right.shape) == 3 else right[...]
            out = dot(left, value, ((0,), (0,)))
            if not has_add:
                outs[0][...] = out.astype(BF16)
                return
            out = (out + add_ref[...].astype(F32)).astype(BF16)
            if axis == 1:
                put_split(out, flags[1], 1, *outs)
                return
            which = 2 * start // total if halves > 1 else 0
            give, keep = outs[2 * which : 2 * which + 2]
            for z in range(give.shape[0]):
                part = out[128 * z : 128 * z + 128]
                put_split(part, flags[1 + which], 0, give.at[z], keep.at[z])

        if len(jobs) == 1:
            work()
        else:
            step = pl.program_id(0)
            pl.when((step >= start) & (step < start + steps))(work)


def call_product(order, axis, grid, jobs, flags, specs, operands, out_specs, out_shapes):
    waits = order.take()
    has_add = len(out_shapes) > 1
    out = pl.pallas_call(
        functools.partial(product_kernel, jobs, has_add, axis, len(out_shapes) // 2),
        grid_spec=pltpu.PrefetchScalarGridSpec(
            num_scalar_prefetch=1,
            grid=grid,
            in_specs=specs + [pl.BlockSpec(memory_space=pl.ANY)] * len(waits),
            out_specs=out_specs,
        ),
        out_shape=out_shapes,
        compiler_params=params(),
        cost_estimate=cost(3 + 2e-6 * sum(v.size for v in out_shapes)),
    )(flags, *operands, *waits)
    order.after(out[0])
    return out


def grad_rows(order, pairs, flags, add=None):
    count = pairs[0][0].shape[1] // 256
    total = sum(columns for _, _, _, columns in pairs)
    tile = next(t for t in (1408, 1024) if all(c % t == 0 for _, _, _, c in pairs))
    specs, operands, jobs, start = [], [], [], 0
    for left, right, place, columns in pairs:
        rows, steps = left.shape[0], columns // tile
        specs += [
            pl.BlockSpec((rows, 128), lambda j, f, z=z: (0, 2 * z + f[0])) for z in range(count)
        ]
        block = lambda j, f, start=start, steps=steps: jnp.clip(j - start, 0, steps - 1)
        if right.ndim == 3:
            specs.append(
                pl.BlockSpec((1, rows, tile), lambda j, f, b=block, p=place: (p, 0, b(j, f)))
            )
        else:
            specs.append(
                pl.BlockSpec((rows, tile), lambda j, f, b=block, p=place: (0, p + b(j, f)))
            )
        operands += [left] * count + [right]
        jobs.append((count, start, steps))
        start += steps
    block = pl.BlockSpec((count * 128, tile), lambda j, f: (0, j))
    if add is None:
        shapes, outs = [jax.ShapeDtypeStruct((count * 128, total), BF16)], [block]
    else:
        specs.append(block)
        operands.append(add)
        halves = flags.shape[0] - 1
        shapes = [jax.ShapeDtypeStruct((count, 64, total // halves), BF16)] * (2 * halves)
        outs, most = [], start // halves
        for i in range(halves):
            place = lambda j, f, i=i: (0, 0, jnp.clip(j - i * most, 0, most - 1))
            outs += [pl.BlockSpec((count, 64, tile), place)] * 2
    return call_product(order, 0, (start,), jobs, flags, specs, operands, outs, shapes)


def grad_columns(order, left, right, flags, add=None):
    rows, width = left.shape
    half = right.shape[1] // 2
    tile = next(t for t in (1408, 1024) if width % t == 0)
    block = lambda columns: pl.BlockSpec((tile, columns), lambda j, f: (j, 0))
    specs = [
        pl.BlockSpec((rows, tile), lambda j, f: (0, j)),
        pl.BlockSpec((rows, half), lambda j, f: (0, f[0])),
    ]
    operands = [left, right]
    if add is None:
        shapes, outs = [jax.ShapeDtypeStruct((width, half), BF16)], [block(half)]
    else:
        specs.append(block(half))
        operands.append(add)
        shapes = [jax.ShapeDtypeStruct((width, half // 2), BF16)] * 2
        outs = [block(half // 2)] * 2
    steps = width // tile
    return call_product(
        order, 1, (steps,), [(1, 0, steps)], flags, specs, operands, outs, shapes
    )


def land_kernel(count, axis, flags, *refs):
    outs = refs[len(refs) - (2 * count if axis is not None else 1) :]
    column = 0
    for i in range(count):
        total = refs[2 * i][...] + refs[2 * i + 1][...]
        if axis is None:
            columns = total.shape[-1]
            outs[0][..., column : column + columns] = total
            column += columns
        elif axis == 1:
            put_split(total, flags[i], 1, *outs[2 * i : 2 * i + 2])
        else:
            for z in range(total.shape[0]):
                put_split(
                    total[z], flags[i], 0, outs[2 * i].at[z], outs[2 * i + 1].at[z]
                )


def land_sums(order, pairs, flags, axis):
    waits = order.take()
    steps = 2
    block = lambda shape: pl.BlockSpec(
        (shape[0] // steps, *shape[1:]), lambda j, f: (j,) + (0,) * (len(shape) - 1)
    )
    specs, operands, shapes = [], [], []
    for keep, got in pairs:
        specs += [block(keep.shape)] * 2
        operands += [keep, got]
        shape = list(keep.shape)
        if axis is not None:
            shape[-2 if axis == 0 else -1] //= 2
            shapes += [tuple(shape)] * 2
    if axis is None:
        total = sum(keep.shape[-1] for keep, _ in pairs)
        shapes = [(*pairs[0][0].shape[:-1], total)]
    out = pl.pallas_call(
        functools.partial(land_kernel, len(pairs), axis),
        grid_spec=pltpu.PrefetchScalarGridSpec(
            num_scalar_prefetch=1,
            grid=(steps,),
            in_specs=specs + [pl.BlockSpec(memory_space=pl.ANY)] * len(waits),
            out_specs=[block(shape) for shape in shapes],
        ),
        out_shape=[jax.ShapeDtypeStruct(shape, BF16) for shape in shapes],
        compiler_params=params(),
        cost_estimate=cost(1.5 + 1.7e-6 * sum(k.size for k, _ in pairs)),
    )(jnp.stack(flags), *operands, *waits)
    order.after(out[0])
    return out


def join_kernel(count, pieces, flags, *refs):
    outs = refs[len(refs) - count * pieces :]
    for i in range(count):
        own, got = refs[2 * i], refs[2 * i + 1]
        half, columns = own.shape[0], own.shape[1] // pieces
        for k in range(pieces):
            out = outs[i * pieces + k]
            at = slice(k * columns, (k + 1) * columns)

            def put(low, high, out=out, at=at, half=half):
                out[:half] = low[:, at].astype(out.dtype)
                out[half:] = high[:, at].astype(out.dtype)

            pl.when(flags[i] == 0)(functools.partial(put, own, got))
            pl.when(flags[i] > 0)(functools.partial(put, got, own))


def land_joins(order, pairs, flags, pieces, kind):
    waits = order.take()
    whole = lambda shape: pl.BlockSpec(shape, lambda j, f: (0, 0))
    specs, operands, shapes = [], [], []
    for own, got in pairs:
        specs += [whole(own.shape)] * 2
        operands += [own, got]
        shapes += [(2 * own.shape[0], own.shape[1] // pieces)] * pieces
    out = pl.pallas_call(
        functools.partial(join_kernel, len(pairs), pieces),
        grid_spec=pltpu.PrefetchScalarGridSpec(
            num_scalar_prefetch=1,
            grid=(1,),
            in_specs=specs + [pl.BlockSpec(memory_space=pl.ANY)] * len(waits),
            out_specs=[whole(shape) for shape in shapes],
        ),
        out_shape=[jax.ShapeDtypeStruct(shape, kind) for shape in shapes],
        compiler_params=params(),
        cost_estimate=cost(2 + 1.5e-6 * sum(v.size for v, _ in pairs)),
    )(jnp.stack(flags), *operands, *waits)
    order.after(out[0])
    return out


def segment_kernel(steps, has_next, waits, *refs):
    x_ref, w_ref, v_ref, b_ref, g_ref = refs[:5]
    n_ref = refs[5] if has_next else None
    refs = refs[5 + has_next + waits :]
    if has_next:
        d_ref, gg_ref, e_ref, o_ref, acc = refs
    else:
        d_ref, gg_ref, acc = refs
    step = pl.program_id(0)
    x = x_ref[0] if len(x_ref.shape) == 3 else x_ref[...]
    partial = dot(x, w_ref[...], ((1,), (1,)))

    @pl.when(step == 0)
    def _():
        acc[...] = partial

    @pl.when(step > 0)
    def _():
        acc[...] += partial

    @pl.when(step == steps - 1)
    def _():
        gain = g_ref[...]
        rows, chunk = acc.shape[0], 144
        gg_ref[...] = jnp.zeros_like(gg_ref)

        @pl.loop(0, rows // chunk)
        def _(i):
            at = pl.ds(pl.multiple_of(i * chunk, chunk), chunk)
            grad = acc[at, :]
            value = v_ref[at, :].astype(F32)
            factor = lax.rsqrt(jnp.mean(value * value, axis=-1, keepdims=True) + EPSILON)
            scaled = gain * grad
            along = jnp.mean(scaled * value, axis=-1, keepdims=True)
            back = factor * scaled - value * (factor * factor * factor * along)
            gg_ref[...] += jnp.sum(grad * value * factor, axis=0, keepdims=True)
            total = b_ref[at, :].astype(F32) + back
            d_ref[at, :] = total
            if has_next:
                e_ref[at, :] = total.astype(BF16)

        if has_next:
            o_ref[...] = dot(e_ref[...], n_ref[...], ((1,), (1,))).astype(BF16)


def segment(order, x, w, column, tile, value, base, gain, after=None):
    rows, width = value.shape
    steps = x.shape[-1] * (x.shape[0] if x.ndim == 3 else 1) // tile
    if x.ndim == 3:
        per = x.shape[-1] // tile
        x_spec = pl.BlockSpec((1, rows, tile), lambda k: (k // per, 0, k % per))
    else:
        x_spec = pl.BlockSpec((rows, tile), lambda k: (0, k))
    whole = pl.BlockSpec((rows, width), lambda k: (0, 0))
    line = pl.BlockSpec((1, width), lambda k: (0, 0))
    specs = [x_spec, pl.BlockSpec((width, tile), lambda k: (0, k + column)), whole, whole, line]
    operands = [x, w, value, base, gain.reshape(1, width)]
    shapes = [
        jax.ShapeDtypeStruct((rows, width), F32),
        jax.ShapeDtypeStruct((1, width), F32),
    ]
    outs = [whole, line]
    if after is not None:
        matrix, at = after
        specs.append(pl.BlockSpec((width, width), lambda k: (0, at)))
        operands.append(matrix)
        shapes += [jax.ShapeDtypeStruct((rows, width), BF16)] * 2
        outs += [whole, whole]
    waits = order.take()
    out = pl.pallas_call(
        functools.partial(segment_kernel, steps, after is not None, len(waits)),
        grid=(steps,),
        in_specs=specs + [pl.BlockSpec(memory_space=pl.ANY)] * len(waits),
        out_specs=outs,
        out_shape=shapes,
        scratch_shapes=[pltpu.VMEM((rows, width), F32)],
        compiler_params=params(),
        cost_estimate=cost(5 + x.size * width / 2.6e8),
    )(*operands, *waits)
    order.after(out[1])
    return out


def mlp_kernel(a_ref, e_ref, wg_ref, wu_ref, wd_ref, i_ref, d_ref):
    grad = dot(e_ref[...], wd_ref[...], ((1,), (1,)))
    gate = dot(a_ref[...], wg_ref[...], ((1,), (0,)))
    up = dot(a_ref[...], wu_ref[...], ((1,), (0,)))
    slope, cubic = 0.7978845608028654, 0.044715
    square = gate * gate
    bend = jnp.tanh(slope * gate * (1.0 + cubic * square))
    half = 0.5 * (1.0 + bend)
    act = gate * half
    turn = half + 0.5 * gate * (1.0 - bend * bend) * slope * (1.0 + 3.0 * cubic * square)
    i_ref[...] = (act * up).astype(BF16)
    d_ref[0] = (grad * up * turn).astype(BF16)
    d_ref[1] = (grad * act).astype(BF16)


def mlp(a3, e3, w_wide, w_down):
    rows, width = a3.shape
    hidden = w_down.shape[0]
    tile = 256
    count = hidden // tile
    whole = pl.BlockSpec((rows, width), lambda j: (0, 0))
    return pl.pallas_call(
        mlp_kernel,
        grid=(count,),
        in_specs=[
            whole,
            whole,
            pl.BlockSpec((width, tile), lambda j: (0, j)),
            pl.BlockSpec((width, tile), lambda j: (0, count + j)),
            pl.BlockSpec((tile, width), lambda j: (j, 0)),
        ],
        out_specs=[
            pl.BlockSpec((rows, tile), lambda j: (0, j)),
            pl.BlockSpec((2, rows, tile), lambda j: (0, 0, j)),
        ],
        out_shape=[
            jax.ShapeDtypeStruct((rows, hidden), BF16),
            jax.ShapeDtypeStruct((2, rows, hidden), BF16),
        ],
        compiler_params=params(),
        cost_estimate=cost(20),
    )(a3, e3, w_wide, w_wide, w_down)


def forward_out_kernel(steps, waits, x_ref, w_ref, b_ref, *refs):
    o_ref, acc = refs[waits:]
    step = pl.program_id(0)
    partial = dot(x_ref[...], w_ref[...], ((1,), (0,)))

    @pl.when(step == 0)
    def _():
        acc[...] = partial + b_ref[...]

    @pl.when(step > 0)
    def _():
        acc[...] += partial

    @pl.when(step == steps - 1)
    def _():
        o_ref[...] = acc[...].astype(BF16)


def forward_out(order, x, w, base):
    rows, width = base.shape
    tile = next(t for t in (1408, 1024) if w.shape[0] % t == 0)
    steps = w.shape[0] // tile
    whole = pl.BlockSpec((rows, width), lambda k: (0, 0))
    waits = order.take()
    out = pl.pallas_call(
        functools.partial(forward_out_kernel, steps, len(waits)),
        grid=(steps,),
        in_specs=[
            pl.BlockSpec((rows, tile), lambda k: (0, k)),
            pl.BlockSpec((tile, width), lambda k: (k, 0)),
            whole,
        ]
        + [pl.BlockSpec(memory_space=pl.ANY)] * len(waits),
        out_specs=whole,
        out_shape=jax.ShapeDtypeStruct((rows, width), BF16),
        scratch_shapes=[pltpu.VMEM((rows, width), F32)],
        compiler_params=params(),
        cost_estimate=cost(8),
    )(x, w, base, *waits)
    return order.after(out)


def back_product_kernel(waits, x_ref, w_ref, *refs):
    refs[-1][...] = dot(x_ref[...], w_ref[...], ((1,), (1,)))


def back_product(order, x, w):
    rows, depth = x.shape
    width = w.shape[0]
    tile = 256
    waits = order.take()
    out = pl.pallas_call(
        functools.partial(back_product_kernel, len(waits)),
        grid=(width // tile,),
        in_specs=[
            pl.BlockSpec((rows, depth), lambda j: (0, 0)),
            pl.BlockSpec((tile, depth), lambda j: (j, 0)),
        ]
        + [pl.BlockSpec(memory_space=pl.ANY)] * len(waits),
        out_specs=pl.BlockSpec((rows, tile), lambda j: (0, j)),
        out_shape=jax.ShapeDtypeStruct((rows, width), F32),
        compiler_params=params(),
        cost_estimate=cost(9),
    )(x, w, *waits)
    return order.after(out)


def bit_of(spot, bit):
    return (spot // bit) % 2


class Sum:
    def __init__(self, order, spot, axis, product, first, second):
        self.order, self.axis, self.product = order, axis, product
        self.first, self.second = first, second
        self.bits = bit_of(spot, 1), bit_of(spot, first), bit_of(spot, second)
        core, one, _ = self.bits
        (give,) = product(jnp.stack([1 - core, one]))
        self.flight = swap(give, 1)

    def core(self):
        core, one, _ = self.bits
        give, self.keep = self.product(jnp.stack([core, one]), self.flight)
        self.flight = swap(give, self.first)


class Part:
    def __init__(self, spot, first, second):
        self.first, self.second, self.axis = first, second, 0
        self.bits = bit_of(spot, 1), bit_of(spot, first), bit_of(spot, second)


class Pair:
    def __init__(self, order, spot, pairs):
        self.product = functools.partial(grad_rows, order, pairs)
        self.parts = [Part(spot, 2, 4), Part(spot, 4, 2)]
        self.flags = [bit_of(spot, b) for b in (1, 2, 4)]
        core, one, two = self.flags
        (give,) = self.product(jnp.stack([1 - core, one, two]))
        self.flight = swap(give, 1)

    def core(self):
        core, one, two = self.flags
        out = self.product(jnp.stack([core, one, two]), self.flight)
        for i, part in enumerate(self.parts):
            part.keep = out[2 * i + 1]
            part.flight = swap(out[2 * i], part.first)
        return self.parts


def region(axis, first, cross):
    return (first, cross) if axis == 0 else (cross, first)


def either(flag, put, one, two):
    pl.when(flag == 0)(lambda: put(one, two))
    pl.when(flag > 0)(lambda: put(two, one))


def cut_kernel(axis, z_ref, *refs):
    a_ref, b_ref = refs[-2:]
    half = z_ref.shape[2 - axis] // 2
    a_ref[0] = z_ref.at[0][region(axis, slice(None), slice(0, half))]
    b_ref[0] = z_ref.at[0][region(axis, slice(None), slice(half, None))]


def pairs_kernel(axis, flags, *refs):
    ins, outs = refs[:4], refs[-2:]
    for i in range(2):
        size = ins[2 * i].shape[1 + axis]

        def put(low, high, out=outs[i], size=size):
            out.at[0][region(axis, slice(0, size), slice(None))] = low[0]
            out.at[0][region(axis, slice(size, None), slice(None))] = high[0]

        either(flags[i], put, ins[2 * i], ins[2 * i + 1])


def quads_kernel(axis, flags, *refs):
    a_own, a_got, b_own, b_got = refs[:4]
    out = refs[-1].at[0]
    two, half = a_own.shape[1 + axis], a_own.shape[2 - axis]
    n = two // 2

    def put_a(low, high):
        out[region(axis, slice(0, two), slice(0, half))] = low[0]
        out[region(axis, slice(two, None), slice(0, half))] = high[0]

    def put_b(low, high):
        for y in range(2):
            for x, ref in enumerate((low, high)):
                at = (2 * y + x) * n
                out[region(axis, slice(at, at + n), slice(half, None))] = ref.at[0][
                    region(axis, slice(y * n, y * n + n), slice(None))
                ]

    either(flags[1], put_a, a_own, a_got)
    either(flags[0], put_b, b_own, b_got)


def cores_kernel(axis, flags, own_ref, got_ref, *refs):
    out = refs[-1].at[0]
    size = own_ref.shape[1 + axis]

    def put(low, high):
        out[region(axis, slice(0, size), slice(None))] = low[0]
        out[region(axis, slice(size, None), slice(None))] = high[0]

    either(flags[2], put, own_ref, got_ref)


def by_shard(order, kernel, axis, flags, operands, shapes):
    waits = order.take()
    block = lambda shape: pl.BlockSpec((1, *shape[1:]), lambda j, *f: (j, 0, 0))
    out = pl.pallas_call(
        functools.partial(kernel, axis),
        grid_spec=pltpu.PrefetchScalarGridSpec(
            num_scalar_prefetch=len(flags),
            grid=(operands[0].shape[0],),
            in_specs=[block(v.shape) for v in operands]
            + [pl.BlockSpec(memory_space=pl.ANY)] * len(waits),
            out_specs=[block(shape) for shape in shapes],
        ),
        out_shape=[jax.ShapeDtypeStruct(shape, BF16) for shape in shapes],
        compiler_params=params(),
        cost_estimate=cost(2.5 + 1.1e-6 * sum(v.size for v in operands)),
    )(*flags, *operands, *waits)
    order.after(out[0])
    return out


class Gather:
    def __init__(self, order, spot, shard, axis):
        self.order, self.axis = order, axis
        self.flags = [jnp.stack([bit_of(spot, b) for b in (2, 4, 1)])]
        size = shard.shape[axis] // 8
        seat = 4 * bit_of(spot, 1) + 2 * bit_of(spot, 4) + bit_of(spot, 2)
        piece = lax.dynamic_slice_in_dim(shard, seat * size, size, axis)
        self.value = lax.all_gather(piece, "fsdp", axis=0)

    def scaled(self, shape, along, across):
        shape = list(shape)
        shape[1 + self.axis] = shape[1 + self.axis] * along
        shape[2 - self.axis] = shape[2 - self.axis] * across // 2
        return tuple(shape)

    def run(self, kernel, flags, operands, shapes):
        return by_shard(self.order, kernel, self.axis, flags, operands, shapes)

    def one(self):
        shape = self.scaled(self.value.shape, 1, 1)
        self.a, self.b = self.run(cut_kernel, [], [self.value], [shape] * 2)
        self.got = swap(self.a, 2), swap(self.b, 4)

    def two(self):
        shape = self.scaled(self.a.shape, 2, 2)
        self.a, self.b = self.run(
            pairs_kernel, self.flags, [self.a, self.got[0], self.b, self.got[1]], [shape] * 2
        )
        self.got = swap(self.a, 4), swap(self.b, 2)

    def three(self):
        shape = self.scaled(self.a.shape, 2, 4)
        (self.half,) = self.run(
            quads_kernel, self.flags, [self.a, self.got[0], self.b, self.got[1]], [shape]
        )
        self.got = swap(self.half, 1)

    def four(self):
        shape = self.scaled(self.half.shape, 2, 2)
        (whole,) = self.run(cores_kernel, self.flags, [self.half, self.got], [shape])
        return whole.reshape(-1, whole.shape[-1])


def land_first(order, *sums):
    out = land_sums(
        order, [(s.keep, s.flight) for s in sums], [s.bits[2] for s in sums], sums[0].axis
    )
    for i, s in enumerate(sums):
        s.keep = out[2 * i + 1]
        s.flight = swap(out[2 * i], s.second)


def land_second(order, *sums):
    (out,) = land_sums(
        order, [(s.keep, s.flight) for s in sums], [s.bits[2] for s in sums], None
    )
    return out.reshape(-1, out.shape[-1])


class Spread:
    def __init__(self, order, spot, values):
        self.order, self.spot = order, spot
        self.values = values
        self.bits = [(4, 2), (2, 4), (1, 1)]
        self.send()

    def send(self):
        self.flights = [swap(v, b) for v, b in zip(self.values, self.bits[0])]

    def land(self):
        flags = [bit_of(self.spot, b) for b in self.bits.pop(0)]
        pairs = list(zip(self.values, self.flights))
        last = not self.bits
        self.values = land_joins(
            self.order, pairs, flags, 2 if last else 1, F32 if last else BF16
        )
        if not last:
            self.send()


def unpack_rows_kernel(v_ref, *refs):
    gate_ref, up_ref = refs[-2:]
    columns = gate_ref.shape[1]
    gate_ref[...] = v_ref[0, :, :columns].astype(F32)
    up_ref[...] = v_ref[0, :, columns:].astype(F32)


def unpack_rows(order, value):
    count, n, both = value.shape
    c = both // 2
    waits = order.take()
    out = pl.pallas_call(
        unpack_rows_kernel,
        grid=(count,),
        in_specs=[pl.BlockSpec((1, n, both), lambda j: (j, 0, 0))]
        + [pl.BlockSpec(memory_space=pl.ANY)] * len(waits),
        out_specs=[
            pl.BlockSpec((n, c), lambda j: (4 * (j % 2) + 2 * (j // 2 % 2) + j // 4, 0)),
            pl.BlockSpec((n, c), lambda j: (4 * (j % 2) + j // 2, 0)),
        ],
        out_shape=[jax.ShapeDtypeStruct((count * n, c), F32)] * 2,
        compiler_params=params(),
        cost_estimate=cost(6),
    )(value, *waits)
    order.after(out[0])
    return out


def unpack_columns_kernel(v_ref, *refs):
    out_ref = refs[-1]
    out_ref[...] = v_ref[0, : out_ref.shape[0], :].astype(F32)


def unpack_columns(order, value, n):
    count, held, c = value.shape
    waits = order.take()
    out = pl.pallas_call(
        unpack_columns_kernel,
        grid=(count,),
        in_specs=[pl.BlockSpec((1, held, c), lambda j: (j, 0, 0))]
        + [pl.BlockSpec(memory_space=pl.ANY)] * len(waits),
        out_specs=pl.BlockSpec((n, c), lambda j: (0, 4 * (j % 2) + 2 * (j // 2 % 2) + j // 4)),
        out_shape=jax.ShapeDtypeStruct((n, count * c), F32),
        compiler_params=params(),
        cost_estimate=cost(6),
    )(value, *waits)
    return order.after(out)


def from_group(value):
    return lax.all_gather(value, ("y", "x", "core"), axis=0)


def over_groups(value):
    value = lax.psum_scatter(value, "fsdp", scatter_dimension=0, tiled=True)
    size = lax.axis_size("group")
    ring = [(i, (i + 1) % size) for i in range(size)]
    total = step = value
    for _ in range(size - 1):
        step = lax.ppermute(step, "group", ring)
        total = total + step
    return total


def on_device(
    text,
    memory,
    text_lengths,
    memory_mask,
    grad_out,
    self_gain,
    self_query,
    self_key,
    self_value,
    self_output,
    cross_gain,
    cross_query,
    cross_key,
    cross_value,
    cross_output,
    mlp_gain,
    mlp_gate,
    mlp_up,
    mlp_down,
):
    items, rows, width = text.shape
    keys = memory.shape[1]
    spot = 4 * lax.axis_index("y") + 2 * lax.axis_index("x") + lax.axis_index("core")

    gains = lax.all_gather(jnp.stack([self_gain, cross_gain, mlp_gain]), "fsdp", axis=1, tiled=True)
    gains = gains.astype(F32)
    order = Order()
    gather = lambda shard, axis=0: Gather(order, spot, shard, axis)
    join = lambda *parts: jnp.concatenate(parts, axis=1)
    g_down = gather(mlp_down, 1)
    g_self = gather(join(self_query, self_key, self_value, self_output))
    g_cross = gather(join(cross_key, cross_value, cross_query, cross_output))
    g_wide = gather(join(mlp_gate, mlp_up))
    hidden = mlp_gate.shape[1]

    x = text.reshape(-1, width).astype(F32)
    flat_memory = memory.reshape(-1, width)
    e3 = grad_out.reshape(-1, width)
    mask = memory_mask[:, None, :]

    g_down.one()
    g_down.two()
    g_self.one()
    g_down.three()
    g_self.two()
    w_down = g_down.four()
    g_cross.one()
    g_self.three()
    g_cross.two()
    w_self = g_self.four()
    w_qkv, w_so = w_self[:, : 3 * width], w_self[:, 3 * width :]
    c1 = factor_of(x)
    a1 = (x * c1 * gains[0]).astype(BF16)
    qkv = matmul(a1, w_qkv).astype(BF16).reshape(items, rows, 3 * width)
    o1, p1 = self_forward(qkv, text_lengths)
    o1 = order.after(o1).reshape(-1, width)
    g_wide.one()
    g_cross.three()
    g_wide.two()
    h1 = x + matmul(o1, w_so)
    c2 = factor_of(h1)
    a2 = (h1 * c2 * gains[1]).astype(BF16)
    order.after(a2)
    w_cross = g_cross.four()
    w_kv = w_cross[:, : 2 * width]
    w_cq, w_co = w_cross[:, 2 * width : 3 * width], w_cross[:, 3 * width :]
    kv = matmul(flat_memory, w_kv).astype(BF16).reshape(items, keys, 2 * width)
    q2 = matmul(a2, w_cq).astype(BF16).reshape(items, rows, width)
    o2, p2 = cross_forward(q2, kv, mask)
    o2 = order.after(o2).reshape(-1, width)
    g_wide.three()
    h2 = h1 + matmul(o2, w_co)
    c3 = factor_of(h2)
    a3 = (h2 * c3 * gains[2]).astype(BF16)
    order.after(a3)
    w_wide = g_wide.four()
    inner, d_wide = mlp(a3, e3, w_wide, w_down)
    order.take()

    sum_of = lambda first, second, pairs: Sum(
        order, spot, 0, functools.partial(grad_rows, order, pairs), first, second
    )
    s_gate = sum_of(2, 4, [(a3, d_wide, 0, hidden)])
    s_up = sum_of(4, 2, [(a3, d_wide, 1, hidden)])
    s_down = Sum(order, spot, 1, functools.partial(grad_columns, order, inner, e3), 2, 4)
    s_gate.core()
    s_up.core()
    d_h2, gg3, e2, d_o2 = segment(
        order, d_wide, w_wide, 0, hidden // 2, h2, e3, gains[2], (w_cross, 3)
    )
    s_down.core()
    d_q2, d_kv = cross_backward(order, q2, kv, p2, d_o2.reshape(text.shape), mask)
    d_q2 = d_q2.reshape(-1, width)
    d_kv = d_kv.reshape(-1, 2 * width)
    land_first(order, s_gate, s_up)
    s_cross = Pair(
        order,
        spot,
        [
            (flat_memory, d_kv, 0, 2 * width),
            (a2, d_q2, 0, width),
            (o2, e2, 0, width),
        ],
    )
    d_h1, gg2, e1, d_o1 = segment(
        order, d_q2, w_cross, 4, width // 2, h1, d_h2, gains[1], (w_self, 3)
    )
    z_wide = over_groups(land_second(order, s_gate, s_up))
    land_first(order, s_down)
    cross = s_cross.core()
    d_qkv = self_backward(order, qkv, p1, d_o1.reshape(text.shape)).reshape(-1, 3 * width)
    z_down = over_groups(land_second(order, s_down))
    s_self = Pair(
        order,
        spot,
        [
            (a1, d_qkv, 0, 2 * width),
            (a1, d_qkv, 2, width),
            (o1, e1, 0, width),
        ],
    )
    land_first(order, *cross)
    z_wide = hold(order, z_wide)
    all_wide = from_group(z_wide)
    both = s_self.core()
    grad_text, gg1 = segment(order, d_qkv, w_self, 0, width, x, d_h1, gains[0])
    lines = jnp.concatenate([gg1, gg2, gg3]).astype(BF16).reshape(-1, width // 8)
    z_down = hold(order, jnp.concatenate([z_down, jnp.pad(lines, ((0, 8), (0, 0)))]))
    all_down = from_group(z_down)
    z_cross = over_groups(land_second(order, *cross))
    land_first(order, *both)
    grad_memory = back_product(order, d_kv, w_cross)
    g_gate, g_up = unpack_rows(order, all_wide)
    block_out = forward_out(order, inner, w_down, h2)
    g_down = unpack_columns(order, all_down, mlp_down.shape[0])
    lines = jnp.sum(all_down[:, mlp_down.shape[0] : -8].astype(F32), axis=0)
    shards, own = lax.axis_size("fsdp"), self_gain.shape[0]
    lines = lines.reshape(3, shards, own).transpose(1, 0, 2).reshape(shards, -1)
    lines = jnp.pad(lines, ((0, 0), (0, 32 * 128 - 3 * own))).astype(BF16).reshape(-1, 128)
    z_self = over_groups(jnp.concatenate([land_second(order, *both), lines], axis=1))
    z_cross = hold(order, z_cross)
    t_cross = Spread(order, spot, [z_cross[:, : 2 * width], z_cross[:, 2 * width :]])
    t_cross.land()
    t_cross.land()
    t_cross.land()
    g_ck, g_cv, g_cq, g_co = t_cross.values
    z_self = hold(order, z_self)
    t_self = Spread(order, spot, [z_self[:, : 2 * width], z_self[:, 2 * width : 4 * width]])
    gg = z_self[:, 4 * width :].reshape(-1)[: 3 * own].reshape(3, own).astype(F32)
    t_self.land()
    t_self.land()
    t_self.land()
    g_sq, g_sk, g_sv, g_so = t_self.values

    return (
        block_out.reshape(text.shape),
        grad_text.reshape(text.shape),
        grad_memory.reshape(memory.shape),
        gg[0],
        g_sq,
        g_sk,
        g_sv,
        g_so,
        gg[1],
        g_cq,
        g_ck,
        g_cv,
        g_co,
        gg[2],
        g_gate,
        g_up,
        g_down,
    )


def solution(mesh):
    shape = mesh.devices.shape
    mesh = jax.sharding.Mesh(
        mesh.devices.reshape(shape[0] // 8, 2, 2, 2, shape[1]),
        ("group", "y", "x", "core", "fsdp"),
    )
    every = ("group", "y", "x", "core", "fsdp")
    rows = P(every, None, None)
    gain, weight = P("fsdp"), P("fsdp", None)
    weights = (gain, weight, weight, weight, weight) * 2 + (gain, weight, weight, weight)
    return jax.shard_map(
        on_device,
        mesh=mesh,
        in_specs=(rows, rows, P(every), P(every, None), rows) + weights,
        out_specs=(rows, rows, rows) + weights,
        check_vma=False,
    )
```

```python
import functools

import jax
import jax.numpy as jnp
from jax import lax
from jax.experimental import pallas as pl
from jax.experimental.pallas import tpu as pltpu
from jax.sharding import PartitionSpec as P

HEAD_DIM = 64
QUAD = 4
WIDE = HEAD_DIM * QUAD
EPSILON = 1e-06
MASKED = -1e30
SCALE = 0.125
VMEM_LIMIT = 56 * 1024 * 1024

C_LONG = 100
C_SEG1 = 20

BF16 = jnp.bfloat16
F32 = jnp.float32


def params():
    return pltpu.CompilerParams(vmem_limit_bytes=VMEM_LIMIT)


def dot(a, b, dims):
    return lax.dot_general(a, b, (dims, ((), ())), preferred_element_type=F32)


def stack_heads(value):
    lane = lax.broadcasted_iota(jnp.int32, value.shape, 1) // HEAD_DIM
    zero = jnp.zeros_like(value)
    return jnp.concatenate([jnp.where(lane == j, value, zero) for j in range(QUAD)], axis=0)


def join_heads(stacked):
    rows = stacked.shape[0] // QUAD
    lane = lax.broadcasted_iota(jnp.int32, (rows, WIDE), 1) // HEAD_DIM
    out = stacked[:rows]
    for j in range(1, QUAD):
        out = jnp.where(lane == j, stacked[j * rows : (j + 1) * rows], out)
    return out


def causal_mask(rows, keys, length):
    t = lax.broadcasted_iota(jnp.int32, (rows, keys), 0)
    u = lax.broadcasted_iota(jnp.int32, (rows, keys), 1)
    one = (u <= t) & (u < length)
    return jnp.concatenate([one] * QUAD, axis=0)


def forward_quad(q, k, v, allowed):
    stacked = stack_heads(q)
    scores = dot(stacked, k, ((1,), (1,))) * SCALE
    scores = jnp.where(allowed, scores, MASKED)
    top = jnp.max(scores, axis=-1, keepdims=True)
    lifted = jnp.exp(scores - top)
    total = jnp.sum(lifted, axis=-1, keepdims=True)
    probs = (lifted / total).astype(BF16)
    mixed = join_heads(dot(probs, v, ((1,), (0,))))
    return probs, mixed.astype(BF16)


def backward_quad(q, k, v, probs, grad, allowed):
    q_stack = stack_heads(q)
    g_stack = stack_heads(grad)
    grad_v = dot(probs, g_stack, ((0,), (0,)))
    grad_p = dot(g_stack, v, ((1,), (1,)))
    p = probs.astype(F32)
    inner = jnp.sum(grad_p * p, axis=-1, keepdims=True)
    grad_s = p * (grad_p - inner)
    if allowed is not None:
        grad_s = jnp.where(allowed, grad_s, 0.0)
    grad_s = grad_s.astype(BF16)
    grad_q = join_heads(dot(grad_s, k, ((1,), (0,)))) * SCALE
    grad_k = dot(grad_s, q_stack, ((0,), (0,))) * SCALE
    return grad_q.astype(BF16), grad_k.astype(BF16), grad_v.astype(BF16)


def self_forward_kernel(lengths, qkv_ref, o_ref, p_ref):
    rows, width = o_ref.shape[1], o_ref.shape[2]
    allowed = causal_mask(rows, rows, lengths[pl.program_id(0)])
    for h in range(width // WIDE):
        c = h * WIDE
        probs, mixed = forward_quad(
            qkv_ref[0, :, c : c + WIDE],
            qkv_ref[0, :, width + c : width + c + WIDE],
            qkv_ref[0, :, 2 * width + c : 2 * width + c + WIDE],
            allowed,
        )
        o_ref[0, :, c : c + WIDE] = mixed
        p_ref[0, h] = probs


def self_forward(qkv, lengths):
    items, rows, width3 = qkv.shape
    width = width3 // 3
    quads = width // WIDE
    return pl.pallas_call(
        self_forward_kernel,
        grid_spec=pltpu.PrefetchScalarGridSpec(
            num_scalar_prefetch=1,
            grid=(items,),
            in_specs=[pl.BlockSpec((1, rows, width3), lambda i, s: (i, 0, 0))],
            out_specs=[
                pl.BlockSpec((1, rows, width), lambda i, s: (i, 0, 0)),
                pl.BlockSpec((1, quads, QUAD * rows, rows), lambda i, s: (i, 0, 0, 0)),
            ],
        ),
        out_shape=[
            jax.ShapeDtypeStruct((items, rows, width), BF16),
            jax.ShapeDtypeStruct((items, quads, QUAD * rows, rows), BF16),
        ],
        compiler_params=params(),
        cost_estimate=cost(0.1),
    )(lengths, qkv)


def self_backward_kernel(qkv_ref, p_ref, g_ref, *refs):
    d_ref = refs[-1]
    width = g_ref.shape[2]
    for h in range(width // WIDE):
        c = h * WIDE
        grad_q, grad_k, grad_v = backward_quad(
            qkv_ref[0, :, c : c + WIDE],
            qkv_ref[0, :, width + c : width + c + WIDE],
            qkv_ref[0, :, 2 * width + c : 2 * width + c + WIDE],
            p_ref[0, h],
            g_ref[0, :, c : c + WIDE],
            None,
        )
        d_ref[0, :, c : c + WIDE] = grad_q
        d_ref[0, :, width + c : width + c + WIDE] = grad_k
        d_ref[0, :, 2 * width + c : 2 * width + c + WIDE] = grad_v


def self_backward(order, qkv, probs, grad):
    items, rows, width3 = qkv.shape
    width = width3 // 3
    quads = width // WIDE
    waits = order.take()
    out = pl.pallas_call(
        self_backward_kernel,
        grid=(items,),
        in_specs=[
            pl.BlockSpec((1, rows, width3), lambda i: (i, 0, 0)),
            pl.BlockSpec((1, quads, QUAD * rows, rows), lambda i: (i, 0, 0, 0)),
            pl.BlockSpec((1, rows, width), lambda i: (i, 0, 0)),
        ]
        + [pl.BlockSpec(memory_space=pl.ANY)] * len(waits),
        out_specs=pl.BlockSpec((1, rows, width3), lambda i: (i, 0, 0)),
        out_shape=jax.ShapeDtypeStruct((items, rows, width3), BF16),
        compiler_params=params(),
        cost_estimate=cost(order.long()),
    )(qkv, probs, grad, *waits)
    return order.after(out)


def cross_forward_kernel(q_ref, kv_ref, m_ref, o_ref, p_ref):
    rows, width = o_ref.shape[1], o_ref.shape[2]
    allowed = m_ref[0] > 0
    for h in range(width // WIDE):
        c = h * WIDE
        probs, mixed = forward_quad(
            q_ref[0, :, c : c + WIDE],
            kv_ref[0, :, c : c + WIDE],
            kv_ref[0, :, width + c : width + c + WIDE],
            allowed,
        )
        o_ref[0, :, c : c + WIDE] = mixed
        p_ref[0, h] = probs


def cross_forward(q, kv, mask):
    items, rows, width = q.shape
    keys = kv.shape[1]
    quads = width // WIDE
    return pl.pallas_call(
        cross_forward_kernel,
        grid=(items,),
        in_specs=[
            pl.BlockSpec((1, rows, width), lambda i: (i, 0, 0)),
            pl.BlockSpec((1, keys, 2 * width), lambda i: (i, 0, 0)),
            pl.BlockSpec((1, 1, keys), lambda i: (i, 0, 0)),
        ],
        out_specs=[
            pl.BlockSpec((1, rows, width), lambda i: (i, 0, 0)),
            pl.BlockSpec((1, quads, QUAD * rows, keys), lambda i: (i, 0, 0, 0)),
        ],
        out_shape=[
            jax.ShapeDtypeStruct((items, rows, width), BF16),
            jax.ShapeDtypeStruct((items, quads, QUAD * rows, keys), BF16),
        ],
        compiler_params=params(),
        cost_estimate=cost(0.1),
    )(q, kv, mask)


def cross_backward_kernel(q_ref, kv_ref, p_ref, g_ref, m_ref, *refs):
    dq_ref, dkv_ref = refs[-2:]
    width = g_ref.shape[2]
    allowed = m_ref[0] > 0
    for h in range(width // WIDE):
        c = h * WIDE
        grad_q, grad_k, grad_v = backward_quad(
            q_ref[0, :, c : c + WIDE],
            kv_ref[0, :, c : c + WIDE],
            kv_ref[0, :, width + c : width + c + WIDE],
            p_ref[0, h],
            g_ref[0, :, c : c + WIDE],
            allowed,
        )
        dq_ref[0, :, c : c + WIDE] = grad_q
        dkv_ref[0, :, c : c + WIDE] = grad_k
        dkv_ref[0, :, width + c : width + c + WIDE] = grad_v


def cross_backward(order, q, kv, probs, grad, mask):
    items, rows, width = q.shape
    keys = kv.shape[1]
    quads = width // WIDE
    waits = order.take()
    out = pl.pallas_call(
        cross_backward_kernel,
        grid=(items,),
        in_specs=[
            pl.BlockSpec((1, rows, width), lambda i: (i, 0, 0)),
            pl.BlockSpec((1, keys, 2 * width), lambda i: (i, 0, 0)),
            pl.BlockSpec((1, quads, QUAD * rows, keys), lambda i: (i, 0, 0, 0)),
            pl.BlockSpec((1, rows, width), lambda i: (i, 0, 0)),
            pl.BlockSpec((1, 1, keys), lambda i: (i, 0, 0)),
        ]
        + [pl.BlockSpec(memory_space=pl.ANY)] * len(waits),
        out_specs=[
            pl.BlockSpec((1, rows, width), lambda i: (i, 0, 0)),
            pl.BlockSpec((1, keys, 2 * width), lambda i: (i, 0, 0)),
        ],
        out_shape=[
            jax.ShapeDtypeStruct((items, rows, width), BF16),
            jax.ShapeDtypeStruct((items, keys, 2 * width), BF16),
        ],
        compiler_params=params(),
        cost_estimate=cost(order.long()),
    )(q, kv, probs, grad, mask, *waits)
    order.after(out[0])
    return out


def factor_of(value):
    return lax.rsqrt(jnp.mean(value * value, axis=-1, keepdims=True) + EPSILON)


def matmul(left, right):
    return jnp.dot(left, right, preferred_element_type=F32)


AXES = {1: "core", 2: "x", 4: "y"}


def swap(value, bit):
    return lax.ppermute(value, AXES[bit], [(0, 1), (1, 0)])


class Order:
    def __init__(self):
        self.waits, self.micros = [], 0.1

    def long(self):
        micros, self.micros = self.micros, 0.1
        return micros

    def take(self):
        waits, self.waits = self.waits, []
        return waits

    def after(self, array):
        self.waits.append(array)
        return array


def hold_kernel(*refs):
    pass


def hold(order, array):
    whole = pl.BlockSpec(memory_space=pl.ANY)
    waits = order.take()
    out = pl.pallas_call(
        hold_kernel,
        in_specs=[whole] * (1 + len(waits)),
        out_specs=whole,
        out_shape=jax.ShapeDtypeStruct(array.shape, array.dtype),
        input_output_aliases={0: 0},
        compiler_params=pltpu.CompilerParams(vmem_limit_bytes=1024 * 1024),
        cost_estimate=cost(order.long()),
    )(array, *waits)
    return order.after(out)


def cost(micros):
    return pl.CostEstimate(
        flops=int(micros * 1.15e9), bytes_accessed=int(micros * 3.6e6), transcendentals=0
    )


def put_split(value, flag, axis, give_ref, keep_ref):
    half = value.shape[axis] // 2
    low, high = (value[:half], value[half:]) if axis == 0 else (value[:, :half], value[:, half:])

    @pl.when(flag == 0)
    def _():
        keep_ref[...] = low
        give_ref[...] = high

    @pl.when(flag > 0)
    def _():
        keep_ref[...] = high
        give_ref[...] = low


def product_kernel(jobs, has_add, axis, halves, flags, *refs):
    outs = refs[-halves * 2 :] if has_add else refs[-1:]
    add_ref = refs[sum(count + 1 for count, _, _ in jobs)]
    at = 0
    total = sum(steps for _, _, steps in jobs)
    for count, start, steps in jobs:
        lefts, right = refs[at : at + count], refs[at + count]
        at += count + 1

        def work(lefts=lefts, right=right, start=start):
            left = jnp.concatenate([r[...] for r in lefts], axis=1)
            value = right[0] if len(right.shape) == 3 else right[...]
            out = dot(left, value, ((0,), (0,)))
            if not has_add:
                outs[0][...] = out.astype(BF16)
                return
            out = (out + add_ref[...].astype(F32)).astype(BF16)
            if axis == 1:
                put_split(out, flags[1], 1, *outs)
                return
            which = 2 * start // total if halves > 1 else 0
            give, keep = outs[2 * which : 2 * which + 2]
            for z in range(give.shape[0]):
                part = out[128 * z : 128 * z + 128]
                put_split(part, flags[1 + which], 0, give.at[z], keep.at[z])

        if len(jobs) == 1:
            work()
        else:
            step = pl.program_id(0)
            pl.when((step >= start) & (step < start + steps))(work)


def call_product(order, axis, grid, jobs, flags, specs, operands, out_specs, out_shapes):
    waits = order.take()
    has_add = len(out_shapes) > 1
    out = pl.pallas_call(
        functools.partial(product_kernel, jobs, has_add, axis, len(out_shapes) // 2),
        grid_spec=pltpu.PrefetchScalarGridSpec(
            num_scalar_prefetch=1,
            grid=grid,
            in_specs=specs + [pl.BlockSpec(memory_space=pl.ANY)] * len(waits),
            out_specs=out_specs,
        ),
        out_shape=out_shapes,
        compiler_params=params(),
        cost_estimate=cost(order.long()),
    )(flags, *operands, *waits)
    order.after(out[0])
    return out


def grad_rows(order, pairs, flags, add=None):
    count = pairs[0][0].shape[1] // 256
    total = sum(columns for _, _, _, columns in pairs)
    tile = next(t for t in (1408, 1024) if all(c % t == 0 for _, _, _, c in pairs))
    specs, operands, jobs, start = [], [], [], 0
    for left, right, place, columns in pairs:
        rows, steps = left.shape[0], columns // tile
        specs += [
            pl.BlockSpec((rows, 128), lambda j, f, z=z: (0, 2 * z + f[0])) for z in range(count)
        ]
        block = lambda j, f, start=start, steps=steps: jnp.clip(j - start, 0, steps - 1)
        if right.ndim == 3:
            specs.append(
                pl.BlockSpec((1, rows, tile), lambda j, f, b=block, p=place: (p, 0, b(j, f)))
            )
        else:
            specs.append(
                pl.BlockSpec((rows, tile), lambda j, f, b=block, p=place: (0, p + b(j, f)))
            )
        operands += [left] * count + [right]
        jobs.append((count, start, steps))
        start += steps
    block = pl.BlockSpec((count * 128, tile), lambda j, f: (0, j))
    if add is None:
        shapes, outs = [jax.ShapeDtypeStruct((count * 128, total), BF16)], [block]
    else:
        specs.append(block)
        operands.append(add)
        halves = flags.shape[0] - 1
        shapes = [jax.ShapeDtypeStruct((count, 64, total // halves), BF16)] * (2 * halves)
        outs, most = [], start // halves
        for i in range(halves):
            place = lambda j, f, i=i: (0, 0, jnp.clip(j - i * most, 0, most - 1))
            outs += [pl.BlockSpec((count, 64, tile), place)] * 2
    return call_product(order, 0, (start,), jobs, flags, specs, operands, outs, shapes)


def grad_columns(order, left, right, flags, add=None):
    rows, width = left.shape
    half = right.shape[1] // 2
    tile = next(t for t in (1408, 1024) if width % t == 0)
    block = lambda columns: pl.BlockSpec((tile, columns), lambda j, f: (j, 0))
    specs = [
        pl.BlockSpec((rows, tile), lambda j, f: (0, j)),
        pl.BlockSpec((rows, half), lambda j, f: (0, f[0])),
    ]
    operands = [left, right]
    if add is None:
        shapes, outs = [jax.ShapeDtypeStruct((width, half), BF16)], [block(half)]
    else:
        specs.append(block(half))
        operands.append(add)
        shapes = [jax.ShapeDtypeStruct((width, half // 2), BF16)] * 2
        outs = [block(half // 2)] * 2
    steps = width // tile
    return call_product(
        order, 1, (steps,), [(1, 0, steps)], flags, specs, operands, outs, shapes
    )


def land_kernel(count, axis, flags, *refs):
    outs = refs[len(refs) - (2 * count if axis is not None else 1) :]
    column = 0
    for i in range(count):
        total = refs[2 * i][...] + refs[2 * i + 1][...]
        if axis is None:
            columns = total.shape[-1]
            outs[0][..., column : column + columns] = total
            column += columns
        elif axis == 1:
            put_split(total, flags[i], 1, *outs[2 * i : 2 * i + 2])
        else:
            for z in range(total.shape[0]):
                put_split(
                    total[z], flags[i], 0, outs[2 * i].at[z], outs[2 * i + 1].at[z]
                )


def land_sums(order, pairs, flags, axis):
    waits = order.take()
    steps = 2
    block = lambda shape: pl.BlockSpec(
        (shape[0] // steps, *shape[1:]), lambda j, f: (j,) + (0,) * (len(shape) - 1)
    )
    specs, operands, shapes = [], [], []
    for keep, got in pairs:
        specs += [block(keep.shape)] * 2
        operands += [keep, got]
        shape = list(keep.shape)
        if axis is not None:
            shape[-2 if axis == 0 else -1] //= 2
            shapes += [tuple(shape)] * 2
    if axis is None:
        total = sum(keep.shape[-1] for keep, _ in pairs)
        shapes = [(*pairs[0][0].shape[:-1], total)]
    out = pl.pallas_call(
        functools.partial(land_kernel, len(pairs), axis),
        grid_spec=pltpu.PrefetchScalarGridSpec(
            num_scalar_prefetch=1,
            grid=(steps,),
            in_specs=specs + [pl.BlockSpec(memory_space=pl.ANY)] * len(waits),
            out_specs=[block(shape) for shape in shapes],
        ),
        out_shape=[jax.ShapeDtypeStruct(shape, BF16) for shape in shapes],
        compiler_params=params(),
        cost_estimate=cost(order.long()),
    )(jnp.stack(flags), *operands, *waits)
    order.after(out[0])
    return out


def join_kernel(axis, parts, turned, flag, own_ref, got_ref, *refs):
    outs = refs[len(refs) - len(parts) :]
    half = own_ref.shape[axis]

    def put(low, high):
        column = 0
        for out, columns, turn in zip(outs, parts, turned):
            at = slice(column, column + columns)
            column += columns
            for start, ref in ((0, low), (half, high)):
                value = ref[:, at].astype(out.dtype)
                if axis == 1:
                    out[:, start : start + half] = value
                elif turn:
                    n = half // 4
                    for i, j in enumerate((0, 2, 1, 3)):
                        out[start + j * n : start + (j + 1) * n] = value[i * n : (i + 1) * n]
                else:
                    out[start : start + half] = value

    either(flag[0], put, own_ref, got_ref)


def land_join(order, own, got, flag, axis, parts, turned, kind):
    waits = order.take()
    whole = lambda shape: pl.BlockSpec(shape, lambda j, f: (0, 0))
    n, c = own.shape
    shapes = [(2 * n, columns) for columns in parts] if axis == 0 else [(n, 2 * c)]
    out = pl.pallas_call(
        functools.partial(join_kernel, axis, parts, turned),
        grid_spec=pltpu.PrefetchScalarGridSpec(
            num_scalar_prefetch=1,
            grid=(1,),
            in_specs=[whole(own.shape)] * 2 + [pl.BlockSpec(memory_space=pl.ANY)] * len(waits),
            out_specs=[whole(shape) for shape in shapes],
        ),
        out_shape=[jax.ShapeDtypeStruct(shape, kind) for shape in shapes],
        compiler_params=params(),
        cost_estimate=cost(order.long()),
    )(flag.reshape(1), own, got, *waits)
    order.after(out[0])
    return out


def segment_kernel(steps, has_next, waits, *refs):
    x_ref, w_ref, v_ref, b_ref, g_ref = refs[:5]
    n_ref = refs[5] if has_next else None
    refs = refs[5 + has_next + waits :]
    if has_next:
        d_ref, gg_ref, e_ref, o_ref, acc = refs
    else:
        d_ref, gg_ref, acc = refs
    step = pl.program_id(0)
    x = x_ref[0] if len(x_ref.shape) == 3 else x_ref[...]
    partial = dot(x, w_ref[...], ((1,), (1,)))

    @pl.when(step == 0)
    def _():
        acc[...] = partial

    @pl.when(step > 0)
    def _():
        acc[...] += partial

    @pl.when(step == steps - 1)
    def _():
        gain = g_ref[...]
        rows, chunk = acc.shape[0], 144
        gg_ref[...] = jnp.zeros_like(gg_ref)

        @pl.loop(0, rows // chunk)
        def _(i):
            at = pl.ds(pl.multiple_of(i * chunk, chunk), chunk)
            grad = acc[at, :]
            value = v_ref[at, :].astype(F32)
            factor = lax.rsqrt(jnp.mean(value * value, axis=-1, keepdims=True) + EPSILON)
            scaled = gain * grad
            along = jnp.mean(scaled * value, axis=-1, keepdims=True)
            back = factor * scaled - value * (factor * factor * factor * along)
            gg_ref[...] += jnp.sum(grad * value * factor, axis=0, keepdims=True)
            total = b_ref[at, :].astype(F32) + back
            d_ref[at, :] = total
            if has_next:
                e_ref[at, :] = total.astype(BF16)

        if has_next:
            o_ref[...] = dot(e_ref[...], n_ref[...], ((1,), (1,))).astype(BF16)


def segment(order, x, w, column, tile, value, base, gain, after=None):
    rows, width = value.shape
    steps = x.shape[-1] * (x.shape[0] if x.ndim == 3 else 1) // tile
    if x.ndim == 3:
        per = x.shape[-1] // tile
        x_spec = pl.BlockSpec((1, rows, tile), lambda k: (k // per, 0, k % per))
    else:
        x_spec = pl.BlockSpec((rows, tile), lambda k: (0, k))
    whole = pl.BlockSpec((rows, width), lambda k: (0, 0))
    line = pl.BlockSpec((1, width), lambda k: (0, 0))
    specs = [x_spec, pl.BlockSpec((width, tile), lambda k: (0, k + column)), whole, whole, line]
    operands = [x, w, value, base, gain.reshape(1, width)]
    shapes = [
        jax.ShapeDtypeStruct((rows, width), F32),
        jax.ShapeDtypeStruct((1, width), F32),
    ]
    outs = [whole, line]
    if after is not None:
        matrix, at = after
        specs.append(pl.BlockSpec((width, width), lambda k: (0, at)))
        operands.append(matrix)
        shapes += [jax.ShapeDtypeStruct((rows, width), BF16)] * 2
        outs += [whole, whole]
    waits = order.take()
    out = pl.pallas_call(
        functools.partial(segment_kernel, steps, after is not None, len(waits)),
        grid=(steps,),
        in_specs=specs + [pl.BlockSpec(memory_space=pl.ANY)] * len(waits),
        out_specs=outs,
        out_shape=shapes,
        scratch_shapes=[pltpu.VMEM((rows, width), F32)],
        compiler_params=params(),
        cost_estimate=cost(order.long()),
    )(*operands, *waits)
    order.after(out[1])
    return out


def mlp_kernel(a_ref, e_ref, wg_ref, wu_ref, wd_ref, i_ref, d_ref):
    grad = dot(e_ref[...], wd_ref[...], ((1,), (1,)))
    gate = dot(a_ref[...], wg_ref[...], ((1,), (0,)))
    up = dot(a_ref[...], wu_ref[...], ((1,), (0,)))
    slope, cubic = 0.7978845608028654, 0.044715
    square = gate * gate
    bend = jnp.tanh(slope * gate * (1.0 + cubic * square))
    half = 0.5 * (1.0 + bend)
    act = gate * half
    turn = half + 0.5 * gate * (1.0 - bend * bend) * slope * (1.0 + 3.0 * cubic * square)
    i_ref[...] = (act * up).astype(BF16)
    d_ref[0] = (grad * up * turn).astype(BF16)
    d_ref[1] = (grad * act).astype(BF16)


def mlp(order, a3, e3, w_wide, w_down):
    rows, width = a3.shape
    hidden = w_down.shape[0]
    tile = 256
    count = hidden // tile
    whole = pl.BlockSpec((rows, width), lambda j: (0, 0))
    return pl.pallas_call(
        mlp_kernel,
        grid=(count,),
        in_specs=[
            whole,
            whole,
            pl.BlockSpec((width, tile), lambda j: (0, j)),
            pl.BlockSpec((width, tile), lambda j: (0, count + j)),
            pl.BlockSpec((tile, width), lambda j: (j, 0)),
        ],
        out_specs=[
            pl.BlockSpec((rows, tile), lambda j: (0, j)),
            pl.BlockSpec((2, rows, tile), lambda j: (0, 0, j)),
        ],
        out_shape=[
            jax.ShapeDtypeStruct((rows, hidden), BF16),
            jax.ShapeDtypeStruct((2, rows, hidden), BF16),
        ],
        compiler_params=params(),
        cost_estimate=cost(order.long()),
    )(a3, e3, w_wide, w_wide, w_down)


def forward_out_kernel(steps, waits, x_ref, w_ref, b_ref, *refs):
    o_ref, acc = refs[waits:]
    step = pl.program_id(0)
    partial = dot(x_ref[...], w_ref[...], ((1,), (0,)))

    @pl.when(step == 0)
    def _():
        acc[...] = partial + b_ref[...]

    @pl.when(step > 0)
    def _():
        acc[...] += partial

    @pl.when(step == steps - 1)
    def _():
        o_ref[...] = acc[...].astype(BF16)


def forward_out(order, x, w, base):
    rows, width = base.shape
    tile = next(t for t in (1408, 1024) if w.shape[0] % t == 0)
    steps = w.shape[0] // tile
    whole = pl.BlockSpec((rows, width), lambda k: (0, 0))
    waits = order.take()
    out = pl.pallas_call(
        functools.partial(forward_out_kernel, steps, len(waits)),
        grid=(steps,),
        in_specs=[
            pl.BlockSpec((rows, tile), lambda k: (0, k)),
            pl.BlockSpec((tile, width), lambda k: (k, 0)),
            whole,
        ]
        + [pl.BlockSpec(memory_space=pl.ANY)] * len(waits),
        out_specs=whole,
        out_shape=jax.ShapeDtypeStruct((rows, width), BF16),
        scratch_shapes=[pltpu.VMEM((rows, width), F32)],
        compiler_params=params(),
        cost_estimate=cost(order.long()),
    )(x, w, base, *waits)
    return order.after(out)


def back_product_kernel(waits, x_ref, w_ref, *refs):
    refs[-1][...] = dot(x_ref[...], w_ref[...], ((1,), (1,)))


def back_product(order, x, w):
    rows, depth = x.shape
    width = w.shape[0]
    tile = 256
    waits = order.take()
    out = pl.pallas_call(
        functools.partial(back_product_kernel, len(waits)),
        grid=(width // tile,),
        in_specs=[
            pl.BlockSpec((rows, depth), lambda j: (0, 0)),
            pl.BlockSpec((tile, depth), lambda j: (j, 0)),
        ]
        + [pl.BlockSpec(memory_space=pl.ANY)] * len(waits),
        out_specs=pl.BlockSpec((rows, tile), lambda j: (0, j)),
        out_shape=jax.ShapeDtypeStruct((rows, width), F32),
        compiler_params=params(),
        cost_estimate=cost(order.long()),
    )(x, w, *waits)
    return order.after(out)


def bit_of(spot, bit):
    return (spot // bit) % 2


class Sum:
    def __init__(self, order, spot, axis, product, first, second):
        self.order, self.axis, self.product = order, axis, product
        self.first, self.second = first, second
        self.bits = bit_of(spot, 1), bit_of(spot, first), bit_of(spot, second)
        core, one, _ = self.bits
        (give,) = product(jnp.stack([1 - core, one]))
        self.flight = swap(give, 1)

    def core(self):
        core, one, _ = self.bits
        give, self.keep = self.product(jnp.stack([core, one]), self.flight)
        self.flight = swap(give, self.first)


class Part:
    def __init__(self, spot, first, second):
        self.first, self.second, self.axis = first, second, 0
        self.bits = bit_of(spot, 1), bit_of(spot, first), bit_of(spot, second)


class Pair:
    def __init__(self, order, spot, pairs):
        self.product = functools.partial(grad_rows, order, pairs)
        self.parts = [Part(spot, 2, 4), Part(spot, 4, 2)]
        self.flags = [bit_of(spot, b) for b in (1, 2, 4)]
        core, one, two = self.flags
        (give,) = self.product(jnp.stack([1 - core, one, two]))
        self.flight = swap(give, 1)

    def core(self):
        core, one, two = self.flags
        out = self.product(jnp.stack([core, one, two]), self.flight)
        for i, part in enumerate(self.parts):
            part.keep = out[2 * i + 1]
            part.flight = swap(out[2 * i], part.first)
        return self.parts


def region(axis, first, cross):
    return (first, cross) if axis == 0 else (cross, first)


def either(flag, put, one, two):
    pl.when(flag == 0)(lambda: put(one, two))
    pl.when(flag > 0)(lambda: put(two, one))


def cut_kernel(axis, z_ref, *refs):
    a_ref, b_ref = refs[-2:]
    half = z_ref.shape[2 - axis] // 2
    a_ref[0] = z_ref.at[0][region(axis, slice(None), slice(0, half))]
    b_ref[0] = z_ref.at[0][region(axis, slice(None), slice(half, None))]


def cut(order, value, axis, column, columns):
    waits = order.take()
    z, n, _ = value.shape
    shape = (z, n, columns // 2) if axis == 0 else (z, n // 2, columns)
    out = pl.pallas_call(
        functools.partial(cut_kernel, axis),
        grid=(z,),
        in_specs=[pl.BlockSpec((1, n, columns), lambda j: (j, 0, column))]
        + [pl.BlockSpec(memory_space=pl.ANY)] * len(waits),
        out_specs=[pl.BlockSpec((1, *shape[1:]), lambda j: (j, 0, 0))] * 2,
        out_shape=[jax.ShapeDtypeStruct(shape, BF16)] * 2,
        compiler_params=params(),
        cost_estimate=cost(order.long()),
    )(value, *waits)
    order.after(out[0])
    return out


def eighth(spot, shard, axis):
    size = shard.shape[axis] // 8
    seat = 4 * bit_of(spot, 1) + 2 * bit_of(spot, 4) + bit_of(spot, 2)
    return lax.dynamic_slice_in_dim(shard, seat * size, size, axis)


def pairs_kernel(axis, flags, *refs):
    ins, outs = refs[:4], refs[-2:]
    for i in range(2):
        size = ins[2 * i].shape[1 + axis]

        def put(low, high, out=outs[i], size=size):
            out.at[0][region(axis, slice(0, size), slice(None))] = low[0]
            out.at[0][region(axis, slice(size, None), slice(None))] = high[0]

        either(flags[i], put, ins[2 * i], ins[2 * i + 1])


def quads_kernel(axis, flags, *refs):
    a_own, a_got, b_own, b_got = refs[:4]
    out = refs[-1].at[0]
    two, half = a_own.shape[1 + axis], a_own.shape[2 - axis]
    n = two // 2

    def put_a(low, high):
        out[region(axis, slice(0, two), slice(0, half))] = low[0]
        out[region(axis, slice(two, None), slice(0, half))] = high[0]

    def put_b(low, high):
        for y in range(2):
            for x, ref in enumerate((low, high)):
                at = (2 * y + x) * n
                out[region(axis, slice(at, at + n), slice(half, None))] = ref.at[0][
                    region(axis, slice(y * n, y * n + n), slice(None))
                ]

    either(flags[1], put_a, a_own, a_got)
    either(flags[0], put_b, b_own, b_got)


def cores_kernel(axis, flags, own_ref, got_ref, *refs):
    out = refs[-1].at[0]
    size = own_ref.shape[1 + axis]

    def put(low, high):
        out[region(axis, slice(0, size), slice(None))] = low[0]
        out[region(axis, slice(size, None), slice(None))] = high[0]

    either(flags[2], put, own_ref, got_ref)


def by_shard(order, kernel, axis, flags, operands, shapes):
    waits = order.take()
    block = lambda shape: pl.BlockSpec((1, *shape[1:]), lambda j, *f: (j, 0, 0))
    out = pl.pallas_call(
        functools.partial(kernel, axis),
        grid_spec=pltpu.PrefetchScalarGridSpec(
            num_scalar_prefetch=len(flags),
            grid=(operands[0].shape[0],),
            in_specs=[block(v.shape) for v in operands]
            + [pl.BlockSpec(memory_space=pl.ANY)] * len(waits),
            out_specs=[block(shape) for shape in shapes],
        ),
        out_shape=[jax.ShapeDtypeStruct(shape, BF16) for shape in shapes],
        compiler_params=params(),
        cost_estimate=cost(order.long()),
    )(*flags, *operands, *waits)
    order.after(out[0])
    return out


class Gather:
    def __init__(self, order, spot, value, axis, column=0, columns=None):
        self.order, self.axis = order, axis
        self.flags = [jnp.stack([bit_of(spot, b) for b in (2, 4, 1)])]
        self.value, self.place = value, (column, columns or value.shape[2])

    def scaled(self, shape, along, across):
        shape = list(shape)
        shape[1 + self.axis] = shape[1 + self.axis] * along
        shape[2 - self.axis] = shape[2 - self.axis] * across // 2
        return tuple(shape)

    def run(self, kernel, flags, operands, shapes):
        return by_shard(self.order, kernel, self.axis, flags, operands, shapes)

    def one(self):
        self.a, self.b = cut(self.order, self.value, self.axis, *self.place)
        self.got = swap(self.a, 2), swap(self.b, 4)

    def two(self):
        shape = self.scaled(self.a.shape, 2, 2)
        self.a, self.b = self.run(
            pairs_kernel, self.flags, [self.a, self.got[0], self.b, self.got[1]], [shape] * 2
        )
        self.got = swap(self.a, 4), swap(self.b, 2)

    def three(self):
        shape = self.scaled(self.a.shape, 2, 4)
        (self.half,) = self.run(
            quads_kernel, self.flags, [self.a, self.got[0], self.b, self.got[1]], [shape]
        )
        self.got = swap(self.half, 1)

    def four(self):
        shape = self.scaled(self.half.shape, 2, 2)
        (whole,) = self.run(cores_kernel, self.flags, [self.half, self.got], [shape])
        return whole.reshape(-1, whole.shape[-1])


def land_first(order, *sums):
    out = land_sums(
        order, [(s.keep, s.flight) for s in sums], [s.bits[2] for s in sums], sums[0].axis
    )
    for i, s in enumerate(sums):
        s.keep = out[2 * i + 1]
        s.flight = swap(out[2 * i], s.second)


def land_second(order, *sums):
    (out,) = land_sums(
        order, [(s.keep, s.flight) for s in sums], [s.bits[2] for s in sums], None
    )
    return out.reshape(-1, out.shape[-1])


def over_shards(value):
    value = lax.psum_scatter(value, "fsdp", scatter_dimension=0, tiled=True)
    return across_groups(value)


def across_groups(value):
    size = lax.axis_size("group")
    ring = [(i, (i + 1) % size) for i in range(size)]
    total = step = value
    for _ in range(size - 1):
        step = lax.ppermute(step, "group", ring)
        total = total + step
    return total


class Spread:
    def __init__(self, order, spot, value, parts, turned, axis=0):
        self.order, self.spot, self.axis = order, spot, axis
        self.value, self.parts, self.turned = value, parts, turned
        self.bits = [4, 2, 1]
        self.send()

    def send(self):
        self.flight = swap(self.value, self.bits[0])

    def land(self):
        bit = self.bits.pop(0)
        last = not self.bits
        out = land_join(
            self.order,
            self.value,
            self.flight,
            bit_of(self.spot, bit),
            self.axis,
            self.parts if last else [self.value.shape[1]],
            self.turned if last else [False],
            F32 if last else BF16,
        )
        if last:
            self.values = out
        else:
            self.value = out[0]
            self.send()


def on_device(
    text,
    memory,
    text_lengths,
    memory_mask,
    grad_out,
    self_gain,
    self_query,
    self_key,
    self_value,
    self_output,
    cross_gain,
    cross_query,
    cross_key,
    cross_value,
    cross_output,
    mlp_gain,
    mlp_gate,
    mlp_up,
    mlp_down,
):
    items, rows, width = text.shape
    keys = memory.shape[1]
    spot = 4 * lax.axis_index("y") + 2 * lax.axis_index("x") + lax.axis_index("core")

    order = Order()
    join = lambda *parts: jnp.concatenate(parts, axis=1)
    gather = lambda value: lax.all_gather(value, "fsdp", axis=0)
    g_down = Gather(order, spot, gather(eighth(spot, mlp_down, 1)), 1)
    own = self_gain.shape[0]
    lines = jnp.stack([self_gain, cross_gain, mlp_gain]).reshape(-1, 128)
    squares = [
        self_query,
        self_key,
        self_value,
        self_output,
        cross_key,
        cross_value,
        cross_query,
        cross_output,
    ]
    lines = jnp.pad(lines, ((0, width // 32 - lines.shape[0]), (0, 0)))
    both = gather(join(*[eighth(spot, w, 0) for w in squares], lines))
    g_self = Gather(order, spot, both, 0, 0, 4 * width)
    g_cross = Gather(order, spot, both, 0, 1, 4 * width)
    shards = both.shape[0]
    gains = both[:, : 3 * own // 128, 8 * width :].reshape(shards, 3, own)
    gains = gains.transpose(1, 0, 2).reshape(3, width).astype(F32)
    g_wide = Gather(
        order, spot, gather(join(eighth(spot, mlp_gate, 0), eighth(spot, mlp_up, 0))), 0
    )
    hidden = mlp_gate.shape[1]

    x = text.reshape(-1, width).astype(F32)
    flat_memory = memory.reshape(-1, width)
    e3 = grad_out.reshape(-1, width)
    mask = memory_mask[:, None, :]

    g_down.one()
    g_down.two()
    g_self.one()
    g_cross.one()
    order.micros = C_LONG
    g_down.three()
    g_self.two()
    g_cross.two()
    order.micros = C_LONG
    w_down = g_down.four()
    g_wide.one()
    g_self.three()
    w_self = g_self.four()
    w_qkv, w_so = w_self[:, : 3 * width], w_self[:, 3 * width :]
    c1 = factor_of(x)
    a1 = (x * c1 * gains[0]).astype(BF16)
    qkv = matmul(a1, w_qkv).astype(BF16).reshape(items, rows, 3 * width)
    o1, p1 = self_forward(qkv, text_lengths)
    o1 = order.after(o1).reshape(-1, width)
    g_wide.two()
    g_cross.three()
    h1 = x + matmul(o1, w_so)
    c2 = factor_of(h1)
    a2 = (h1 * c2 * gains[1]).astype(BF16)
    order.after(a2)
    order.micros = C_LONG
    w_cross = g_cross.four()
    w_kv = w_cross[:, : 2 * width]
    w_cq, w_co = w_cross[:, 2 * width : 3 * width], w_cross[:, 3 * width :]
    kv = matmul(flat_memory, w_kv).astype(BF16).reshape(items, keys, 2 * width)
    q2 = matmul(a2, w_cq).astype(BF16).reshape(items, rows, width)
    o2, p2 = cross_forward(q2, kv, mask)
    o2 = order.after(o2).reshape(-1, width)
    g_wide.three()
    h2 = h1 + matmul(o2, w_co)
    c3 = factor_of(h2)
    a3 = (h2 * c3 * gains[2]).astype(BF16)
    order.after(a3)
    w_wide = g_wide.four()
    inner, d_wide = mlp(order, a3, e3, w_wide, w_down)
    order.take()

    sum_of = lambda first, second, pairs: Sum(
        order, spot, 0, functools.partial(grad_rows, order, pairs), first, second
    )
    s_gate = sum_of(2, 4, [(a3, d_wide, 0, hidden)])
    s_up = sum_of(4, 2, [(a3, d_wide, 1, hidden)])
    s_down = Sum(order, spot, 1, functools.partial(grad_columns, order, inner, e3), 2, 4)
    s_gate.core()
    s_up.core()
    order.micros = C_LONG
    d_h2, gg3, e2, d_o2 = segment(
        order, d_wide, w_wide, 0, hidden // 2, h2, e3, gains[2], (w_cross, 3)
    )
    d_q2, d_kv = cross_backward(order, q2, kv, p2, d_o2.reshape(text.shape), mask)
    d_q2 = d_q2.reshape(-1, width)
    d_kv = d_kv.reshape(-1, 2 * width)
    s_cross = Pair(
        order,
        spot,
        [
            (flat_memory, d_kv, 0, 2 * width),
            (a2, d_q2, 0, width),
            (o2, e2, 0, width),
        ],
    )
    s_down.core()
    land_first(order, s_gate, s_up)
    order.micros = C_LONG
    d_h1, gg2, e1, d_o1 = segment(
        order, d_q2, w_cross, 4, width // 2, h1, d_h2, gains[1], (w_self, 3)
    )
    d_qkv = self_backward(order, qkv, p1, d_o1.reshape(text.shape)).reshape(-1, 3 * width)
    s_self = Pair(
        order,
        spot,
        [
            (a1, d_qkv, 0, 2 * width),
            (a1, d_qkv, 2, width),
            (o1, e1, 0, width),
        ],
    )
    cross = s_cross.core()
    land_first(order, s_down)
    z_wide = over_shards(land_second(order, s_gate, s_up))
    order.micros = C_LONG
    grad_memory = back_product(order, d_kv, w_cross)
    both = s_self.core()
    land_first(order, *cross)
    z_down = over_shards(land_second(order, s_down))
    order.micros = C_SEG1
    grad_text, gg1 = segment(order, d_qkv, w_self, 0, width, x, d_h1, gains[0])
    z_wide = hold(order, z_wide)
    t_wide = Spread(order, spot, z_wide, [hidden, hidden], [False, True])
    z_down = hold(order, z_down)
    z_cross = over_shards(land_second(order, *cross))
    land_first(order, *both)
    lines = jnp.concatenate([gg1, gg2, gg3]).reshape(3, shards, own).transpose(1, 0, 2)
    lines = lines.reshape(shards, -1, 128)
    lines = jnp.pad(lines, ((0, 0), (0, width // 32 - lines.shape[1]), (0, 0)))
    lines = order.after(lines.astype(BF16).reshape(-1, 128))
    order.micros = C_LONG
    t_wide.land()
    z_self = land_second(order, *both)
    z_self = over_shards(jnp.concatenate([z_self, lines], axis=1))
    z_cross = hold(order, z_cross)
    order.micros = C_LONG
    block_out = forward_out(order, inner, w_down, h2)
    squares = [width] * 4
    t_cross = Spread(order, spot, z_cross, squares, [False, False, True, True])
    t_down = Spread(order, spot, z_down, [width], [False], 1)
    t_wide.land()
    t_cross.land()
    t_down.land()
    t_wide.land()
    t_cross.land()
    z_self = hold(order, z_self)
    t_self = Spread(
        order, spot, z_self, [*squares, 128], [False, False, True, True, False]
    )
    t_down.land()
    t_cross.land()
    t_self.land()
    t_down.land()
    t_self.land()
    t_self.land()
    g_gate, g_up = t_wide.values
    (g_down,) = t_down.values
    g_ck, g_cv, g_cq, g_co = t_cross.values
    g_sq, g_sk, g_sv, g_so, lines = t_self.values
    lines = jnp.sum(lines.reshape(8, -1, 128), axis=0)
    gg = lines[: 3 * own // 128].reshape(3, own)

    return (
        block_out.reshape(text.shape),
        grad_text.reshape(text.shape),
        grad_memory.reshape(memory.shape),
        gg[0],
        g_sq,
        g_sk,
        g_sv,
        g_so,
        gg[1],
        g_cq,
        g_ck,
        g_cv,
        g_co,
        gg[2],
        g_gate,
        g_up,
        g_down,
    )


def solution(mesh):
    shape = mesh.devices.shape
    mesh = jax.sharding.Mesh(
        mesh.devices.reshape(shape[0] // 8, 2, 2, 2, shape[1]),
        ("group", "y", "x", "core", "fsdp"),
    )
    every = ("group", "y", "x", "core", "fsdp")
    rows = P(every, None, None)
    gain, weight = P("fsdp"), P("fsdp", None)
    weights = (gain, weight, weight, weight, weight) * 2 + (gain, weight, weight, weight)
    return jax.shard_map(
        on_device,
        mesh=mesh,
        in_specs=(rows, rows, P(every), P(every, None), rows) + weights,
        out_specs=(rows, rows, rows) + weights,
        check_vma=False,
    )
```

```python
import functools

import jax
import jax.numpy as jnp
from jax import lax
from jax.experimental import pallas as pl
from jax.experimental.pallas import tpu as pltpu
from jax.sharding import PartitionSpec as P

HEAD_DIM = 64
QUAD = 4
WIDE = HEAD_DIM * QUAD
EPSILON = 1e-06
MASKED = -1e30
SCALE = 0.125
VMEM_LIMIT = 56 * 1024 * 1024

C_LONG = 100
MLP_TILE = 256
C_SEG2 = 11
C_MID = 8

BF16 = jnp.bfloat16
F32 = jnp.float32


def params():
    return pltpu.CompilerParams(vmem_limit_bytes=VMEM_LIMIT)


def dot(a, b, dims):
    return lax.dot_general(a, b, (dims, ((), ())), preferred_element_type=F32)


def stack_heads(value):
    lane = lax.broadcasted_iota(jnp.int32, value.shape, 1) // HEAD_DIM
    zero = jnp.zeros_like(value)
    return jnp.concatenate([jnp.where(lane == j, value, zero) for j in range(QUAD)], axis=0)


def join_heads(stacked):
    rows = stacked.shape[0] // QUAD
    lane = lax.broadcasted_iota(jnp.int32, (rows, WIDE), 1) // HEAD_DIM
    out = stacked[:rows]
    for j in range(1, QUAD):
        out = jnp.where(lane == j, stacked[j * rows : (j + 1) * rows], out)
    return out


def causal_mask(rows, keys, length):
    t = lax.broadcasted_iota(jnp.int32, (rows, keys), 0)
    u = lax.broadcasted_iota(jnp.int32, (rows, keys), 1)
    one = (u <= t) & (u < length)
    return jnp.concatenate([one] * QUAD, axis=0)


def forward_quad(q, k, v, allowed):
    stacked = stack_heads(q)
    scores = dot(stacked, k, ((1,), (1,))) * SCALE
    scores = jnp.where(allowed, scores, MASKED)
    top = jnp.max(scores, axis=-1, keepdims=True)
    lifted = jnp.exp(scores - top)
    total = jnp.sum(lifted, axis=-1, keepdims=True)
    probs = (lifted / total).astype(BF16)
    mixed = join_heads(dot(probs, v, ((1,), (0,))))
    return probs, mixed.astype(BF16)


def backward_quad(q, k, v, probs, grad, allowed):
    q_stack = stack_heads(q)
    g_stack = stack_heads(grad)
    grad_v = dot(probs, g_stack, ((0,), (0,)))
    grad_p = dot(g_stack, v, ((1,), (1,)))
    p = probs.astype(F32)
    inner = jnp.sum(grad_p * p, axis=-1, keepdims=True)
    grad_s = p * (grad_p - inner)
    if allowed is not None:
        grad_s = jnp.where(allowed, grad_s, 0.0)
    grad_s = grad_s.astype(BF16)
    grad_q = join_heads(dot(grad_s, k, ((1,), (0,)))) * SCALE
    grad_k = dot(grad_s, q_stack, ((0,), (0,))) * SCALE
    return grad_q.astype(BF16), grad_k.astype(BF16), grad_v.astype(BF16)


def self_forward_kernel(lengths, qkv_ref, o_ref, p_ref):
    rows, width = o_ref.shape[1], o_ref.shape[2]
    allowed = causal_mask(rows, rows, lengths[pl.program_id(0)])
    for h in range(width // WIDE):
        c = h * WIDE
        probs, mixed = forward_quad(
            qkv_ref[0, :, c : c + WIDE],
            qkv_ref[0, :, width + c : width + c + WIDE],
            qkv_ref[0, :, 2 * width + c : 2 * width + c + WIDE],
            allowed,
        )
        o_ref[0, :, c : c + WIDE] = mixed
        p_ref[0, h] = probs


def self_forward(qkv, lengths):
    items, rows, width3 = qkv.shape
    width = width3 // 3
    quads = width // WIDE
    return pl.pallas_call(
        self_forward_kernel,
        grid_spec=pltpu.PrefetchScalarGridSpec(
            num_scalar_prefetch=1,
            grid=(items,),
            in_specs=[pl.BlockSpec((1, rows, width3), lambda i, s: (i, 0, 0))],
            out_specs=[
                pl.BlockSpec((1, rows, width), lambda i, s: (i, 0, 0)),
                pl.BlockSpec((1, quads, QUAD * rows, rows), lambda i, s: (i, 0, 0, 0)),
            ],
        ),
        out_shape=[
            jax.ShapeDtypeStruct((items, rows, width), BF16),
            jax.ShapeDtypeStruct((items, quads, QUAD * rows, rows), BF16),
        ],
        compiler_params=params(),
        cost_estimate=cost(0.1),
    )(lengths, qkv)


def self_backward_kernel(qkv_ref, p_ref, g_ref, *refs):
    d_ref = refs[-1]
    width = g_ref.shape[2]
    for h in range(width // WIDE):
        c = h * WIDE
        grad_q, grad_k, grad_v = backward_quad(
            qkv_ref[0, :, c : c + WIDE],
            qkv_ref[0, :, width + c : width + c + WIDE],
            qkv_ref[0, :, 2 * width + c : 2 * width + c + WIDE],
            p_ref[0, h],
            g_ref[0, :, c : c + WIDE],
            None,
        )
        d_ref[0, :, c : c + WIDE] = grad_q
        d_ref[0, :, width + c : width + c + WIDE] = grad_k
        d_ref[0, :, 2 * width + c : 2 * width + c + WIDE] = grad_v


def self_backward(order, qkv, probs, grad):
    items, rows, width3 = qkv.shape
    width = width3 // 3
    quads = width // WIDE
    waits = order.take()
    out = pl.pallas_call(
        self_backward_kernel,
        grid=(items,),
        in_specs=[
            pl.BlockSpec((1, rows, width3), lambda i: (i, 0, 0)),
            pl.BlockSpec((1, quads, QUAD * rows, rows), lambda i: (i, 0, 0, 0)),
            pl.BlockSpec((1, rows, width), lambda i: (i, 0, 0)),
        ]
        + [pl.BlockSpec(memory_space=pl.ANY)] * len(waits),
        out_specs=pl.BlockSpec((1, rows, width3), lambda i: (i, 0, 0)),
        out_shape=jax.ShapeDtypeStruct((items, rows, width3), BF16),
        compiler_params=params(),
        cost_estimate=cost(order.long()),
    )(qkv, probs, grad, *waits)
    return order.after(out)


def cross_forward_kernel(q_ref, kv_ref, m_ref, o_ref, p_ref):
    rows, width = o_ref.shape[1], o_ref.shape[2]
    allowed = m_ref[0] > 0
    for h in range(width // WIDE):
        c = h * WIDE
        probs, mixed = forward_quad(
            q_ref[0, :, c : c + WIDE],
            kv_ref[0, :, c : c + WIDE],
            kv_ref[0, :, width + c : width + c + WIDE],
            allowed,
        )
        o_ref[0, :, c : c + WIDE] = mixed
        p_ref[0, h] = probs


def cross_forward(q, kv, mask):
    items, rows, width = q.shape
    keys = kv.shape[1]
    quads = width // WIDE
    return pl.pallas_call(
        cross_forward_kernel,
        grid=(items,),
        in_specs=[
            pl.BlockSpec((1, rows, width), lambda i: (i, 0, 0)),
            pl.BlockSpec((1, keys, 2 * width), lambda i: (i, 0, 0)),
            pl.BlockSpec((1, 1, keys), lambda i: (i, 0, 0)),
        ],
        out_specs=[
            pl.BlockSpec((1, rows, width), lambda i: (i, 0, 0)),
            pl.BlockSpec((1, quads, QUAD * rows, keys), lambda i: (i, 0, 0, 0)),
        ],
        out_shape=[
            jax.ShapeDtypeStruct((items, rows, width), BF16),
            jax.ShapeDtypeStruct((items, quads, QUAD * rows, keys), BF16),
        ],
        compiler_params=params(),
        cost_estimate=cost(0.1),
    )(q, kv, mask)


def cross_backward_kernel(q_ref, kv_ref, p_ref, g_ref, m_ref, *refs):
    dq_ref, dkv_ref = refs[-2:]
    width = g_ref.shape[2]
    allowed = m_ref[0] > 0
    for h in range(width // WIDE):
        c = h * WIDE
        grad_q, grad_k, grad_v = backward_quad(
            q_ref[0, :, c : c + WIDE],
            kv_ref[0, :, c : c + WIDE],
            kv_ref[0, :, width + c : width + c + WIDE],
            p_ref[0, h],
            g_ref[0, :, c : c + WIDE],
            allowed,
        )
        dq_ref[0, :, c : c + WIDE] = grad_q
        dkv_ref[0, :, c : c + WIDE] = grad_k
        dkv_ref[0, :, width + c : width + c + WIDE] = grad_v


def cross_backward(order, q, kv, probs, grad, mask):
    items, rows, width = q.shape
    keys = kv.shape[1]
    quads = width // WIDE
    waits = order.take()
    out = pl.pallas_call(
        cross_backward_kernel,
        grid=(items,),
        in_specs=[
            pl.BlockSpec((1, rows, width), lambda i: (i, 0, 0)),
            pl.BlockSpec((1, keys, 2 * width), lambda i: (i, 0, 0)),
            pl.BlockSpec((1, quads, QUAD * rows, keys), lambda i: (i, 0, 0, 0)),
            pl.BlockSpec((1, rows, width), lambda i: (i, 0, 0)),
            pl.BlockSpec((1, 1, keys), lambda i: (i, 0, 0)),
        ]
        + [pl.BlockSpec(memory_space=pl.ANY)] * len(waits),
        out_specs=[
            pl.BlockSpec((1, rows, width), lambda i: (i, 0, 0)),
            pl.BlockSpec((1, keys, 2 * width), lambda i: (i, 0, 0)),
        ],
        out_shape=[
            jax.ShapeDtypeStruct((items, rows, width), BF16),
            jax.ShapeDtypeStruct((items, keys, 2 * width), BF16),
        ],
        compiler_params=params(),
        cost_estimate=cost(order.long()),
    )(q, kv, probs, grad, mask, *waits)
    order.after(out[0])
    return out


def factor_of(value):
    return lax.rsqrt(jnp.mean(value * value, axis=-1, keepdims=True) + EPSILON)


def matmul(left, right):
    return jnp.dot(left, right, preferred_element_type=F32)


AXES = {1: "core", 2: "x", 4: "y"}


def swap(value, bit):
    return lax.ppermute(value, AXES[bit], [(0, 1), (1, 0)])


class Order:
    def __init__(self):
        self.waits, self.micros = [], 0.1

    def long(self):
        micros, self.micros = self.micros, 0.1
        return micros

    def take(self):
        waits, self.waits = self.waits, []
        return waits

    def after(self, array):
        self.waits.append(array)
        return array


def hold_kernel(*refs):
    pass


def hold(order, array):
    whole = pl.BlockSpec(memory_space=pl.ANY)
    waits = order.take()
    out = pl.pallas_call(
        hold_kernel,
        in_specs=[whole] * (1 + len(waits)),
        out_specs=whole,
        out_shape=jax.ShapeDtypeStruct(array.shape, array.dtype),
        input_output_aliases={0: 0},
        compiler_params=pltpu.CompilerParams(vmem_limit_bytes=1024 * 1024),
        cost_estimate=cost(order.long()),
    )(array, *waits)
    return order.after(out)


def cost(micros):
    return pl.CostEstimate(
        flops=int(micros * 1.15e9), bytes_accessed=int(micros * 3.6e6), transcendentals=0
    )


def put_split(value, flag, axis, give_ref, keep_ref):
    half = value.shape[axis] // 2
    low, high = (value[:half], value[half:]) if axis == 0 else (value[:, :half], value[:, half:])

    @pl.when(flag == 0)
    def _():
        keep_ref[...] = low
        give_ref[...] = high

    @pl.when(flag > 0)
    def _():
        keep_ref[...] = high
        give_ref[...] = low


def product_kernel(jobs, has_add, axis, halves, flags, *refs):
    outs = refs[-halves * 2 :] if has_add else refs[-1:]
    add_ref = refs[sum(count + 1 for count, _, _ in jobs)]
    at = 0
    total = sum(steps for _, _, steps in jobs)
    for count, start, steps in jobs:
        lefts, right = refs[at : at + count], refs[at + count]
        at += count + 1

        def work(lefts=lefts, right=right, start=start):
            left = jnp.concatenate([r[...] for r in lefts], axis=1)
            value = right[0] if len(right.shape) == 3 else right[...]
            out = dot(left, value, ((0,), (0,)))
            if not has_add:
                outs[0][...] = out.astype(BF16)
                return
            out = (out + add_ref[...].astype(F32)).astype(BF16)
            if axis == 1:
                put_split(out, flags[1], 1, *outs)
                return
            which = 2 * start // total if halves > 1 else 0
            give, keep = outs[2 * which : 2 * which + 2]
            for z in range(give.shape[0]):
                part = out[128 * z : 128 * z + 128]
                put_split(part, flags[1 + which], 0, give.at[z], keep.at[z])

        if len(jobs) == 1:
            work()
        else:
            step = pl.program_id(0)
            pl.when((step >= start) & (step < start + steps))(work)


def call_product(order, axis, grid, jobs, flags, specs, operands, out_specs, out_shapes):
    waits = order.take()
    has_add = len(out_shapes) > 1
    out = pl.pallas_call(
        functools.partial(product_kernel, jobs, has_add, axis, len(out_shapes) // 2),
        grid_spec=pltpu.PrefetchScalarGridSpec(
            num_scalar_prefetch=1,
            grid=grid,
            in_specs=specs + [pl.BlockSpec(memory_space=pl.ANY)] * len(waits),
            out_specs=out_specs,
        ),
        out_shape=out_shapes,
        compiler_params=params(),
        cost_estimate=cost(order.long()),
    )(flags, *operands, *waits)
    order.after(out[0])
    return out


def grad_rows(order, pairs, flags, add=None):
    count = pairs[0][0].shape[1] // 256
    total = sum(columns for _, _, _, columns in pairs)
    tile = next(t for t in (1408, 1024) if all(c % t == 0 for _, _, _, c in pairs))
    specs, operands, jobs, start = [], [], [], 0
    for left, right, place, columns in pairs:
        rows, steps = left.shape[0], columns // tile
        specs += [
            pl.BlockSpec((rows, 128), lambda j, f, z=z: (0, 2 * z + f[0])) for z in range(count)
        ]
        block = lambda j, f, start=start, steps=steps: jnp.clip(j - start, 0, steps - 1)
        if right.ndim == 3:
            specs.append(
                pl.BlockSpec((1, rows, tile), lambda j, f, b=block, p=place: (p, 0, b(j, f)))
            )
        else:
            specs.append(
                pl.BlockSpec((rows, tile), lambda j, f, b=block, p=place: (0, p + b(j, f)))
            )
        operands += [left] * count + [right]
        jobs.append((count, start, steps))
        start += steps
    block = pl.BlockSpec((count * 128, tile), lambda j, f: (0, j))
    if add is None:
        shapes, outs = [jax.ShapeDtypeStruct((count * 128, total), BF16)], [block]
    else:
        specs.append(block)
        operands.append(add)
        halves = flags.shape[0] - 1
        shapes = [jax.ShapeDtypeStruct((count, 64, total // halves), BF16)] * (2 * halves)
        outs, most = [], start // halves
        for i in range(halves):
            place = lambda j, f, i=i: (0, 0, jnp.clip(j - i * most, 0, most - 1))
            outs += [pl.BlockSpec((count, 64, tile), place)] * 2
    return call_product(order, 0, (start,), jobs, flags, specs, operands, outs, shapes)


def grad_columns(order, left, right, flags, add=None):
    rows, width = left.shape
    half = right.shape[1] // 2
    tile = next(t for t in (1408, 1024) if width % t == 0)
    block = lambda columns: pl.BlockSpec((tile, columns), lambda j, f: (j, 0))
    specs = [
        pl.BlockSpec((rows, tile), lambda j, f: (0, j)),
        pl.BlockSpec((rows, half), lambda j, f: (0, f[0])),
    ]
    operands = [left, right]
    if add is None:
        shapes, outs = [jax.ShapeDtypeStruct((width, half), BF16)], [block(half)]
    else:
        specs.append(block(half))
        operands.append(add)
        shapes = [jax.ShapeDtypeStruct((width, half // 2), BF16)] * 2
        outs = [block(half // 2)] * 2
    steps = width // tile
    return call_product(
        order, 1, (steps,), [(1, 0, steps)], flags, specs, operands, outs, shapes
    )


def land_kernel(count, axis, flags, *refs):
    outs = refs[len(refs) - (2 * count if axis is not None else 1) :]
    column = 0
    for i in range(count):
        total = refs[2 * i][...] + refs[2 * i + 1][...]
        if axis is None:
            columns = total.shape[-1]
            outs[0][..., column : column + columns] = total
            column += columns
        elif axis == 1:
            put_split(total, flags[i], 1, *outs[2 * i : 2 * i + 2])
        else:
            for z in range(total.shape[0]):
                put_split(
                    total[z], flags[i], 0, outs[2 * i].at[z], outs[2 * i + 1].at[z]
                )


def land_sums(order, pairs, flags, axis):
    waits = order.take()
    steps = 2
    block = lambda shape: pl.BlockSpec(
        (shape[0] // steps, *shape[1:]), lambda j, f: (j,) + (0,) * (len(shape) - 1)
    )
    specs, operands, shapes = [], [], []
    for keep, got in pairs:
        specs += [block(keep.shape)] * 2
        operands += [keep, got]
        shape = list(keep.shape)
        if axis is not None:
            shape[-2 if axis == 0 else -1] //= 2
            shapes += [tuple(shape)] * 2
    if axis is None:
        total = sum(keep.shape[-1] for keep, _ in pairs)
        shapes = [(*pairs[0][0].shape[:-1], total)]
    out = pl.pallas_call(
        functools.partial(land_kernel, len(pairs), axis),
        grid_spec=pltpu.PrefetchScalarGridSpec(
            num_scalar_prefetch=1,
            grid=(steps,),
            in_specs=specs + [pl.BlockSpec(memory_space=pl.ANY)] * len(waits),
            out_specs=[block(shape) for shape in shapes],
        ),
        out_shape=[jax.ShapeDtypeStruct(shape, BF16) for shape in shapes],
        compiler_params=params(),
        cost_estimate=cost(order.long()),
    )(jnp.stack(flags), *operands, *waits)
    order.after(out[0])
    return out


def join_kernel(axis, parts, turned, flag, own_ref, got_ref, *refs):
    outs = refs[len(refs) - len(parts) :]
    half = own_ref.shape[axis]

    def put(low, high):
        column = 0
        for out, columns, turn in zip(outs, parts, turned):
            at = slice(column, column + columns)
            column += columns
            for start, ref in ((0, low), (half, high)):
                value = ref[:, at].astype(out.dtype)
                if axis == 1:
                    out[:, start : start + half] = value
                elif turn:
                    n = half // 4
                    for i, j in enumerate((0, 2, 1, 3)):
                        out[start + j * n : start + (j + 1) * n] = value[i * n : (i + 1) * n]
                else:
                    out[start : start + half] = value

    either(flag[0], put, own_ref, got_ref)


def land_join(order, own, got, flag, axis, parts, turned, kind):
    waits = order.take()
    whole = lambda shape: pl.BlockSpec(shape, lambda j, f: (0, 0))
    n, c = own.shape
    shapes = [(2 * n, columns) for columns in parts] if axis == 0 else [(n, 2 * c)]
    out = pl.pallas_call(
        functools.partial(join_kernel, axis, parts, turned),
        grid_spec=pltpu.PrefetchScalarGridSpec(
            num_scalar_prefetch=1,
            grid=(1,),
            in_specs=[whole(own.shape)] * 2 + [pl.BlockSpec(memory_space=pl.ANY)] * len(waits),
            out_specs=[whole(shape) for shape in shapes],
        ),
        out_shape=[jax.ShapeDtypeStruct(shape, kind) for shape in shapes],
        compiler_params=params(),
        cost_estimate=cost(order.long()),
    )(flag.reshape(1), own, got, *waits)
    order.after(out[0])
    return out


def segment_kernel(steps, has_next, split, waits, flag, *refs):
    x_ref, w_ref, v_ref, b_ref, g_ref = refs[:5]
    n_ref = refs[5] if has_next else None
    u_ref = refs[5 + has_next] if split else None
    refs = refs[5 + has_next + split + waits :]
    if has_next:
        d_ref, gg_ref, e_ref, o_ref, acc = refs
    else:
        d_ref, gg_ref, acc = refs
    step = pl.program_id(0)
    x = x_ref[0] if len(x_ref.shape) == 3 else x_ref[...]
    size = w_ref.shape[0]
    for at, ref in ((0, w_ref), (size, u_ref)):
        if ref is None:
            continue
        partial = dot(x, ref[...], ((1,), (1,)))

        @pl.when(step == 0)
        def _(at=at, partial=partial):
            acc[:, at : at + size] = partial

        @pl.when(step > 0)
        def _(at=at, partial=partial):
            acc[:, at : at + size] += partial

    @pl.when(step == steps - 1)
    def _():
        gain = g_ref[...]
        rows, chunk = acc.shape[0], 144
        gg_ref[...] = jnp.zeros_like(gg_ref)

        @pl.loop(0, rows // chunk)
        def _(i):
            at = pl.ds(pl.multiple_of(i * chunk, chunk), chunk)
            grad = acc[at, :]
            if split:
                own, other = grad[:, :size], grad[:, size:]
                low, high = jnp.where(flag[0] == 0, own, other), jnp.where(flag[0] == 0, other, own)
                blocks = []
                for k in range(0, size, 128):
                    blocks += [low[:, k : k + 128], high[:, k : k + 128]]
                grad = jnp.concatenate(blocks, axis=1)
            value = v_ref[at, :].astype(F32)
            factor = lax.rsqrt(jnp.mean(value * value, axis=-1, keepdims=True) + EPSILON)
            scaled = gain * grad
            along = jnp.mean(scaled * value, axis=-1, keepdims=True)
            back = factor * scaled - value * (factor * factor * factor * along)
            gg_ref[...] += jnp.sum(grad * value * factor, axis=0, keepdims=True)
            total = b_ref[at, :].astype(F32) + back
            d_ref[at, :] = total
            if has_next:
                e_ref[at, :] = total.astype(BF16)

        if has_next:
            o_ref[...] = dot(e_ref[...], n_ref[...], ((1,), (1,))).astype(BF16)


def segment(order, core, x, w, column, tile, value, base, gain, after=None):
    rows, width = value.shape
    steps = x.shape[-1] * (x.shape[0] if x.ndim == 3 else 1) // tile
    if x.ndim == 3:
        per = x.shape[-1] // tile
        x_spec = pl.BlockSpec((1, rows, tile), lambda k, f: (k // per, 0, k % per))
    else:
        x_spec = pl.BlockSpec((rows, tile), lambda k, f: (0, k))
    whole = pl.BlockSpec((rows, width), lambda k, f: (0, 0))
    line = pl.BlockSpec((1, width), lambda k, f: (0, 0))
    split = isinstance(w, tuple)
    w = w if split else (w,)
    w_spec = pl.BlockSpec((w[0].shape[0], tile), lambda k, f: (0, k + column))
    specs = [x_spec, w_spec, whole, whole, line]
    operands = [x, w[0], value, base, gain.reshape(1, width)]
    shapes = [
        jax.ShapeDtypeStruct((rows, width), F32),
        jax.ShapeDtypeStruct((1, width), F32),
    ]
    outs = [whole, line]
    if after is not None:
        matrix, at = after
        specs.append(pl.BlockSpec((width, width), lambda k, f: (0, at)))
        operands.append(matrix)
        shapes += [jax.ShapeDtypeStruct((rows, width), BF16)] * 2
        outs += [whole, whole]
    if split:
        specs.append(w_spec)
        operands.append(w[1])
    waits = order.take()
    out = pl.pallas_call(
        functools.partial(segment_kernel, steps, after is not None, split, len(waits)),
        grid_spec=pltpu.PrefetchScalarGridSpec(
            num_scalar_prefetch=1,
            grid=(steps,),
            in_specs=specs + [pl.BlockSpec(memory_space=pl.ANY)] * len(waits),
            out_specs=outs,
            scratch_shapes=[pltpu.VMEM((rows, width), F32)],
        ),
        out_shape=shapes,
        compiler_params=params(),
        cost_estimate=cost(order.long()),
    )(core.reshape(1), *operands, *waits)
    order.after(out[1])
    return out


def halves_of(value):
    starts = range(0, value.shape[1], 256)
    return [
        jnp.concatenate([value[:, k + j : k + j + 128] for k in starts], axis=1)
        for j in (0, 128)
    ]


def mlp_kernel(flag, a_ref, e_ref, wg_ref, wu_ref, vg_ref, vu_ref, wd_ref, i_ref, d_ref, mine):
    @pl.when(pl.program_id(0) == 0)
    def _():
        def put(own, other):
            mine[0] = own
            mine[1] = other

        either(flag[0], put, *halves_of(a_ref[...]))

    grad = dot(e_ref[...], wd_ref[...], ((1,), (1,)))
    product = lambda w, v: dot(mine[0], w[...], ((1,), (0,))) + dot(mine[1], v[...], ((1,), (0,)))
    gate, up = product(wg_ref, vg_ref), product(wu_ref, vu_ref)
    slope, cubic = 0.7978845608028654, 0.044715
    square = gate * gate
    bend = jnp.tanh(slope * gate * (1.0 + cubic * square))
    half = 0.5 * (1.0 + bend)
    act = gate * half
    turn = half + 0.5 * gate * (1.0 - bend * bend) * slope * (1.0 + 3.0 * cubic * square)
    i_ref[...] = (act * up).astype(BF16)
    d_ref[0] = (grad * up * turn).astype(BF16)
    d_ref[1] = (grad * act).astype(BF16)


def mlp(order, core, a3, e3, own, other, w_down):
    rows, width = a3.shape
    hidden = w_down.shape[0]
    tile = MLP_TILE
    count = hidden // tile
    whole = pl.BlockSpec((rows, width), lambda j, f: (0, 0))
    gate = pl.BlockSpec((width // 2, tile), lambda j, f: (0, j))
    up = pl.BlockSpec((width // 2, tile), lambda j, f: (0, count + j))
    return pl.pallas_call(
        mlp_kernel,
        grid_spec=pltpu.PrefetchScalarGridSpec(
            num_scalar_prefetch=1,
            grid=(count,),
            in_specs=[
                whole,
                whole,
                gate,
                up,
                gate,
                up,
                pl.BlockSpec((tile, width), lambda j, f: (j, 0)),
            ],
            out_specs=[
                pl.BlockSpec((rows, tile), lambda j, f: (0, j)),
                pl.BlockSpec((2, rows, tile), lambda j, f: (0, 0, j)),
            ],
            scratch_shapes=[pltpu.VMEM((2, rows, width // 2), BF16)],
        ),
        out_shape=[
            jax.ShapeDtypeStruct((rows, hidden), BF16),
            jax.ShapeDtypeStruct((2, rows, hidden), BF16),
        ],
        compiler_params=params(),
        cost_estimate=cost(order.long()),
    )(core.reshape(1), a3, e3, own, own, other, other, w_down)


def forward_out_kernel(steps, waits, x_ref, w_ref, b_ref, *refs):
    o_ref, acc = refs[waits:]
    step = pl.program_id(0)
    partial = dot(x_ref[...], w_ref[...], ((1,), (0,)))

    @pl.when(step == 0)
    def _():
        acc[...] = partial + b_ref[...]

    @pl.when(step > 0)
    def _():
        acc[...] += partial

    @pl.when(step == steps - 1)
    def _():
        o_ref[...] = acc[...].astype(BF16)


def forward_out(order, x, w, base):
    rows, width = base.shape
    tile = next(t for t in (1408, 1024) if w.shape[0] % t == 0)
    steps = w.shape[0] // tile
    whole = pl.BlockSpec((rows, width), lambda k: (0, 0))
    waits = order.take()
    out = pl.pallas_call(
        functools.partial(forward_out_kernel, steps, len(waits)),
        grid=(steps,),
        in_specs=[
            pl.BlockSpec((rows, tile), lambda k: (0, k)),
            pl.BlockSpec((tile, width), lambda k: (k, 0)),
            whole,
        ]
        + [pl.BlockSpec(memory_space=pl.ANY)] * len(waits),
        out_specs=whole,
        out_shape=jax.ShapeDtypeStruct((rows, width), BF16),
        scratch_shapes=[pltpu.VMEM((rows, width), F32)],
        compiler_params=params(),
        cost_estimate=cost(order.long()),
    )(x, w, base, *waits)
    return order.after(out)


def back_product_kernel(waits, x_ref, w_ref, *refs):
    refs[-1][...] = dot(x_ref[...], w_ref[...], ((1,), (1,)))


def back_product(order, x, w):
    rows, depth = x.shape
    width = w.shape[0]
    tile = 256
    waits = order.take()
    out = pl.pallas_call(
        functools.partial(back_product_kernel, len(waits)),
        grid=(width // tile,),
        in_specs=[
            pl.BlockSpec((rows, depth), lambda j: (0, 0)),
            pl.BlockSpec((tile, depth), lambda j: (j, 0)),
        ]
        + [pl.BlockSpec(memory_space=pl.ANY)] * len(waits),
        out_specs=pl.BlockSpec((rows, tile), lambda j: (0, j)),
        out_shape=jax.ShapeDtypeStruct((rows, width), F32),
        compiler_params=params(),
        cost_estimate=cost(order.long()),
    )(x, w, *waits)
    return order.after(out)


def bit_of(spot, bit):
    return (spot // bit) % 2


class Sum:
    def __init__(self, order, spot, axis, product, first, second):
        self.order, self.axis, self.product = order, axis, product
        self.first, self.second = first, second
        self.bits = bit_of(spot, 1), bit_of(spot, first), bit_of(spot, second)
        core, one, _ = self.bits
        (give,) = product(jnp.stack([1 - core, one]))
        self.flight = swap(give, 1)

    def core(self):
        core, one, _ = self.bits
        give, self.keep = self.product(jnp.stack([core, one]), self.flight)
        self.flight = swap(give, self.first)


class Part:
    def __init__(self, spot, first, second):
        self.first, self.second, self.axis = first, second, 0
        self.bits = bit_of(spot, 1), bit_of(spot, first), bit_of(spot, second)


class Pair:
    def __init__(self, order, spot, pairs):
        self.product = functools.partial(grad_rows, order, pairs)
        self.parts = [Part(spot, 2, 4), Part(spot, 4, 2)]
        self.flags = [bit_of(spot, b) for b in (1, 2, 4)]
        core, one, two = self.flags
        (give,) = self.product(jnp.stack([1 - core, one, two]))
        self.flight = swap(give, 1)

    def core(self):
        core, one, two = self.flags
        out = self.product(jnp.stack([core, one, two]), self.flight)
        for i, part in enumerate(self.parts):
            part.keep = out[2 * i + 1]
            part.flight = swap(out[2 * i], part.first)
        return self.parts


def region(axis, first, cross):
    return (first, cross) if axis == 0 else (cross, first)


def either(flag, put, one, two):
    pl.when(flag == 0)(lambda: put(one, two))
    pl.when(flag > 0)(lambda: put(two, one))


def cut_kernel(axis, z_ref, *refs):
    a_ref, b_ref = refs[-2:]
    half = z_ref.shape[2 - axis] // 2
    a_ref[0] = z_ref.at[0][region(axis, slice(None), slice(0, half))]
    b_ref[0] = z_ref.at[0][region(axis, slice(None), slice(half, None))]


def cut(order, value, axis, column, columns):
    waits = order.take()
    z, n, _ = value.shape
    shape = (z, n, columns // 2) if axis == 0 else (z, n // 2, columns)
    out = pl.pallas_call(
        functools.partial(cut_kernel, axis),
        grid=(z,),
        in_specs=[pl.BlockSpec((1, n, columns), lambda j: (j, 0, column))]
        + [pl.BlockSpec(memory_space=pl.ANY)] * len(waits),
        out_specs=[pl.BlockSpec((1, *shape[1:]), lambda j: (j, 0, 0))] * 2,
        out_shape=[jax.ShapeDtypeStruct(shape, BF16)] * 2,
        compiler_params=params(),
        cost_estimate=cost(order.long()),
    )(value, *waits)
    order.after(out[0])
    return out


def pack_kernel(tall, place, *refs):
    refs = list(refs)
    if tall:
        last_in, last_out = refs.pop(len(refs) - 3), refs.pop()
        last_out[...] = last_in[...]
    column = 0
    for ref in refs[:-1]:
        refs[-1][:, column : column + ref.shape[1]] = ref[...]
        column += ref.shape[1]


def pack(spot, shards, last=None, tall=None):
    n = shards[0].shape[0] // 8
    seat = 4 * bit_of(spot, 1) + 2 * bit_of(spot, 4) + bit_of(spot, 2)
    specs = [pl.BlockSpec((n, w.shape[1]), lambda j, f: (f[0], 0)) for w in shards]
    total = sum(w.shape[1] for w in shards)
    operands = list(shards)
    if last is not None:
        specs.append(pl.BlockSpec(last.shape, lambda j, f: (0, 0)))
        operands.append(last)
        total += last.shape[1]
    outs, shapes = [pl.BlockSpec((n, total), lambda j, f: (0, 0))], [(n, total)]
    if tall is not None:
        piece = (tall.shape[0], tall.shape[1] // 8)
        specs.append(pl.BlockSpec(piece, lambda j, f: (0, f[0])))
        operands.append(tall)
        outs.append(pl.BlockSpec(piece, lambda j, f: (0, 0)))
        shapes.append(piece)
    return pl.pallas_call(
        functools.partial(pack_kernel, tall is not None),
        grid_spec=pltpu.PrefetchScalarGridSpec(
            num_scalar_prefetch=1, grid=(1,), in_specs=specs, out_specs=outs
        ),
        out_shape=[jax.ShapeDtypeStruct(shape, BF16) for shape in shapes],
        compiler_params=params(),
        cost_estimate=cost(1),
    )(seat.reshape(1), *operands)


def pairs_kernel(axis, flags, *refs):
    ins, outs = refs[:4], refs[-2:]
    for i in range(2):
        size = ins[2 * i].shape[1 + axis]

        def put(low, high, out=outs[i], size=size):
            out.at[0][region(axis, slice(0, size), slice(None))] = low[0]
            out.at[0][region(axis, slice(size, None), slice(None))] = high[0]

        either(flags[i], put, ins[2 * i], ins[2 * i + 1])


def quads_kernel(axis, flags, *refs):
    a_own, a_got, b_own, b_got = refs[:4]
    out = refs[-1].at[0]
    two, half = a_own.shape[1 + axis], a_own.shape[2 - axis]
    n = two // 2

    def put_a(low, high):
        out[region(axis, slice(0, two), slice(0, half))] = low[0]
        out[region(axis, slice(two, None), slice(0, half))] = high[0]

    def put_b(low, high):
        for y in range(2):
            for x, ref in enumerate((low, high)):
                at = (2 * y + x) * n
                out[region(axis, slice(at, at + n), slice(half, None))] = ref.at[0][
                    region(axis, slice(y * n, y * n + n), slice(None))
                ]

    either(flags[1], put_a, a_own, a_got)
    either(flags[0], put_b, b_own, b_got)


def cores_kernel(axis, flags, own_ref, got_ref, *refs):
    out = refs[-1].at[0]
    size = own_ref.shape[1 + axis]

    def put(low, high):
        out[region(axis, slice(0, size), slice(None))] = low[0]
        out[region(axis, slice(size, None), slice(None))] = high[0]

    either(flags[2], put, own_ref, got_ref)


def by_shard(order, kernel, axis, flags, operands, shapes):
    waits = order.take()
    block = lambda shape: pl.BlockSpec((1, *shape[1:]), lambda j, *f: (j, 0, 0))
    out = pl.pallas_call(
        functools.partial(kernel, axis),
        grid_spec=pltpu.PrefetchScalarGridSpec(
            num_scalar_prefetch=len(flags),
            grid=(operands[0].shape[0],),
            in_specs=[block(v.shape) for v in operands]
            + [pl.BlockSpec(memory_space=pl.ANY)] * len(waits),
            out_specs=[block(shape) for shape in shapes],
        ),
        out_shape=[jax.ShapeDtypeStruct(shape, BF16) for shape in shapes],
        compiler_params=params(),
        cost_estimate=cost(order.long()),
    )(*flags, *operands, *waits)
    order.after(out[0])
    return out


class Gather:
    def __init__(self, order, spot, value, axis, column=0, columns=None):
        self.order, self.axis = order, axis
        self.flags = [jnp.stack([bit_of(spot, b) for b in (2, 4, 1)])]
        self.value, self.place = value, (column, columns or value.shape[2])

    def scaled(self, shape, along, across):
        shape = list(shape)
        shape[1 + self.axis] = shape[1 + self.axis] * along
        shape[2 - self.axis] = shape[2 - self.axis] * across // 2
        return tuple(shape)

    def run(self, kernel, flags, operands, shapes):
        return by_shard(self.order, kernel, self.axis, flags, operands, shapes)

    def one(self):
        self.a, self.b = cut(self.order, self.value, self.axis, *self.place)
        self.got = swap(self.a, 2), swap(self.b, 4)

    def two(self):
        shape = self.scaled(self.a.shape, 2, 2)
        self.a, self.b = self.run(
            pairs_kernel, self.flags, [self.a, self.got[0], self.b, self.got[1]], [shape] * 2
        )
        self.got = swap(self.a, 4), swap(self.b, 2)

    def three(self):
        shape = self.scaled(self.a.shape, 2, 4)
        (self.half,) = self.run(
            quads_kernel, self.flags, [self.a, self.got[0], self.b, self.got[1]], [shape]
        )
        self.got = swap(self.half, 1)

    def four(self):
        shape = self.scaled(self.half.shape, 2, 2)
        (whole,) = self.run(cores_kernel, self.flags, [self.half, self.got], [shape])
        return whole.reshape(-1, whole.shape[-1])


def land_first(order, *sums):
    out = land_sums(
        order, [(s.keep, s.flight) for s in sums], [s.bits[2] for s in sums], sums[0].axis
    )
    for i, s in enumerate(sums):
        s.keep = out[2 * i + 1]
        s.flight = swap(out[2 * i], s.second)


def land_second(order, *sums):
    (out,) = land_sums(
        order, [(s.keep, s.flight) for s in sums], [s.bits[2] for s in sums], None
    )
    return out.reshape(-1, out.shape[-1])


def over_shards(value):
    value = lax.psum_scatter(value, "fsdp", scatter_dimension=0, tiled=True)
    return across_groups(value)


def across_groups(value):
    size = lax.axis_size("group")
    ring = [(i, (i + 1) % size) for i in range(size)]
    total = step = value
    for _ in range(size - 1):
        step = lax.ppermute(step, "group", ring)
        total = total + step
    return total


class Spread:
    def __init__(self, order, spot, value, parts, turned, axis=0):
        self.order, self.spot, self.axis = order, spot, axis
        self.value, self.parts, self.turned = value, parts, turned
        self.bits = [4, 2, 1]
        self.send()

    def send(self):
        self.flight = swap(self.value, self.bits[0])

    def land(self):
        bit = self.bits.pop(0)
        last = not self.bits
        out = land_join(
            self.order,
            self.value,
            self.flight,
            bit_of(self.spot, bit),
            self.axis,
            self.parts if last else [self.value.shape[1]],
            self.turned if last else [False],
            F32 if last else BF16,
        )
        if last:
            self.values = out
        else:
            self.value = out[0]
            self.send()


def on_device(
    text,
    memory,
    text_lengths,
    memory_mask,
    grad_out,
    self_gain,
    self_query,
    self_key,
    self_value,
    self_output,
    cross_gain,
    cross_query,
    cross_key,
    cross_value,
    cross_output,
    mlp_gain,
    mlp_gate,
    mlp_up,
    mlp_down,
):
    items, rows, width = text.shape
    keys = memory.shape[1]
    spot = 4 * lax.axis_index("y") + 2 * lax.axis_index("x") + lax.axis_index("core")

    order = Order()
    gather = lambda value: lax.all_gather(value, "fsdp", axis=0)
    own = self_gain.shape[0]
    lines = jnp.stack([self_gain, cross_gain, mlp_gain]).reshape(-1, 128)
    squares = [
        self_query,
        self_key,
        self_value,
        self_output,
        cross_key,
        cross_value,
        cross_query,
        cross_output,
    ]
    lines = jnp.pad(lines, ((0, width // 32 - lines.shape[0]), (0, 0)))
    piece, piece_down = pack(spot, squares, lines, mlp_down)
    both = gather(piece)
    g_down = Gather(order, spot, gather(piece_down), 1)
    g_self = Gather(order, spot, both, 0, 0, 4 * width)
    g_cross = Gather(order, spot, both, 0, 1, 4 * width)
    shards = both.shape[0]
    gains = both[:, : 3 * own // 128, 8 * width :].reshape(shards, 3, own)
    gains = gains.transpose(1, 0, 2).reshape(3, width).astype(F32)
    g_wide = Gather(order, spot, gather(*pack(spot, [mlp_gate, mlp_up])), 0)
    hidden = mlp_gate.shape[1]

    x = text.reshape(-1, width).astype(F32)
    flat_memory = memory.reshape(-1, width)
    e3 = grad_out.reshape(-1, width)
    mask = memory_mask[:, None, :]

    g_down.one()
    g_down.two()
    g_self.one()
    g_cross.one()
    order.micros = C_LONG
    g_down.three()
    g_self.two()
    g_cross.two()
    order.micros = C_LONG
    w_down = g_down.four()
    g_wide.one()
    g_self.three()
    w_self = g_self.four()
    w_qkv, w_so = w_self[:, : 3 * width], w_self[:, 3 * width :]
    c1 = factor_of(x)
    a1 = (x * c1 * gains[0]).astype(BF16)
    qkv = matmul(a1, w_qkv).astype(BF16).reshape(items, rows, 3 * width)
    o1, p1 = self_forward(qkv, text_lengths)
    o1 = order.after(o1).reshape(-1, width)
    g_wide.two()
    g_cross.three()
    h1 = x + matmul(o1, w_so)
    c2 = factor_of(h1)
    a2 = (h1 * c2 * gains[1]).astype(BF16)
    order.after(a2)
    order.micros = C_LONG
    w_cross = g_cross.four()
    w_kv = w_cross[:, : 2 * width]
    w_cq, w_co = w_cross[:, 2 * width : 3 * width], w_cross[:, 3 * width :]
    kv = matmul(flat_memory, w_kv).astype(BF16).reshape(items, keys, 2 * width)
    q2 = matmul(a2, w_cq).astype(BF16).reshape(items, rows, width)
    o2, p2 = cross_forward(q2, kv, mask)
    o2 = order.after(o2).reshape(-1, width)
    g_wide.three()
    h2 = h1 + matmul(o2, w_co)
    c3 = factor_of(h2)
    a3 = (h2 * c3 * gains[2]).astype(BF16)
    core = bit_of(spot, 1)
    flat = lambda value: value.reshape(-1, 2 * hidden)
    w_wide = flat(g_wide.half), flat(g_wide.got)
    inner, d_wide = mlp(order, core, a3, e3, *w_wide, w_down)
    order.take()

    s_wide = Pair(order, spot, [(a3, d_wide, 0, hidden), (a3, d_wide, 1, hidden)])
    s_down = Sum(order, spot, 1, functools.partial(grad_columns, order, inner, e3), 2, 4)
    wide = s_wide.core()
    s_down.core()
    order.micros = C_LONG
    d_h2, gg3, e2, d_o2 = segment(
        order, core, d_wide, w_wide, 0, hidden // 2, h2, e3, gains[2], (w_cross, 3)
    )
    d_q2, d_kv = cross_backward(order, q2, kv, p2, d_o2.reshape(text.shape), mask)
    d_q2 = d_q2.reshape(-1, width)
    d_kv = d_kv.reshape(-1, 2 * width)
    s_cross = Pair(
        order,
        spot,
        [
            (flat_memory, d_kv, 0, 2 * width),
            (a2, d_q2, 0, width),
            (o2, e2, 0, width),
        ],
    )
    land_first(order, *wide)
    order.micros = C_SEG2
    d_h1, gg2, e1, d_o1 = segment(
        order, core, d_q2, w_cross, 4, width // 2, h1, d_h2, gains[1], (w_self, 3)
    )
    land_first(order, s_down)
    order.micros = C_LONG
    z_wide = land_second(order, *wide)
    d_qkv = self_backward(order, qkv, p1, d_o1.reshape(text.shape)).reshape(-1, 3 * width)
    z_down = land_second(order, s_down)
    s_self = Pair(
        order,
        spot,
        [
            (a1, d_qkv, 0, 2 * width),
            (a1, d_qkv, 2, width),
            (o1, e1, 0, width),
        ],
    )
    cross = s_cross.core()
    z_wide = over_shards(z_wide)
    order.micros = C_LONG
    both = s_self.core()
    order.micros = C_LONG
    grad_text, gg1 = segment(order, core, d_qkv, w_self, 0, width, x, d_h1, gains[0])
    land_first(order, *cross)
    order.micros = C_MID
    z_wide = hold(order, z_wide)
    z_down = over_shards(z_down)
    land_first(order, *both)
    z_down = hold(order, z_down)
    z_cross = over_shards(land_second(order, *cross))
    t_wide = Spread(order, spot, z_wide, [hidden, hidden], [False, True])
    lines = jnp.concatenate([gg1, gg2, gg3]).reshape(3, shards, own).transpose(1, 0, 2)
    lines = lines.reshape(shards, -1, 128)
    lines = jnp.pad(lines, ((0, 0), (0, width // 32 - lines.shape[1]), (0, 0)))
    lines = order.after(lines.astype(BF16).reshape(-1, 128))
    z_self = land_second(order, *both)
    z_self = order.after(jnp.concatenate([z_self, lines], axis=1))
    t_wide.land()
    t_down = Spread(order, spot, z_down, [width], [False], 1)
    z_cross = hold(order, z_cross)
    z_self = over_shards(z_self)
    squares = [width] * 4
    t_cross = Spread(order, spot, z_cross, squares, [False, False, True, True])
    block_out = forward_out(order, inner, w_down, h2)
    t_down.land()
    t_cross.land()
    t_wide.land()
    grad_memory = back_product(order, d_kv, w_cross)
    z_self = hold(order, z_self)
    t_self = Spread(
        order, spot, z_self, [*squares, 128], [False, False, True, True, False]
    )
    t_down.land()
    t_cross.land()
    t_wide.land()
    t_self.land()
    t_down.land()
    t_cross.land()
    t_self.land()
    t_self.land()
    g_gate, g_up = t_wide.values
    (g_down,) = t_down.values
    g_ck, g_cv, g_cq, g_co = t_cross.values
    g_sq, g_sk, g_sv, g_so, lines = t_self.values
    lines = jnp.sum(lines.reshape(8, -1, 128), axis=0)
    gg = lines[: 3 * own // 128].reshape(3, own)

    return (
        block_out.reshape(text.shape),
        grad_text.reshape(text.shape),
        grad_memory.reshape(memory.shape),
        gg[0],
        g_sq,
        g_sk,
        g_sv,
        g_so,
        gg[1],
        g_cq,
        g_ck,
        g_cv,
        g_co,
        gg[2],
        g_gate,
        g_up,
        g_down,
    )


def solution(mesh):
    shape = mesh.devices.shape
    mesh = jax.sharding.Mesh(
        mesh.devices.reshape(shape[0] // 8, 2, 2, 2, shape[1]),
        ("group", "y", "x", "core", "fsdp"),
    )
    every = ("group", "y", "x", "core", "fsdp")
    rows = P(every, None, None)
    gain, weight = P("fsdp"), P("fsdp", None)
    weights = (gain, weight, weight, weight, weight) * 2 + (gain, weight, weight, weight)
    return jax.shard_map(
        on_device,
        mesh=mesh,
        in_specs=(rows, rows, P(every), P(every, None), rows) + weights,
        out_specs=(rows, rows, rows) + weights,
        check_vma=False,
    )
```

```python
import functools

import jax
import jax.numpy as jnp
from jax import lax
from jax.experimental import pallas as pl
from jax.experimental.pallas import tpu as pltpu
from jax.sharding import PartitionSpec as P

HEAD_DIM = 64
QUAD = 4
WIDE = HEAD_DIM * QUAD
EPSILON = 1e-06
MASKED = -1e30
SCALE = 0.125
VMEM_LIMIT = 56 * 1024 * 1024

C_LONG = 100
MLP_TILE = 1408
C_SEG2 = 11
C_MID = 8

BF16 = jnp.bfloat16
F32 = jnp.float32


def params():
    return pltpu.CompilerParams(vmem_limit_bytes=VMEM_LIMIT)


def dot(a, b, dims):
    return lax.dot_general(a, b, (dims, ((), ())), preferred_element_type=F32)


def stack_heads(value):
    lane = lax.broadcasted_iota(jnp.int32, value.shape, 1) // HEAD_DIM
    zero = jnp.zeros_like(value)
    return jnp.concatenate([jnp.where(lane == j, value, zero) for j in range(QUAD)], axis=0)


def join_heads(stacked):
    rows = stacked.shape[0] // QUAD
    lane = lax.broadcasted_iota(jnp.int32, (rows, WIDE), 1) // HEAD_DIM
    out = stacked[:rows]
    for j in range(1, QUAD):
        out = jnp.where(lane == j, stacked[j * rows : (j + 1) * rows], out)
    return out


def causal_mask(rows, keys, length):
    t = lax.broadcasted_iota(jnp.int32, (rows, keys), 0)
    u = lax.broadcasted_iota(jnp.int32, (rows, keys), 1)
    one = (u <= t) & (u < length)
    return jnp.concatenate([one] * QUAD, axis=0)


def forward_quad(q, k, v, allowed):
    stacked = stack_heads(q)
    scores = dot(stacked, k, ((1,), (1,))) * SCALE
    scores = jnp.where(allowed, scores, MASKED)
    top = jnp.max(scores, axis=-1, keepdims=True)
    lifted = jnp.exp(scores - top)
    total = jnp.sum(lifted, axis=-1, keepdims=True)
    probs = (lifted / total).astype(BF16)
    mixed = join_heads(dot(probs, v, ((1,), (0,))))
    return probs, mixed.astype(BF16)


def backward_quad(q, k, v, probs, grad, allowed):
    q_stack = stack_heads(q)
    g_stack = stack_heads(grad)
    grad_v = dot(probs, g_stack, ((0,), (0,)))
    grad_p = dot(g_stack, v, ((1,), (1,)))
    p = probs.astype(F32)
    inner = jnp.sum(grad_p * p, axis=-1, keepdims=True)
    grad_s = p * (grad_p - inner)
    if allowed is not None:
        grad_s = jnp.where(allowed, grad_s, 0.0)
    grad_s = grad_s.astype(BF16)
    grad_q = join_heads(dot(grad_s, k, ((1,), (0,)))) * SCALE
    grad_k = dot(grad_s, q_stack, ((0,), (0,))) * SCALE
    return grad_q.astype(BF16), grad_k.astype(BF16), grad_v.astype(BF16)


def self_forward_kernel(lengths, qkv_ref, o_ref, p_ref):
    rows, width = o_ref.shape[1], o_ref.shape[2]
    allowed = causal_mask(rows, rows, lengths[pl.program_id(0)])
    for h in range(width // WIDE):
        c = h * WIDE
        probs, mixed = forward_quad(
            qkv_ref[0, :, c : c + WIDE],
            qkv_ref[0, :, width + c : width + c + WIDE],
            qkv_ref[0, :, 2 * width + c : 2 * width + c + WIDE],
            allowed,
        )
        o_ref[0, :, c : c + WIDE] = mixed
        p_ref[0, h] = probs


def self_forward(qkv, lengths):
    items, rows, width3 = qkv.shape
    width = width3 // 3
    quads = width // WIDE
    return pl.pallas_call(
        self_forward_kernel,
        grid_spec=pltpu.PrefetchScalarGridSpec(
            num_scalar_prefetch=1,
            grid=(items,),
            in_specs=[pl.BlockSpec((1, rows, width3), lambda i, s: (i, 0, 0))],
            out_specs=[
                pl.BlockSpec((1, rows, width), lambda i, s: (i, 0, 0)),
                pl.BlockSpec((1, quads, QUAD * rows, rows), lambda i, s: (i, 0, 0, 0)),
            ],
        ),
        out_shape=[
            jax.ShapeDtypeStruct((items, rows, width), BF16),
            jax.ShapeDtypeStruct((items, quads, QUAD * rows, rows), BF16),
        ],
        compiler_params=params(),
        cost_estimate=cost(0.1),
    )(lengths, qkv)


def self_backward_kernel(qkv_ref, p_ref, g_ref, *refs):
    d_ref = refs[-1]
    width = g_ref.shape[2]
    for h in range(width // WIDE):
        c = h * WIDE
        grad_q, grad_k, grad_v = backward_quad(
            qkv_ref[0, :, c : c + WIDE],
            qkv_ref[0, :, width + c : width + c + WIDE],
            qkv_ref[0, :, 2 * width + c : 2 * width + c + WIDE],
            p_ref[0, h],
            g_ref[0, :, c : c + WIDE],
            None,
        )
        d_ref[0, :, c : c + WIDE] = grad_q
        d_ref[0, :, width + c : width + c + WIDE] = grad_k
        d_ref[0, :, 2 * width + c : 2 * width + c + WIDE] = grad_v


def self_backward(order, qkv, probs, grad):
    items, rows, width3 = qkv.shape
    width = width3 // 3
    quads = width // WIDE
    waits = order.take()
    out = pl.pallas_call(
        self_backward_kernel,
        grid=(items,),
        in_specs=[
            pl.BlockSpec((1, rows, width3), lambda i: (i, 0, 0)),
            pl.BlockSpec((1, quads, QUAD * rows, rows), lambda i: (i, 0, 0, 0)),
            pl.BlockSpec((1, rows, width), lambda i: (i, 0, 0)),
        ]
        + [pl.BlockSpec(memory_space=pl.ANY)] * len(waits),
        out_specs=pl.BlockSpec((1, rows, width3), lambda i: (i, 0, 0)),
        out_shape=jax.ShapeDtypeStruct((items, rows, width3), BF16),
        compiler_params=params(),
        cost_estimate=cost(order.long()),
    )(qkv, probs, grad, *waits)
    return order.after(out)


def cross_forward_kernel(q_ref, kv_ref, m_ref, o_ref, p_ref):
    rows, width = o_ref.shape[1], o_ref.shape[2]
    allowed = m_ref[0] > 0
    for h in range(width // WIDE):
        c = h * WIDE
        probs, mixed = forward_quad(
            q_ref[0, :, c : c + WIDE],
            kv_ref[0, :, c : c + WIDE],
            kv_ref[0, :, width + c : width + c + WIDE],
            allowed,
        )
        o_ref[0, :, c : c + WIDE] = mixed
        p_ref[0, h] = probs


def cross_forward(q, kv, mask):
    items, rows, width = q.shape
    keys = kv.shape[1]
    quads = width // WIDE
    return pl.pallas_call(
        cross_forward_kernel,
        grid=(items,),
        in_specs=[
            pl.BlockSpec((1, rows, width), lambda i: (i, 0, 0)),
            pl.BlockSpec((1, keys, 2 * width), lambda i: (i, 0, 0)),
            pl.BlockSpec((1, 1, keys), lambda i: (i, 0, 0)),
        ],
        out_specs=[
            pl.BlockSpec((1, rows, width), lambda i: (i, 0, 0)),
            pl.BlockSpec((1, quads, QUAD * rows, keys), lambda i: (i, 0, 0, 0)),
        ],
        out_shape=[
            jax.ShapeDtypeStruct((items, rows, width), BF16),
            jax.ShapeDtypeStruct((items, quads, QUAD * rows, keys), BF16),
        ],
        compiler_params=params(),
        cost_estimate=cost(0.1),
    )(q, kv, mask)


def cross_backward_kernel(q_ref, kv_ref, p_ref, g_ref, m_ref, *refs):
    dq_ref, dkv_ref = refs[-2:]
    width = g_ref.shape[2]
    allowed = m_ref[0] > 0
    for h in range(width // WIDE):
        c = h * WIDE
        grad_q, grad_k, grad_v = backward_quad(
            q_ref[0, :, c : c + WIDE],
            kv_ref[0, :, c : c + WIDE],
            kv_ref[0, :, width + c : width + c + WIDE],
            p_ref[0, h],
            g_ref[0, :, c : c + WIDE],
            allowed,
        )
        dq_ref[0, :, c : c + WIDE] = grad_q
        dkv_ref[0, :, c : c + WIDE] = grad_k
        dkv_ref[0, :, width + c : width + c + WIDE] = grad_v


def cross_backward(order, q, kv, probs, grad, mask):
    items, rows, width = q.shape
    keys = kv.shape[1]
    quads = width // WIDE
    waits = order.take()
    out = pl.pallas_call(
        cross_backward_kernel,
        grid=(items,),
        in_specs=[
            pl.BlockSpec((1, rows, width), lambda i: (i, 0, 0)),
            pl.BlockSpec((1, keys, 2 * width), lambda i: (i, 0, 0)),
            pl.BlockSpec((1, quads, QUAD * rows, keys), lambda i: (i, 0, 0, 0)),
            pl.BlockSpec((1, rows, width), lambda i: (i, 0, 0)),
            pl.BlockSpec((1, 1, keys), lambda i: (i, 0, 0)),
        ]
        + [pl.BlockSpec(memory_space=pl.ANY)] * len(waits),
        out_specs=[
            pl.BlockSpec((1, rows, width), lambda i: (i, 0, 0)),
            pl.BlockSpec((1, keys, 2 * width), lambda i: (i, 0, 0)),
        ],
        out_shape=[
            jax.ShapeDtypeStruct((items, rows, width), BF16),
            jax.ShapeDtypeStruct((items, keys, 2 * width), BF16),
        ],
        compiler_params=params(),
        cost_estimate=cost(order.long()),
    )(q, kv, probs, grad, mask, *waits)
    order.after(out[0])
    return out


def factor_of(value):
    return lax.rsqrt(jnp.mean(value * value, axis=-1, keepdims=True) + EPSILON)


AXES = {1: "core", 2: "x", 4: "y"}


def swap(value, bit):
    return lax.ppermute(value, AXES[bit], [(0, 1), (1, 0)])


class Order:
    def __init__(self):
        self.waits, self.micros = [], 0.1

    def long(self):
        micros, self.micros = self.micros, 0.1
        return micros

    def take(self):
        waits, self.waits = self.waits, []
        return waits

    def after(self, array):
        self.waits.append(array)
        return array


def hold_kernel(*refs):
    pass


def hold(order, array):
    whole = pl.BlockSpec(memory_space=pl.ANY)
    waits = order.take()
    out = pl.pallas_call(
        hold_kernel,
        in_specs=[whole] * (1 + len(waits)),
        out_specs=whole,
        out_shape=jax.ShapeDtypeStruct(array.shape, array.dtype),
        input_output_aliases={0: 0},
        compiler_params=pltpu.CompilerParams(vmem_limit_bytes=1024 * 1024),
        cost_estimate=cost(order.long()),
    )(array, *waits)
    return order.after(out)


def cost(micros):
    return pl.CostEstimate(
        flops=int(micros * 1.15e9), bytes_accessed=int(micros * 3.6e6), transcendentals=0
    )


def put_split(value, flag, axis, give_ref, keep_ref):
    half = value.shape[axis] // 2
    low, high = (value[:half], value[half:]) if axis == 0 else (value[:, :half], value[:, half:])

    @pl.when(flag == 0)
    def _():
        keep_ref[...] = low
        give_ref[...] = high

    @pl.when(flag > 0)
    def _():
        keep_ref[...] = high
        give_ref[...] = low


def product_kernel(jobs, has_add, axis, halves, flags, *refs):
    outs = refs[-halves * 2 :] if has_add else refs[-1:]
    add_ref = refs[sum(count + 1 for count, _, _ in jobs)]
    at = 0
    total = sum(steps for _, _, steps in jobs)
    for count, start, steps in jobs:
        lefts, right = refs[at : at + count], refs[at + count]
        at += count + 1

        def work(lefts=lefts, right=right, start=start):
            left = jnp.concatenate([r[...] for r in lefts], axis=1)
            value = right[0] if len(right.shape) == 3 else right[...]
            out = dot(left, value, ((0,), (0,)))
            if not has_add:
                outs[0][...] = out.astype(BF16)
                return
            out = (out + add_ref[...].astype(F32)).astype(BF16)
            if axis == 1:
                put_split(out, flags[1], 1, *outs)
                return
            which = 2 * start // total if halves > 1 else 0
            give, keep = outs[2 * which : 2 * which + 2]
            for z in range(give.shape[0]):
                part = out[128 * z : 128 * z + 128]
                put_split(part, flags[1 + which], 0, give.at[z], keep.at[z])

        if len(jobs) == 1:
            work()
        else:
            step = pl.program_id(0)
            pl.when((step >= start) & (step < start + steps))(work)


def call_product(order, axis, grid, jobs, flags, specs, operands, out_specs, out_shapes):
    waits = order.take()
    has_add = len(out_shapes) > 1
    out = pl.pallas_call(
        functools.partial(product_kernel, jobs, has_add, axis, len(out_shapes) // 2),
        grid_spec=pltpu.PrefetchScalarGridSpec(
            num_scalar_prefetch=1,
            grid=grid,
            in_specs=specs + [pl.BlockSpec(memory_space=pl.ANY)] * len(waits),
            out_specs=out_specs,
        ),
        out_shape=out_shapes,
        compiler_params=params(),
        cost_estimate=cost(order.long()),
    )(flags, *operands, *waits)
    order.after(out[0])
    return out


def grad_rows(order, pairs, flags, add=None):
    count = pairs[0][0].shape[1] // 256
    total = sum(columns for _, _, _, columns in pairs)
    tile = next(t for t in (1408, 1024) if all(c % t == 0 for _, _, _, c in pairs))
    specs, operands, jobs, start = [], [], [], 0
    for left, right, place, columns in pairs:
        rows, steps = left.shape[0], columns // tile
        specs += [
            pl.BlockSpec((rows, 128), lambda j, f, z=z: (0, 2 * z + f[0])) for z in range(count)
        ]
        block = lambda j, f, start=start, steps=steps: jnp.clip(j - start, 0, steps - 1)
        if right.ndim == 3:
            specs.append(
                pl.BlockSpec((1, rows, tile), lambda j, f, b=block, p=place: (p, 0, b(j, f)))
            )
        else:
            specs.append(
                pl.BlockSpec((rows, tile), lambda j, f, b=block, p=place: (0, p + b(j, f)))
            )
        operands += [left] * count + [right]
        jobs.append((count, start, steps))
        start += steps
    block = pl.BlockSpec((count * 128, tile), lambda j, f: (0, j))
    if add is None:
        shapes, outs = [jax.ShapeDtypeStruct((count * 128, total), BF16)], [block]
    else:
        specs.append(block)
        operands.append(add)
        halves = flags.shape[0] - 1
        shapes = [jax.ShapeDtypeStruct((count, 64, total // halves), BF16)] * (2 * halves)
        outs, most = [], start // halves
        for i in range(halves):
            place = lambda j, f, i=i: (0, 0, jnp.clip(j - i * most, 0, most - 1))
            outs += [pl.BlockSpec((count, 64, tile), place)] * 2
    return call_product(order, 0, (start,), jobs, flags, specs, operands, outs, shapes)


def grad_columns(order, left, right, flags, add=None):
    rows, width = left.shape
    half = right.shape[1] // 2
    tile = next(t for t in (1408, 1024) if width % t == 0)
    block = lambda columns: pl.BlockSpec((tile, columns), lambda j, f: (j, 0))
    specs = [
        pl.BlockSpec((rows, tile), lambda j, f: (0, j)),
        pl.BlockSpec((rows, half), lambda j, f: (0, f[0])),
    ]
    operands = [left, right]
    if add is None:
        shapes, outs = [jax.ShapeDtypeStruct((width, half), BF16)], [block(half)]
    else:
        specs.append(block(half))
        operands.append(add)
        shapes = [jax.ShapeDtypeStruct((width, half // 2), BF16)] * 2
        outs = [block(half // 2)] * 2
    steps = width // tile
    return call_product(
        order, 1, (steps,), [(1, 0, steps)], flags, specs, operands, outs, shapes
    )


def land_kernel(count, axis, flags, *refs):
    outs = refs[len(refs) - (2 * count if axis is not None else 1) :]
    column = 0
    for i in range(count):
        total = refs[2 * i][...] + refs[2 * i + 1][...]
        if axis is None:
            columns = total.shape[-1]
            outs[0][..., column : column + columns] = total
            column += columns
        elif axis == 1:
            put_split(total, flags[i], 1, *outs[2 * i : 2 * i + 2])
        else:
            for z in range(total.shape[0]):
                put_split(
                    total[z], flags[i], 0, outs[2 * i].at[z], outs[2 * i + 1].at[z]
                )


def land_sums(order, pairs, flags, axis):
    waits = order.take()
    steps = 2
    block = lambda shape: pl.BlockSpec(
        (shape[0] // steps, *shape[1:]), lambda j, f: (j,) + (0,) * (len(shape) - 1)
    )
    specs, operands, shapes = [], [], []
    for keep, got in pairs:
        specs += [block(keep.shape)] * 2
        operands += [keep, got]
        shape = list(keep.shape)
        if axis is not None:
            shape[-2 if axis == 0 else -1] //= 2
            shapes += [tuple(shape)] * 2
    if axis is None:
        total = sum(keep.shape[-1] for keep, _ in pairs)
        shapes = [(*pairs[0][0].shape[:-1], total)]
    out = pl.pallas_call(
        functools.partial(land_kernel, len(pairs), axis),
        grid_spec=pltpu.PrefetchScalarGridSpec(
            num_scalar_prefetch=1,
            grid=(steps,),
            in_specs=specs + [pl.BlockSpec(memory_space=pl.ANY)] * len(waits),
            out_specs=[block(shape) for shape in shapes],
        ),
        out_shape=[jax.ShapeDtypeStruct(shape, BF16) for shape in shapes],
        compiler_params=params(),
        cost_estimate=cost(order.long()),
    )(jnp.stack(flags), *operands, *waits)
    order.after(out[0])
    return out


def join_kernel(axis, parts, turned, flag, own_ref, got_ref, *refs):
    outs = refs[len(refs) - len(parts) :]
    half = own_ref.shape[axis]

    def put(low, high):
        column = 0
        for out, columns, turn in zip(outs, parts, turned):
            at = slice(column, column + columns)
            column += columns
            for start, ref in ((0, low), (half, high)):
                value = ref[:, at].astype(out.dtype)
                if axis == 1:
                    out[:, start : start + half] = value
                elif turn:
                    n = half // 4
                    for i, j in enumerate((0, 2, 1, 3)):
                        out[start + j * n : start + (j + 1) * n] = value[i * n : (i + 1) * n]
                else:
                    out[start : start + half] = value

    either(flag[0], put, own_ref, got_ref)


def land_join(order, own, got, flag, axis, parts, turned, kind):
    waits = order.take()
    whole = lambda shape: pl.BlockSpec(shape, lambda j, f: (0, 0))
    n, c = own.shape
    shapes = [(2 * n, columns) for columns in parts] if axis == 0 else [(n, 2 * c)]
    out = pl.pallas_call(
        functools.partial(join_kernel, axis, parts, turned),
        grid_spec=pltpu.PrefetchScalarGridSpec(
            num_scalar_prefetch=1,
            grid=(1,),
            in_specs=[whole(own.shape)] * 2 + [pl.BlockSpec(memory_space=pl.ANY)] * len(waits),
            out_specs=[whole(shape) for shape in shapes],
        ),
        out_shape=[jax.ShapeDtypeStruct(shape, kind) for shape in shapes],
        compiler_params=params(),
        cost_estimate=cost(order.long()),
    )(flag.reshape(1), own, got, *waits)
    order.after(out[0])
    return out


def segment_kernel(steps, has_next, split, waits, flag, *refs):
    x_ref, w_ref, v_ref, b_ref, g_ref = refs[:5]
    n_refs = refs[5 : 5 + 2 * has_next]
    u_ref = refs[5 + 2 * has_next] if split else None
    refs = refs[5 + 2 * has_next + split + waits :]
    if has_next:
        d_ref, gg_ref, e_ref, o_ref, acc = refs
    else:
        d_ref, gg_ref, acc = refs
    step = pl.program_id(0)
    x = x_ref[0] if len(x_ref.shape) == 3 else x_ref[...]
    size = w_ref.shape[0]
    for at, ref in ((0, w_ref), (size, u_ref)):
        if ref is None:
            continue
        partial = dot(x, ref[...], ((1,), (1,)))

        @pl.when(step == 0)
        def _(at=at, partial=partial):
            acc[:, at : at + size] = partial

        @pl.when(step > 0)
        def _(at=at, partial=partial):
            acc[:, at : at + size] += partial

    @pl.when(step == steps - 1)
    def _():
        gain = g_ref[...]
        rows, chunk = acc.shape[0], 144
        gg_ref[...] = jnp.zeros_like(gg_ref)

        @pl.loop(0, rows // chunk)
        def _(i):
            at = pl.ds(pl.multiple_of(i * chunk, chunk), chunk)
            grad = acc[at, :]
            if split:
                own, other = grad[:, :size], grad[:, size:]
                low, high = jnp.where(flag[0] == 0, own, other), jnp.where(flag[0] == 0, other, own)
                blocks = []
                for k in range(0, size, 128):
                    blocks += [low[:, k : k + 128], high[:, k : k + 128]]
                grad = jnp.concatenate(blocks, axis=1)
            value = v_ref[at, :].astype(F32)
            factor = lax.rsqrt(jnp.mean(value * value, axis=-1, keepdims=True) + EPSILON)
            scaled = gain * grad
            along = jnp.mean(scaled * value, axis=-1, keepdims=True)
            back = factor * scaled - value * (factor * factor * factor * along)
            gg_ref[...] += jnp.sum(grad * value * factor, axis=0, keepdims=True)
            total = b_ref[at, :].astype(F32) + back
            d_ref[at, :] = total
            if has_next:
                e_ref[at, :] = total.astype(BF16)

        if has_next:
            matrix = interleaved(flag[0], n_refs[0][...], n_refs[1][...])
            o_ref[...] = dot(e_ref[...], matrix, ((1,), (1,))).astype(BF16)


def segment(order, core, x, w, column, tile, value, base, gain, after=None):
    rows, width = value.shape
    steps = x.shape[-1] * (x.shape[0] if x.ndim == 3 else 1) // tile
    if x.ndim == 3:
        per = x.shape[-1] // tile
        x_spec = pl.BlockSpec((1, rows, tile), lambda k, f: (k // per, 0, k % per))
    else:
        x_spec = pl.BlockSpec((rows, tile), lambda k, f: (0, k))
    whole = pl.BlockSpec((rows, width), lambda k, f: (0, 0))
    line = pl.BlockSpec((1, width), lambda k, f: (0, 0))
    split = isinstance(w, tuple)
    w = w if split else (w,)
    w_spec = pl.BlockSpec((w[0].shape[0], tile), lambda k, f: (0, k + column))
    specs = [x_spec, w_spec, whole, whole, line]
    operands = [x, w[0], value, base, gain.reshape(1, width)]
    shapes = [
        jax.ShapeDtypeStruct((rows, width), F32),
        jax.ShapeDtypeStruct((1, width), F32),
    ]
    outs = [whole, line]
    if after is not None:
        matrix, at = after
        specs += [pl.BlockSpec((width // 2, width), lambda k, f: (0, at))] * 2
        operands += matrix
        shapes += [jax.ShapeDtypeStruct((rows, width), BF16)] * 2
        outs += [whole, whole]
    if split:
        specs.append(w_spec)
        operands.append(w[1])
    waits = order.take()
    out = pl.pallas_call(
        functools.partial(segment_kernel, steps, after is not None, split, len(waits)),
        grid_spec=pltpu.PrefetchScalarGridSpec(
            num_scalar_prefetch=1,
            grid=(steps,),
            in_specs=specs + [pl.BlockSpec(memory_space=pl.ANY)] * len(waits),
            out_specs=outs,
            scratch_shapes=[pltpu.VMEM((rows, width), F32)],
        ),
        out_shape=shapes,
        compiler_params=params(),
        cost_estimate=cost(order.long()),
    )(core.reshape(1), *operands, *waits)
    order.after(out[1])
    return out


def halves_of(value):
    starts = range(0, value.shape[1], 256)
    return [
        jnp.concatenate([value[:, k + j : k + j + 128] for k in starts], axis=1)
        for j in (0, 128)
    ]


def mlp_kernel(flag, a_ref, e_ref, wg_ref, wu_ref, vg_ref, vu_ref, wd_ref, i_ref, d_ref, mine):
    @pl.when(pl.program_id(0) == 0)
    def _():
        def put(own, other):
            mine[0] = own
            mine[1] = other

        either(flag[0], put, *halves_of(a_ref[...]))

    grad = dot(e_ref[...], wd_ref[...], ((1,), (1,)))
    product = lambda w, v: dot(mine[0], w[...], ((1,), (0,))) + dot(mine[1], v[...], ((1,), (0,)))
    gate, up = product(wg_ref, vg_ref), product(wu_ref, vu_ref)
    slope, cubic = 0.7978845608028654, 0.044715
    square = gate * gate
    bend = jnp.tanh(slope * gate * (1.0 + cubic * square))
    half = 0.5 * (1.0 + bend)
    act = gate * half
    turn = half + 0.5 * gate * (1.0 - bend * bend) * slope * (1.0 + 3.0 * cubic * square)
    i_ref[...] = (act * up).astype(BF16)
    d_ref[0] = (grad * up * turn).astype(BF16)
    d_ref[1] = (grad * act).astype(BF16)


def mlp(order, core, a3, e3, own, other, w_down):
    rows, width = a3.shape
    hidden = w_down.shape[0]
    tile = MLP_TILE
    count = hidden // tile
    whole = pl.BlockSpec((rows, width), lambda j, f: (0, 0))
    gate = pl.BlockSpec((width // 2, tile), lambda j, f: (0, j))
    up = pl.BlockSpec((width // 2, tile), lambda j, f: (0, count + j))
    return pl.pallas_call(
        mlp_kernel,
        grid_spec=pltpu.PrefetchScalarGridSpec(
            num_scalar_prefetch=1,
            grid=(count,),
            in_specs=[
                whole,
                whole,
                gate,
                up,
                gate,
                up,
                pl.BlockSpec((tile, width), lambda j, f: (j, 0)),
            ],
            out_specs=[
                pl.BlockSpec((rows, tile), lambda j, f: (0, j)),
                pl.BlockSpec((2, rows, tile), lambda j, f: (0, 0, j)),
            ],
            scratch_shapes=[pltpu.VMEM((2, rows, width // 2), BF16)],
        ),
        out_shape=[
            jax.ShapeDtypeStruct((rows, hidden), BF16),
            jax.ShapeDtypeStruct((2, rows, hidden), BF16),
        ],
        compiler_params=params(),
        cost_estimate=cost(order.long()),
    )(core.reshape(1), a3, e3, own, own, other, other, w_down)


def sorted_halves(flag, value):
    low, high = halves_of(value)
    return jnp.where(flag == 0, low, high), jnp.where(flag == 0, high, low)


def interleaved(flag, own, other):
    low, high = jnp.where(flag == 0, own, other), jnp.where(flag == 0, other, own)
    blocks = []
    for k in range(0, own.shape[0], 128):
        blocks += [low[k : k + 128], high[k : k + 128]]
    return jnp.concatenate(blocks, axis=0)


def project_kernel(flag, x_ref, own_ref, other_ref, *refs):
    out_ref, mine = refs[-2:]

    @pl.when(pl.program_id(0) == 0)
    def _():
        mine[0], mine[1] = sorted_halves(flag[0], x_ref[...])

    out = dot(mine[0], own_ref[...], ((1,), (0,))) + dot(mine[1], other_ref[...], ((1,), (0,)))
    out_ref[...] = out.astype(BF16)


def project(order, core, x, w, column, count):
    rows, width = x.shape
    waits = order.take()
    w_spec = pl.BlockSpec((width // 2, width), lambda j, f: (0, j + column))
    out = pl.pallas_call(
        project_kernel,
        grid_spec=pltpu.PrefetchScalarGridSpec(
            num_scalar_prefetch=1,
            grid=(count,),
            in_specs=[pl.BlockSpec((rows, width), lambda j, f: (0, 0)), w_spec, w_spec]
            + [pl.BlockSpec(memory_space=pl.ANY)] * len(waits),
            out_specs=pl.BlockSpec((rows, width), lambda j, f: (0, j)),
            scratch_shapes=[pltpu.VMEM((2, rows, width // 2), BF16)],
        ),
        out_shape=jax.ShapeDtypeStruct((rows, count * width), BF16),
        compiler_params=params(),
        cost_estimate=cost(order.long()),
    )(core.reshape(1), x, *w, *waits)
    return order.after(out)


def forward_norm_kernel(flag, x_ref, own_ref, other_ref, b_ref, g_ref, *refs):
    h_ref, a_ref = refs[-2:]
    mine, yours = sorted_halves(flag[0], x_ref[...])
    h_ref[...] = dot(mine, own_ref[...], ((1,), (0,))) + dot(
        yours, other_ref[...], ((1,), (0,))
    )
    gain = g_ref[...]
    rows, chunk = h_ref.shape[0], 144

    @pl.loop(0, rows // chunk)
    def _(i):
        at = pl.ds(pl.multiple_of(i * chunk, chunk), chunk)
        value = h_ref[at, :] + b_ref[at, :].astype(F32)
        h_ref[at, :] = value
        factor = lax.rsqrt(jnp.mean(value * value, axis=-1, keepdims=True) + EPSILON)
        a_ref[at, :] = (value * factor * gain).astype(BF16)


def forward_norm(order, core, x, w, column, base, gain):
    rows, width = x.shape
    waits = order.take()
    whole = pl.BlockSpec((rows, width), lambda j, f: (0, 0))
    w_spec = pl.BlockSpec((width // 2, width), lambda j, f: (0, column))
    out = pl.pallas_call(
        forward_norm_kernel,
        grid_spec=pltpu.PrefetchScalarGridSpec(
            num_scalar_prefetch=1,
            grid=(1,),
            in_specs=[
                whole,
                w_spec,
                w_spec,
                whole,
                pl.BlockSpec((1, width), lambda j, f: (0, 0)),
            ]
            + [pl.BlockSpec(memory_space=pl.ANY)] * len(waits),
            out_specs=[whole, whole],
        ),
        out_shape=[
            jax.ShapeDtypeStruct((rows, width), F32),
            jax.ShapeDtypeStruct((rows, width), BF16),
        ],
        compiler_params=params(),
        cost_estimate=cost(order.long()),
    )(core.reshape(1), x, *w, base, gain.reshape(1, width), *waits)
    order.after(out[1])
    return out


def forward_out_kernel(steps, waits, x_ref, w_ref, b_ref, *refs):
    o_ref, acc = refs[waits:]
    step = pl.program_id(0)
    partial = dot(x_ref[...], w_ref[...], ((1,), (0,)))

    @pl.when(step == 0)
    def _():
        acc[...] = partial + b_ref[...]

    @pl.when(step > 0)
    def _():
        acc[...] += partial

    @pl.when(step == steps - 1)
    def _():
        o_ref[...] = acc[...].astype(BF16)


def forward_out(order, x, w, base):
    rows, width = base.shape
    tile = next(t for t in (1408, 1024) if w.shape[0] % t == 0)
    steps = w.shape[0] // tile
    whole = pl.BlockSpec((rows, width), lambda k: (0, 0))
    waits = order.take()
    out = pl.pallas_call(
        functools.partial(forward_out_kernel, steps, len(waits)),
        grid=(steps,),
        in_specs=[
            pl.BlockSpec((rows, tile), lambda k: (0, k)),
            pl.BlockSpec((tile, width), lambda k: (k, 0)),
            whole,
        ]
        + [pl.BlockSpec(memory_space=pl.ANY)] * len(waits),
        out_specs=whole,
        out_shape=jax.ShapeDtypeStruct((rows, width), BF16),
        scratch_shapes=[pltpu.VMEM((rows, width), F32)],
        compiler_params=params(),
        cost_estimate=cost(order.long()),
    )(x, w, base, *waits)
    return order.after(out)


def back_product_kernel(flag, x_ref, own_ref, other_ref, *refs):
    w = interleaved(flag[0], own_ref[...], other_ref[...])
    refs[-1][...] = dot(x_ref[...], w, ((1,), (1,)))


def back_product(order, core, x, w):
    rows, depth = x.shape
    half = w[0].shape[0]
    waits = order.take()
    w_spec = pl.BlockSpec((128, depth), lambda j, f: (j, 0))
    out = pl.pallas_call(
        back_product_kernel,
        grid_spec=pltpu.PrefetchScalarGridSpec(
            num_scalar_prefetch=1,
            grid=(half // 128,),
            in_specs=[pl.BlockSpec((rows, depth), lambda j, f: (0, 0)), w_spec, w_spec]
            + [pl.BlockSpec(memory_space=pl.ANY)] * len(waits),
            out_specs=pl.BlockSpec((rows, 256), lambda j, f: (0, j)),
        ),
        out_shape=jax.ShapeDtypeStruct((rows, 2 * half), F32),
        compiler_params=params(),
        cost_estimate=cost(order.long()),
    )(core.reshape(1), x, *w, *waits)
    return order.after(out)


def bit_of(spot, bit):
    return (spot // bit) % 2


class Sum:
    def __init__(self, order, spot, axis, product, first, second):
        self.order, self.axis, self.product = order, axis, product
        self.first, self.second = first, second
        self.bits = bit_of(spot, 1), bit_of(spot, first), bit_of(spot, second)
        core, one, _ = self.bits
        (give,) = product(jnp.stack([1 - core, one]))
        self.flight = swap(give, 1)

    def core(self):
        core, one, _ = self.bits
        give, self.keep = self.product(jnp.stack([core, one]), self.flight)
        self.flight = swap(give, self.first)


class Part:
    def __init__(self, spot, first, second):
        self.first, self.second, self.axis = first, second, 0
        self.bits = bit_of(spot, 1), bit_of(spot, first), bit_of(spot, second)


class Pair:
    def __init__(self, order, spot, pairs):
        self.product = functools.partial(grad_rows, order, pairs)
        self.parts = [Part(spot, 2, 4), Part(spot, 4, 2)]
        self.flags = [bit_of(spot, b) for b in (1, 2, 4)]
        core, one, two = self.flags
        (give,) = self.product(jnp.stack([1 - core, one, two]))
        self.flight = swap(give, 1)

    def core(self):
        core, one, two = self.flags
        out = self.product(jnp.stack([core, one, two]), self.flight)
        for i, part in enumerate(self.parts):
            part.keep = out[2 * i + 1]
            part.flight = swap(out[2 * i], part.first)
        return self.parts


def region(axis, first, cross):
    return (first, cross) if axis == 0 else (cross, first)


def either(flag, put, one, two):
    pl.when(flag == 0)(lambda: put(one, two))
    pl.when(flag > 0)(lambda: put(two, one))


def cut_kernel(axis, z_ref, *refs):
    a_ref, b_ref = refs[-2:]
    half = z_ref.shape[2 - axis] // 2
    a_ref[0] = z_ref.at[0][region(axis, slice(None), slice(0, half))]
    b_ref[0] = z_ref.at[0][region(axis, slice(None), slice(half, None))]


def cut(order, value, axis, column, columns):
    waits = order.take()
    z, n, _ = value.shape
    shape = (z, n, columns // 2) if axis == 0 else (z, n // 2, columns)
    out = pl.pallas_call(
        functools.partial(cut_kernel, axis),
        grid=(z,),
        in_specs=[pl.BlockSpec((1, n, columns), lambda j: (j, 0, column))]
        + [pl.BlockSpec(memory_space=pl.ANY)] * len(waits),
        out_specs=[pl.BlockSpec((1, *shape[1:]), lambda j: (j, 0, 0))] * 2,
        out_shape=[jax.ShapeDtypeStruct(shape, BF16)] * 2,
        compiler_params=params(),
        cost_estimate=cost(order.long()),
    )(value, *waits)
    order.after(out[0])
    return out


def pack_kernel(tall, place, *refs):
    refs = list(refs)
    if tall:
        last_in, last_out = refs.pop(len(refs) - 3), refs.pop()
        last_out[...] = last_in[...]
    column = 0
    for ref in refs[:-1]:
        refs[-1][:, column : column + ref.shape[1]] = ref[...]
        column += ref.shape[1]


def pack(shards, seats, pieces, last=None, tall=None):
    n = shards[0].shape[0] // pieces
    specs = [
        pl.BlockSpec((n, w.shape[1]), lambda j, f, i=i: (f[i % len(seats)], 0))
        for i, w in enumerate(shards)
    ]
    total = sum(w.shape[1] for w in shards)
    operands = list(shards)
    if last is not None:
        specs.append(pl.BlockSpec(last.shape, lambda j, f: (0, 0)))
        operands.append(last)
        total += last.shape[1]
    outs, shapes = [pl.BlockSpec((n, total), lambda j, f: (0, 0))], [(n, total)]
    if tall is not None:
        piece = (tall.shape[0], tall.shape[1] // 8)
        specs.append(pl.BlockSpec(piece, lambda j, f: (0, f[0])))
        operands.append(tall)
        outs.append(pl.BlockSpec(piece, lambda j, f: (0, 0)))
        shapes.append(piece)
    return pl.pallas_call(
        functools.partial(pack_kernel, tall is not None),
        grid_spec=pltpu.PrefetchScalarGridSpec(
            num_scalar_prefetch=1, grid=(1,), in_specs=specs, out_specs=outs
        ),
        out_shape=[jax.ShapeDtypeStruct(shape, BF16) for shape in shapes],
        compiler_params=params(),
        cost_estimate=cost(1),
    )(jnp.stack(seats), *operands)


def pairs_kernel(axis, flags, *refs):
    ins, outs = refs[:4], refs[-2:]
    for i in range(2):
        size = ins[2 * i].shape[1 + axis]

        def put(low, high, out=outs[i], size=size):
            out.at[0][region(axis, slice(0, size), slice(None))] = low[0]
            out.at[0][region(axis, slice(size, None), slice(None))] = high[0]

        either(flags[i], put, ins[2 * i], ins[2 * i + 1])


def quads_kernel(axis, flags, *refs):
    a_own, a_got, b_own, b_got = refs[:4]
    out = refs[-1].at[0]
    two, half = a_own.shape[1 + axis], a_own.shape[2 - axis]
    n = two // 2

    def put_a(low, high):
        out[region(axis, slice(0, two), slice(0, half))] = low[0]
        out[region(axis, slice(two, None), slice(0, half))] = high[0]

    def put_b(low, high):
        for y in range(2):
            for x, ref in enumerate((low, high)):
                at = (2 * y + x) * n
                out[region(axis, slice(at, at + n), slice(half, None))] = ref.at[0][
                    region(axis, slice(y * n, y * n + n), slice(None))
                ]

    either(flags[1], put_a, a_own, a_got)
    either(flags[0], put_b, b_own, b_got)


def sides_kernel(axis, flags, *refs):
    a_own, a_got, b_own, b_got = refs[:4]
    out = refs[-1].at[0]
    n, half = a_own.shape[1], a_own.shape[2]

    def put_in(columns):
        def put(low, high):
            out[:n, columns] = low[0]
            out[n:, columns] = high[0]

        return put

    either(flags[0], put_in(slice(0, half)), a_own, a_got)
    either(flags[1], put_in(slice(half, None)), b_own, b_got)


def cores_kernel(axis, flags, own_ref, got_ref, *refs):
    out = refs[-1].at[0]
    size = own_ref.shape[1 + axis]

    def put(low, high):
        out[region(axis, slice(0, size), slice(None))] = low[0]
        out[region(axis, slice(size, None), slice(None))] = high[0]

    either(flags[2], put, own_ref, got_ref)


def by_shard(order, kernel, axis, flags, operands, shapes):
    waits = order.take()
    block = lambda shape: pl.BlockSpec((1, *shape[1:]), lambda j, *f: (j, 0, 0))
    out = pl.pallas_call(
        functools.partial(kernel, axis),
        grid_spec=pltpu.PrefetchScalarGridSpec(
            num_scalar_prefetch=len(flags),
            grid=(operands[0].shape[0],),
            in_specs=[block(v.shape) for v in operands]
            + [pl.BlockSpec(memory_space=pl.ANY)] * len(waits),
            out_specs=[block(shape) for shape in shapes],
        ),
        out_shape=[jax.ShapeDtypeStruct(shape, BF16) for shape in shapes],
        compiler_params=params(),
        cost_estimate=cost(order.long()),
    )(*flags, *operands, *waits)
    order.after(out[0])
    return out


class Gather:
    def __init__(self, order, spot, value, axis, column=0, columns=None):
        self.order, self.axis = order, axis
        self.flags = [jnp.stack([bit_of(spot, b) for b in (2, 4, 1)])]
        self.value, self.place = value, (column, columns or value.shape[2])

    def scaled(self, shape, along, across):
        shape = list(shape)
        shape[1 + self.axis] = shape[1 + self.axis] * along
        shape[2 - self.axis] = shape[2 - self.axis] * across // 2
        return tuple(shape)

    def run(self, kernel, flags, operands, shapes):
        return by_shard(self.order, kernel, self.axis, flags, operands, shapes)

    def one(self):
        self.a, self.b = cut(self.order, self.value, self.axis, *self.place)
        self.got = swap(self.a, 2), swap(self.b, 4)

    def two(self):
        shape = self.scaled(self.a.shape, 2, 2)
        self.a, self.b = self.run(
            pairs_kernel, self.flags, [self.a, self.got[0], self.b, self.got[1]], [shape] * 2
        )
        self.got = swap(self.a, 4), swap(self.b, 2)

    def three(self):
        shape = self.scaled(self.a.shape, 2, 4)
        (self.half,) = self.run(
            quads_kernel, self.flags, [self.a, self.got[0], self.b, self.got[1]], [shape]
        )
        self.got = swap(self.half, 1)

    def side(self):
        shape = self.scaled(self.a.shape, 2, 4)
        (self.half,) = self.run(
            sides_kernel, self.flags, [self.a, self.got[0], self.b, self.got[1]], [shape]
        )
        self.got = swap(self.half, 1)

    def halves(self):
        flat = lambda value: value.reshape(-1, value.shape[-1])
        return flat(self.half), flat(self.got)

    def four(self):
        shape = self.scaled(self.half.shape, 2, 2)
        (whole,) = self.run(cores_kernel, self.flags, [self.half, self.got], [shape])
        return whole.reshape(-1, whole.shape[-1])


def land_first(order, *sums):
    out = land_sums(
        order, [(s.keep, s.flight) for s in sums], [s.bits[2] for s in sums], sums[0].axis
    )
    for i, s in enumerate(sums):
        s.keep = out[2 * i + 1]
        s.flight = swap(out[2 * i], s.second)


def land_second(order, *sums):
    (out,) = land_sums(
        order, [(s.keep, s.flight) for s in sums], [s.bits[2] for s in sums], None
    )
    return out.reshape(-1, out.shape[-1])


def over_shards(value):
    value = lax.psum_scatter(value, "fsdp", scatter_dimension=0, tiled=True)
    return across_groups(value)


def across_groups(value):
    size = lax.axis_size("group")
    ring = [(i, (i + 1) % size) for i in range(size)]
    total = step = value
    for _ in range(size - 1):
        step = lax.ppermute(step, "group", ring)
        total = total + step
    return total


class Spread:
    def __init__(self, order, spot, value, parts, turned, axis=0):
        self.order, self.spot, self.axis = order, spot, axis
        self.value, self.parts, self.turned = value, parts, turned
        self.bits = [4, 2, 1]
        self.send()

    def send(self):
        self.flight = swap(self.value, self.bits[0])

    def land(self):
        bit = self.bits.pop(0)
        last = not self.bits
        out = land_join(
            self.order,
            self.value,
            self.flight,
            bit_of(self.spot, bit),
            self.axis,
            self.parts if last else [self.value.shape[1]],
            self.turned if last else [False],
            F32 if last else BF16,
        )
        if last:
            self.values = out
        else:
            self.value = out[0]
            self.send()


def on_device(
    text,
    memory,
    text_lengths,
    memory_mask,
    grad_out,
    self_gain,
    self_query,
    self_key,
    self_value,
    self_output,
    cross_gain,
    cross_query,
    cross_key,
    cross_value,
    cross_output,
    mlp_gain,
    mlp_gate,
    mlp_up,
    mlp_down,
):
    items, rows, width = text.shape
    keys = memory.shape[1]
    spot = 4 * lax.axis_index("y") + 2 * lax.axis_index("x") + lax.axis_index("core")

    order = Order()
    gather = lambda value: lax.all_gather(value, "fsdp", axis=0)
    own = self_gain.shape[0]
    lines = jnp.stack([self_gain, cross_gain, mlp_gain]).reshape(-1, 128)
    squares = [
        self_query,
        self_key,
        self_value,
        self_output,
        cross_key,
        cross_value,
        cross_query,
        cross_output,
    ]
    lines = jnp.pad(lines, ((0, width // 32 - lines.shape[0]), (0, 0)))
    x_bit, y_bit, core = (bit_of(spot, b) for b in (2, 4, 1))
    seat = 4 * core + 2 * y_bit + x_bit
    piece, piece_down = pack(squares, [seat], 8, lines, mlp_down)
    both = gather(piece)
    g_down = Gather(order, spot, gather(piece_down), 1)
    g_self = Gather(order, spot, both, 0, 0, 4 * width)
    g_cross = Gather(order, spot, both, 0, 1, 4 * width)
    shards = both.shape[0]
    gains = both[:, : 3 * own // 128, 8 * width :].reshape(shards, 3, own)
    gains = gains.transpose(1, 0, 2).reshape(3, width).astype(F32)
    g_wide = Gather(order, spot, gather(*pack([mlp_gate, mlp_up], [2 * core + x_bit, 2 * core + y_bit], 4)), 0)
    hidden = mlp_gate.shape[1]

    x = text.reshape(-1, width).astype(F32)
    flat_memory = memory.reshape(-1, width)
    e3 = grad_out.reshape(-1, width)
    mask = memory_mask[:, None, :]

    g_down.one()
    g_down.two()
    g_self.one()
    g_cross.one()
    order.micros = C_LONG
    g_down.three()
    g_self.two()
    g_cross.two()
    order.micros = C_LONG
    w_down = g_down.four()
    g_self.three()
    w_self = g_self.halves()
    c1 = factor_of(x)
    a1 = (x * c1 * gains[0]).astype(BF16)
    qkv = project(order, core, a1, w_self, 0, 3).reshape(items, rows, 3 * width)
    o1, p1 = self_forward(qkv, text_lengths)
    o1 = order.after(o1).reshape(-1, width)
    g_wide.one()
    g_cross.three()
    w_cross = g_cross.halves()
    order.micros = C_LONG
    h1, a2 = forward_norm(order, core, o1, w_self, 3, x, gains[1])
    kv = project(order, core, flat_memory, w_cross, 0, 2).reshape(items, keys, 2 * width)
    q2 = project(order, core, a2, w_cross, 2, 1).reshape(items, rows, width)
    o2, p2 = cross_forward(q2, kv, mask)
    o2 = order.after(o2).reshape(-1, width)
    g_wide.side()
    h2, a3 = forward_norm(order, core, o2, w_cross, 3, h1, gains[2])
    w_wide = g_wide.halves()
    inner, d_wide = mlp(order, core, a3, e3, *w_wide, w_down)
    order.take()

    s_wide = Pair(order, spot, [(a3, d_wide, 0, hidden), (a3, d_wide, 1, hidden)])
    s_down = Sum(order, spot, 1, functools.partial(grad_columns, order, inner, e3), 2, 4)
    wide = s_wide.core()
    s_down.core()
    order.micros = C_LONG
    d_h2, gg3, e2, d_o2 = segment(
        order, core, d_wide, w_wide, 0, hidden // 2, h2, e3, gains[2], (w_cross, 3)
    )
    d_q2, d_kv = cross_backward(order, q2, kv, p2, d_o2.reshape(text.shape), mask)
    d_q2 = d_q2.reshape(-1, width)
    d_kv = d_kv.reshape(-1, 2 * width)
    s_cross = Pair(
        order,
        spot,
        [
            (flat_memory, d_kv, 0, 2 * width),
            (a2, d_q2, 0, width),
            (o2, e2, 0, width),
        ],
    )
    land_first(order, *wide)
    order.micros = C_SEG2
    d_h1, gg2, e1, d_o1 = segment(
        order, core, d_q2, w_cross, 4, width // 2, h1, d_h2, gains[1], (w_self, 3)
    )
    land_first(order, s_down)
    order.micros = C_LONG
    z_wide = land_second(order, *wide)
    d_qkv = self_backward(order, qkv, p1, d_o1.reshape(text.shape)).reshape(-1, 3 * width)
    z_down = land_second(order, s_down)
    s_self = Pair(
        order,
        spot,
        [
            (a1, d_qkv, 0, 2 * width),
            (a1, d_qkv, 2, width),
            (o1, e1, 0, width),
        ],
    )
    cross = s_cross.core()
    z_wide = over_shards(z_wide)
    order.micros = C_LONG
    both = s_self.core()
    order.micros = C_LONG
    grad_text, gg1 = segment(order, core, d_qkv, w_self, 0, width, x, d_h1, gains[0])
    land_first(order, *cross)
    order.micros = C_MID
    z_wide = hold(order, z_wide)
    z_down = over_shards(z_down)
    land_first(order, *both)
    z_down = hold(order, z_down)
    z_cross = over_shards(land_second(order, *cross))
    t_wide = Spread(order, spot, z_wide, [hidden, hidden], [False, True])
    lines = jnp.concatenate([gg1, gg2, gg3]).reshape(3, shards, own).transpose(1, 0, 2)
    lines = lines.reshape(shards, -1, 128)
    lines = jnp.pad(lines, ((0, 0), (0, width // 32 - lines.shape[1]), (0, 0)))
    lines = order.after(lines.astype(BF16).reshape(-1, 128))
    z_self = land_second(order, *both)
    z_self = order.after(jnp.concatenate([z_self, lines], axis=1))
    t_wide.land()
    t_down = Spread(order, spot, z_down, [width], [False], 1)
    z_cross = hold(order, z_cross)
    z_self = over_shards(z_self)
    squares = [width] * 4
    t_cross = Spread(order, spot, z_cross, squares, [False, False, True, True])
    block_out = forward_out(order, inner, w_down, h2)
    t_down.land()
    t_cross.land()
    t_wide.land()
    z_self = hold(order, z_self)
    t_self = Spread(
        order, spot, z_self, [*squares, 128], [False, False, True, True, False]
    )
    t_down.land()
    t_wide.land()
    t_cross.land()
    t_self.land()
    grad_memory = back_product(order, core, d_kv, w_cross)
    t_down.land()
    t_self.land()
    t_cross.land()
    t_self.land()
    g_gate, g_up = t_wide.values
    (g_down,) = t_down.values
    g_ck, g_cv, g_cq, g_co = t_cross.values
    g_sq, g_sk, g_sv, g_so, lines = t_self.values
    lines = jnp.sum(lines.reshape(8, -1, 128), axis=0)
    gg = lines[: 3 * own // 128].reshape(3, own)

    return (
        block_out.reshape(text.shape),
        grad_text.reshape(text.shape),
        grad_memory.reshape(memory.shape),
        gg[0],
        g_sq,
        g_sk,
        g_sv,
        g_so,
        gg[1],
        g_cq,
        g_ck,
        g_cv,
        g_co,
        gg[2],
        g_gate,
        g_up,
        g_down,
    )


def solution(mesh):
    shape = mesh.devices.shape
    mesh = jax.sharding.Mesh(
        mesh.devices.reshape(shape[0] // 8, 2, 2, 2, shape[1]),
        ("group", "y", "x", "core", "fsdp"),
    )
    every = ("group", "y", "x", "core", "fsdp")
    rows = P(every, None, None)
    gain, weight = P("fsdp"), P("fsdp", None)
    weights = (gain, weight, weight, weight, weight) * 2 + (gain, weight, weight, weight)
    return jax.shard_map(
        on_device,
        mesh=mesh,
        in_specs=(rows, rows, P(every), P(every, None), rows) + weights,
        out_specs=(rows, rows, rows) + weights,
        check_vma=False,
    )
```

```python
import functools

import jax
import jax.numpy as jnp
from jax import lax
from jax.experimental import pallas as pl
from jax.experimental.pallas import tpu as pltpu
from jax.sharding import PartitionSpec as P

HEAD_DIM = 64
QUAD = 4
WIDE = HEAD_DIM * QUAD
EPSILON = 1e-06
MASKED = -1e30
SCALE = 0.125
VMEM_LIMIT = 44 * 1024 * 1024

C_LONG = 100
MLP_TILE = 1408
C_SEG2 = 11
C_MID = 8

BF16 = jnp.bfloat16
F32 = jnp.float32


def params():
    return pltpu.CompilerParams(vmem_limit_bytes=VMEM_LIMIT)


def dot(a, b, dims):
    return lax.dot_general(a, b, (dims, ((), ())), preferred_element_type=F32)


def stack_heads(value):
    lane = lax.broadcasted_iota(jnp.int32, value.shape, 1) // HEAD_DIM
    zero = jnp.zeros_like(value)
    return jnp.concatenate([jnp.where(lane == j, value, zero) for j in range(QUAD)], axis=0)


def join_heads(stacked):
    rows = stacked.shape[0] // QUAD
    lane = lax.broadcasted_iota(jnp.int32, (rows, WIDE), 1) // HEAD_DIM
    out = stacked[:rows]
    for j in range(1, QUAD):
        out = jnp.where(lane == j, stacked[j * rows : (j + 1) * rows], out)
    return out


def causal_mask(rows, keys, length):
    t = lax.broadcasted_iota(jnp.int32, (rows, keys), 0)
    u = lax.broadcasted_iota(jnp.int32, (rows, keys), 1)
    one = (u <= t) & (u < length)
    return jnp.concatenate([one] * QUAD, axis=0)


def forward_quad(q, k, v, allowed):
    stacked = stack_heads(q)
    scores = dot(stacked, k, ((1,), (1,))) * SCALE
    scores = jnp.where(allowed, scores, MASKED)
    top = jnp.max(scores, axis=-1, keepdims=True)
    lifted = jnp.exp(scores - top)
    total = jnp.sum(lifted, axis=-1, keepdims=True)
    probs = (lifted / total).astype(BF16)
    mixed = join_heads(dot(probs, v, ((1,), (0,))))
    return probs, mixed.astype(BF16)


def backward_quad(q, k, v, probs, grad, allowed):
    q_stack = stack_heads(q)
    g_stack = stack_heads(grad)
    grad_v = dot(probs, g_stack, ((0,), (0,)))
    grad_p = dot(g_stack, v, ((1,), (1,)))
    p = probs.astype(F32)
    inner = jnp.sum(grad_p * p, axis=-1, keepdims=True)
    grad_s = p * (grad_p - inner)
    if allowed is not None:
        grad_s = jnp.where(allowed, grad_s, 0.0)
    grad_s = grad_s.astype(BF16)
    grad_q = join_heads(dot(grad_s, k, ((1,), (0,)))) * SCALE
    grad_k = dot(grad_s, q_stack, ((0,), (0,))) * SCALE
    return grad_q.astype(BF16), grad_k.astype(BF16), grad_v.astype(BF16)


def self_forward_kernel(lengths, qkv_ref, o_ref, p_ref):
    rows, width = o_ref.shape[1], o_ref.shape[2]
    allowed = causal_mask(rows, rows, lengths[pl.program_id(0)])
    for h in range(width // WIDE):
        c = h * WIDE
        probs, mixed = forward_quad(
            qkv_ref[0, :, c : c + WIDE],
            qkv_ref[0, :, width + c : width + c + WIDE],
            qkv_ref[0, :, 2 * width + c : 2 * width + c + WIDE],
            allowed,
        )
        o_ref[0, :, c : c + WIDE] = mixed
        p_ref[0, h] = probs


def self_forward(qkv, lengths):
    items, rows, width3 = qkv.shape
    width = width3 // 3
    quads = width // WIDE
    return pl.pallas_call(
        self_forward_kernel,
        grid_spec=pltpu.PrefetchScalarGridSpec(
            num_scalar_prefetch=1,
            grid=(items,),
            in_specs=[pl.BlockSpec((1, rows, width3), lambda i, s: (i, 0, 0))],
            out_specs=[
                pl.BlockSpec((1, rows, width), lambda i, s: (i, 0, 0)),
                pl.BlockSpec((1, quads, QUAD * rows, rows), lambda i, s: (i, 0, 0, 0)),
            ],
        ),
        out_shape=[
            jax.ShapeDtypeStruct((items, rows, width), BF16),
            jax.ShapeDtypeStruct((items, quads, QUAD * rows, rows), BF16),
        ],
        compiler_params=params(),
        cost_estimate=cost(0.1),
    )(lengths, qkv)


def self_backward_kernel(qkv_ref, p_ref, g_ref, *refs):
    d_ref = refs[-1]
    width = g_ref.shape[2]
    for h in range(width // WIDE):
        c = h * WIDE
        grad_q, grad_k, grad_v = backward_quad(
            qkv_ref[0, :, c : c + WIDE],
            qkv_ref[0, :, width + c : width + c + WIDE],
            qkv_ref[0, :, 2 * width + c : 2 * width + c + WIDE],
            p_ref[0, h],
            g_ref[0, :, c : c + WIDE],
            None,
        )
        d_ref[0, :, c : c + WIDE] = grad_q
        d_ref[0, :, width + c : width + c + WIDE] = grad_k
        d_ref[0, :, 2 * width + c : 2 * width + c + WIDE] = grad_v


def self_backward(order, qkv, probs, grad):
    items, rows, width3 = qkv.shape
    width = width3 // 3
    quads = width // WIDE
    waits = order.take()
    out = pl.pallas_call(
        self_backward_kernel,
        grid=(items,),
        in_specs=[
            pl.BlockSpec((1, rows, width3), lambda i: (i, 0, 0)),
            pl.BlockSpec((1, quads, QUAD * rows, rows), lambda i: (i, 0, 0, 0)),
            pl.BlockSpec((1, rows, width), lambda i: (i, 0, 0)),
        ]
        + [pl.BlockSpec(memory_space=pl.ANY)] * len(waits),
        out_specs=pl.BlockSpec((1, rows, width3), lambda i: (i, 0, 0)),
        out_shape=jax.ShapeDtypeStruct((items, rows, width3), BF16),
        compiler_params=params(),
        cost_estimate=cost(order.long()),
    )(qkv, probs, grad, *waits)
    return order.after(out)


def cross_forward_kernel(q_ref, kv_ref, m_ref, o_ref, p_ref):
    rows, width = o_ref.shape[1], o_ref.shape[2]
    allowed = m_ref[0] > 0
    for h in range(width // WIDE):
        c = h * WIDE
        probs, mixed = forward_quad(
            q_ref[0, :, c : c + WIDE],
            kv_ref[0, :, c : c + WIDE],
            kv_ref[0, :, width + c : width + c + WIDE],
            allowed,
        )
        o_ref[0, :, c : c + WIDE] = mixed
        p_ref[0, h] = probs


def cross_forward(q, kv, mask):
    items, rows, width = q.shape
    keys = kv.shape[1]
    quads = width // WIDE
    return pl.pallas_call(
        cross_forward_kernel,
        grid=(items,),
        in_specs=[
            pl.BlockSpec((1, rows, width), lambda i: (i, 0, 0)),
            pl.BlockSpec((1, keys, 2 * width), lambda i: (i, 0, 0)),
            pl.BlockSpec((1, 1, keys), lambda i: (i, 0, 0)),
        ],
        out_specs=[
            pl.BlockSpec((1, rows, width), lambda i: (i, 0, 0)),
            pl.BlockSpec((1, quads, QUAD * rows, keys), lambda i: (i, 0, 0, 0)),
        ],
        out_shape=[
            jax.ShapeDtypeStruct((items, rows, width), BF16),
            jax.ShapeDtypeStruct((items, quads, QUAD * rows, keys), BF16),
        ],
        compiler_params=params(),
        cost_estimate=cost(0.1),
    )(q, kv, mask)


def cross_backward_kernel(q_ref, kv_ref, p_ref, g_ref, m_ref, *refs):
    dq_ref, dkv_ref = refs[-2:]
    width = g_ref.shape[2]
    allowed = m_ref[0] > 0
    for h in range(width // WIDE):
        c = h * WIDE
        grad_q, grad_k, grad_v = backward_quad(
            q_ref[0, :, c : c + WIDE],
            kv_ref[0, :, c : c + WIDE],
            kv_ref[0, :, width + c : width + c + WIDE],
            p_ref[0, h],
            g_ref[0, :, c : c + WIDE],
            allowed,
        )
        dq_ref[0, :, c : c + WIDE] = grad_q
        dkv_ref[0, :, c : c + WIDE] = grad_k
        dkv_ref[0, :, width + c : width + c + WIDE] = grad_v


def cross_backward(order, q, kv, probs, grad, mask):
    items, rows, width = q.shape
    keys = kv.shape[1]
    quads = width // WIDE
    waits = order.take()
    out = pl.pallas_call(
        cross_backward_kernel,
        grid=(items,),
        in_specs=[
            pl.BlockSpec((1, rows, width), lambda i: (i, 0, 0)),
            pl.BlockSpec((1, keys, 2 * width), lambda i: (i, 0, 0)),
            pl.BlockSpec((1, quads, QUAD * rows, keys), lambda i: (i, 0, 0, 0)),
            pl.BlockSpec((1, rows, width), lambda i: (i, 0, 0)),
            pl.BlockSpec((1, 1, keys), lambda i: (i, 0, 0)),
        ]
        + [pl.BlockSpec(memory_space=pl.ANY)] * len(waits),
        out_specs=[
            pl.BlockSpec((1, rows, width), lambda i: (i, 0, 0)),
            pl.BlockSpec((1, keys, 2 * width), lambda i: (i, 0, 0)),
        ],
        out_shape=[
            jax.ShapeDtypeStruct((items, rows, width), BF16),
            jax.ShapeDtypeStruct((items, keys, 2 * width), BF16),
        ],
        compiler_params=params(),
        cost_estimate=cost(order.long()),
    )(q, kv, probs, grad, mask, *waits)
    order.after(out[0])
    return out


def factor_of(value):
    return lax.rsqrt(jnp.mean(value * value, axis=-1, keepdims=True) + EPSILON)


AXES = {1: "core", 2: "x", 4: "y"}


def swap(value, bit):
    return lax.ppermute(value, AXES[bit], [(0, 1), (1, 0)])


class Order:
    def __init__(self):
        self.waits, self.micros = [], 0.1

    def long(self):
        micros, self.micros = self.micros, 0.1
        return micros

    def take(self):
        waits, self.waits = self.waits, []
        return waits

    def after(self, array):
        self.waits.append(array)
        return array


def hold_kernel(*refs):
    pass


def hold(order, array):
    whole = pl.BlockSpec(memory_space=pl.ANY)
    waits = order.take()
    out = pl.pallas_call(
        hold_kernel,
        in_specs=[whole] * (1 + len(waits)),
        out_specs=whole,
        out_shape=jax.ShapeDtypeStruct(array.shape, array.dtype),
        input_output_aliases={0: 0},
        compiler_params=pltpu.CompilerParams(vmem_limit_bytes=1024 * 1024),
        cost_estimate=cost(order.long()),
    )(array, *waits)
    return order.after(out)


def cost(micros):
    return pl.CostEstimate(
        flops=int(micros * 1.15e9), bytes_accessed=int(micros * 3.6e6), transcendentals=0
    )


def put_split(value, flag, axis, give_ref, keep_ref):
    half = value.shape[axis] // 2
    low, high = (value[:half], value[half:]) if axis == 0 else (value[:, :half], value[:, half:])

    @pl.when(flag == 0)
    def _():
        keep_ref[...] = low
        give_ref[...] = high

    @pl.when(flag > 0)
    def _():
        keep_ref[...] = high
        give_ref[...] = low


def product_kernel(jobs, has_add, axis, halves, flags, *refs):
    outs = refs[-halves * 2 :] if has_add else refs[-1:]
    add_ref = refs[sum(count + 1 for count, _, _ in jobs)]
    at = 0
    total = sum(steps for _, _, steps in jobs)
    for count, start, steps in jobs:
        lefts, right = refs[at : at + count], refs[at + count]
        at += count + 1

        def work(lefts=lefts, right=right, start=start):
            left = jnp.concatenate([r[...] for r in lefts], axis=1)
            value = right[0] if len(right.shape) == 3 else right[...]
            out = dot(left, value, ((0,), (0,)))
            if not has_add:
                outs[0][...] = out.astype(BF16)
                return
            out = (out + add_ref[...].astype(F32)).astype(BF16)
            if axis == 1:
                put_split(out, flags[1], 1, *outs)
                return
            which = 2 * start // total if halves > 1 else 0
            give, keep = outs[2 * which : 2 * which + 2]
            for z in range(give.shape[0]):
                part = out[128 * z : 128 * z + 128]
                put_split(part, flags[1 + which], 0, give.at[z], keep.at[z])

        if len(jobs) == 1:
            work()
        else:
            step = pl.program_id(0)
            pl.when((step >= start) & (step < start + steps))(work)


def call_product(order, axis, grid, jobs, flags, specs, operands, out_specs, out_shapes):
    waits = order.take()
    has_add = len(out_shapes) > 1
    out = pl.pallas_call(
        functools.partial(product_kernel, jobs, has_add, axis, len(out_shapes) // 2),
        grid_spec=pltpu.PrefetchScalarGridSpec(
            num_scalar_prefetch=1,
            grid=grid,
            in_specs=specs + [pl.BlockSpec(memory_space=pl.ANY)] * len(waits),
            out_specs=out_specs,
        ),
        out_shape=out_shapes,
        compiler_params=params(),
        cost_estimate=cost(order.long()),
    )(flags, *operands, *waits)
    order.after(out[0])
    return out


def grad_rows(order, pairs, flags, add=None):
    count = pairs[0][0].shape[1] // 256
    total = sum(columns for _, _, _, columns in pairs)
    tile = next(t for t in (1408, 1024) if all(c % t == 0 for _, _, _, c in pairs))
    specs, operands, jobs, start = [], [], [], 0
    for left, right, place, columns in pairs:
        rows, steps = left.shape[0], columns // tile
        specs += [
            pl.BlockSpec((rows, 128), lambda j, f, z=z: (0, 2 * z + f[0])) for z in range(count)
        ]
        block = lambda j, f, start=start, steps=steps: jnp.clip(j - start, 0, steps - 1)
        if right.ndim == 3:
            specs.append(
                pl.BlockSpec((1, rows, tile), lambda j, f, b=block, p=place: (p, 0, b(j, f)))
            )
        else:
            specs.append(
                pl.BlockSpec((rows, tile), lambda j, f, b=block, p=place: (0, p + b(j, f)))
            )
        operands += [left] * count + [right]
        jobs.append((count, start, steps))
        start += steps
    block = pl.BlockSpec((count * 128, tile), lambda j, f: (0, j))
    if add is None:
        shapes, outs = [jax.ShapeDtypeStruct((count * 128, total), BF16)], [block]
    else:
        specs.append(block)
        operands.append(add)
        halves = flags.shape[0] - 1
        shapes = [jax.ShapeDtypeStruct((count, 64, total // halves), BF16)] * (2 * halves)
        outs, most = [], start // halves
        for i in range(halves):
            place = lambda j, f, i=i: (0, 0, jnp.clip(j - i * most, 0, most - 1))
            outs += [pl.BlockSpec((count, 64, tile), place)] * 2
    return call_product(order, 0, (start,), jobs, flags, specs, operands, outs, shapes)


def grad_columns(order, left, right, flags, add=None):
    rows, width = left.shape
    half = right.shape[1] // 2
    tile = next(t for t in (1408, 1024) if width % t == 0)
    block = lambda columns: pl.BlockSpec((tile, columns), lambda j, f: (j, 0))
    specs = [
        pl.BlockSpec((rows, tile), lambda j, f: (0, j)),
        pl.BlockSpec((rows, half), lambda j, f: (0, f[0])),
    ]
    operands = [left, right]
    if add is None:
        shapes, outs = [jax.ShapeDtypeStruct((width, half), BF16)], [block(half)]
    else:
        specs.append(block(half))
        operands.append(add)
        shapes = [jax.ShapeDtypeStruct((width, half // 2), BF16)] * 2
        outs = [block(half // 2)] * 2
    steps = width // tile
    return call_product(
        order, 1, (steps,), [(1, 0, steps)], flags, specs, operands, outs, shapes
    )


def land_kernel(count, axis, flags, *refs):
    outs = refs[len(refs) - (2 * count if axis is not None else 1) :]
    column = 0
    for i in range(count):
        total = refs[2 * i][...] + refs[2 * i + 1][...]
        if axis is None:
            columns = total.shape[-1]
            outs[0][..., column : column + columns] = total
            column += columns
        elif axis == 1:
            put_split(total, flags[i], 1, *outs[2 * i : 2 * i + 2])
        else:
            for z in range(total.shape[0]):
                put_split(
                    total[z], flags[i], 0, outs[2 * i].at[z], outs[2 * i + 1].at[z]
                )


def land_sums(order, pairs, flags, axis):
    waits = order.take()
    steps = 2
    block = lambda shape: pl.BlockSpec(
        (shape[0] // steps, *shape[1:]), lambda j, f: (j,) + (0,) * (len(shape) - 1)
    )
    specs, operands, shapes = [], [], []
    for keep, got in pairs:
        specs += [block(keep.shape)] * 2
        operands += [keep, got]
        shape = list(keep.shape)
        if axis is not None:
            shape[-2 if axis == 0 else -1] //= 2
            shapes += [tuple(shape)] * 2
    if axis is None:
        total = sum(keep.shape[-1] for keep, _ in pairs)
        shapes = [(*pairs[0][0].shape[:-1], total)]
    out = pl.pallas_call(
        functools.partial(land_kernel, len(pairs), axis),
        grid_spec=pltpu.PrefetchScalarGridSpec(
            num_scalar_prefetch=1,
            grid=(steps,),
            in_specs=specs + [pl.BlockSpec(memory_space=pl.ANY)] * len(waits),
            out_specs=[block(shape) for shape in shapes],
        ),
        out_shape=[jax.ShapeDtypeStruct(shape, BF16) for shape in shapes],
        compiler_params=params(),
        cost_estimate=cost(order.long()),
    )(jnp.stack(flags), *operands, *waits)
    order.after(out[0])
    return out


def join_kernel(axis, parts, turned, flag, own_ref, got_ref, *refs):
    outs = refs[len(refs) - len(parts) :]
    half = own_ref.shape[axis]

    def put(low, high):
        column = 0
        for out, columns, turn in zip(outs, parts, turned):
            at = slice(column, column + columns)
            column += columns
            for start, ref in ((0, low), (half, high)):
                value = ref[:, at].astype(out.dtype)
                if axis == 1:
                    out[:, start : start + half] = value
                elif turn:
                    n = half // 4
                    for i, j in enumerate((0, 2, 1, 3)):
                        out[start + j * n : start + (j + 1) * n] = value[i * n : (i + 1) * n]
                else:
                    out[start : start + half] = value

    either(flag[0], put, own_ref, got_ref)


def land_join(order, own, got, flag, axis, parts, turned, kind):
    waits = order.take()
    whole = lambda shape: pl.BlockSpec(shape, lambda j, f: (0, 0))
    n, c = own.shape
    shapes = [(2 * n, columns) for columns in parts] if axis == 0 else [(n, 2 * c)]
    out = pl.pallas_call(
        functools.partial(join_kernel, axis, parts, turned),
        grid_spec=pltpu.PrefetchScalarGridSpec(
            num_scalar_prefetch=1,
            grid=(1,),
            in_specs=[whole(own.shape)] * 2 + [pl.BlockSpec(memory_space=pl.ANY)] * len(waits),
            out_specs=[whole(shape) for shape in shapes],
        ),
        out_shape=[jax.ShapeDtypeStruct(shape, kind) for shape in shapes],
        compiler_params=params(),
        cost_estimate=cost(order.long()),
    )(flag.reshape(1), own, got, *waits)
    order.after(out[0])
    return out


def segment_kernel(steps, has_next, split, waits, flag, *refs):
    x_ref, w_ref, v_ref, b_ref, g_ref = refs[:5]
    n_refs = refs[5 : 5 + 2 * has_next]
    u_ref = refs[5 + 2 * has_next] if split else None
    refs = refs[5 + 2 * has_next + split + waits :]
    if has_next:
        d_ref, gg_ref, e_ref, o_ref, acc = refs
    else:
        d_ref, gg_ref, acc = refs
    step = pl.program_id(0)
    x = x_ref[0] if len(x_ref.shape) == 3 else x_ref[...]
    size = w_ref.shape[0]
    for at, ref in ((0, w_ref), (size, u_ref)):
        if ref is None:
            continue
        partial = dot(x, ref[...], ((1,), (1,)))

        @pl.when(step == 0)
        def _(at=at, partial=partial):
            acc[:, at : at + size] = partial

        @pl.when(step > 0)
        def _(at=at, partial=partial):
            acc[:, at : at + size] += partial

    @pl.when(step == steps - 1)
    def _():
        gain = g_ref[...]
        rows, chunk = acc.shape[0], 144
        gg_ref[...] = jnp.zeros_like(gg_ref)

        @pl.loop(0, rows // chunk)
        def _(i):
            at = pl.ds(pl.multiple_of(i * chunk, chunk), chunk)
            grad = acc[at, :]
            if split:
                own, other = grad[:, :size], grad[:, size:]
                low, high = jnp.where(flag[0] == 0, own, other), jnp.where(flag[0] == 0, other, own)
                blocks = []
                for k in range(0, size, 128):
                    blocks += [low[:, k : k + 128], high[:, k : k + 128]]
                grad = jnp.concatenate(blocks, axis=1)
            value = v_ref[at, :].astype(F32)
            factor = lax.rsqrt(jnp.mean(value * value, axis=-1, keepdims=True) + EPSILON)
            scaled = gain * grad
            along = jnp.mean(scaled * value, axis=-1, keepdims=True)
            back = factor * scaled - value * (factor * factor * factor * along)
            gg_ref[...] += jnp.sum(grad * value * factor, axis=0, keepdims=True)
            total = b_ref[at, :].astype(F32) + back
            d_ref[at, :] = total
            if has_next:
                e_ref[at, :] = total.astype(BF16)

        if has_next:
            matrix = interleaved(flag[0], n_refs[0][...], n_refs[1][...])
            o_ref[...] = dot(e_ref[...], matrix, ((1,), (1,))).astype(BF16)


def segment(order, core, x, w, column, tile, value, base, gain, after=None):
    rows, width = value.shape
    steps = x.shape[-1] * (x.shape[0] if x.ndim == 3 else 1) // tile
    if x.ndim == 3:
        per = x.shape[-1] // tile
        x_spec = pl.BlockSpec((1, rows, tile), lambda k, f: (k // per, 0, k % per))
    else:
        x_spec = pl.BlockSpec((rows, tile), lambda k, f: (0, k))
    whole = pl.BlockSpec((rows, width), lambda k, f: (0, 0))
    line = pl.BlockSpec((1, width), lambda k, f: (0, 0))
    split = isinstance(w, tuple)
    w = w if split else (w,)
    w_spec = pl.BlockSpec((w[0].shape[0], tile), lambda k, f: (0, k + column))
    specs = [x_spec, w_spec, whole, whole, line]
    operands = [x, w[0], value, base, gain.reshape(1, width)]
    shapes = [
        jax.ShapeDtypeStruct((rows, width), F32),
        jax.ShapeDtypeStruct((1, width), F32),
    ]
    outs = [whole, line]
    if after is not None:
        matrix, at = after
        specs += [pl.BlockSpec((width // 2, width), lambda k, f: (0, at))] * 2
        operands += matrix
        shapes += [jax.ShapeDtypeStruct((rows, width), BF16)] * 2
        outs += [whole, whole]
    if split:
        specs.append(w_spec)
        operands.append(w[1])
    waits = order.take()
    out = pl.pallas_call(
        functools.partial(segment_kernel, steps, after is not None, split, len(waits)),
        grid_spec=pltpu.PrefetchScalarGridSpec(
            num_scalar_prefetch=1,
            grid=(steps,),
            in_specs=specs + [pl.BlockSpec(memory_space=pl.ANY)] * len(waits),
            out_specs=outs,
            scratch_shapes=[pltpu.VMEM((rows, width), F32)],
        ),
        out_shape=shapes,
        compiler_params=params(),
        cost_estimate=cost(order.long()),
    )(core.reshape(1), *operands, *waits)
    order.after(out[1])
    return out


def halves_of(value):
    starts = range(0, value.shape[1], 256)
    return [
        jnp.concatenate([value[:, k + j : k + j + 128] for k in starts], axis=1)
        for j in (0, 128)
    ]


def mlp_kernel(flag, a_ref, e_ref, wg_ref, wu_ref, vg_ref, vu_ref, wd_ref, i_ref, d_ref, mine):
    @pl.when(pl.program_id(0) == 0)
    def _():
        def put(own, other):
            mine[0] = own
            mine[1] = other

        either(flag[0], put, *halves_of(a_ref[...]))

    grad = dot(e_ref[...], wd_ref[...], ((1,), (1,)))
    product = lambda w, v: dot(mine[0], w[...], ((1,), (0,))) + dot(mine[1], v[...], ((1,), (0,)))
    gate, up = product(wg_ref, vg_ref), product(wu_ref, vu_ref)
    slope, cubic = 0.7978845608028654, 0.044715
    square = gate * gate
    bend = jnp.tanh(slope * gate * (1.0 + cubic * square))
    half = 0.5 * (1.0 + bend)
    act = gate * half
    turn = half + 0.5 * gate * (1.0 - bend * bend) * slope * (1.0 + 3.0 * cubic * square)
    i_ref[...] = (act * up).astype(BF16)
    d_ref[0] = (grad * up * turn).astype(BF16)
    d_ref[1] = (grad * act).astype(BF16)


def mlp(order, core, a3, e3, own, other, w_down):
    rows, width = a3.shape
    hidden = w_down.shape[0]
    tile = MLP_TILE
    count = hidden // tile
    whole = pl.BlockSpec((rows, width), lambda j, f: (0, 0))
    gate = pl.BlockSpec((width // 2, tile), lambda j, f: (0, j))
    up = pl.BlockSpec((width // 2, tile), lambda j, f: (0, count + j))
    return pl.pallas_call(
        mlp_kernel,
        grid_spec=pltpu.PrefetchScalarGridSpec(
            num_scalar_prefetch=1,
            grid=(count,),
            in_specs=[
                whole,
                whole,
                gate,
                up,
                gate,
                up,
                pl.BlockSpec((tile, width), lambda j, f: (j, 0)),
            ],
            out_specs=[
                pl.BlockSpec((rows, tile), lambda j, f: (0, j)),
                pl.BlockSpec((2, rows, tile), lambda j, f: (0, 0, j)),
            ],
            scratch_shapes=[pltpu.VMEM((2, rows, width // 2), BF16)],
        ),
        out_shape=[
            jax.ShapeDtypeStruct((rows, hidden), BF16),
            jax.ShapeDtypeStruct((2, rows, hidden), BF16),
        ],
        compiler_params=params(),
        cost_estimate=cost(order.long()),
    )(core.reshape(1), a3, e3, own, own, other, other, w_down)


def sorted_halves(flag, value):
    low, high = halves_of(value)
    return jnp.where(flag == 0, low, high), jnp.where(flag == 0, high, low)


def interleaved(flag, own, other):
    low, high = jnp.where(flag == 0, own, other), jnp.where(flag == 0, other, own)
    blocks = []
    for k in range(0, own.shape[0], 128):
        blocks += [low[k : k + 128], high[k : k + 128]]
    return jnp.concatenate(blocks, axis=0)


def project_kernel(flag, x_ref, own_ref, other_ref, *refs):
    out_ref, mine = refs[-2:]

    @pl.when(pl.program_id(0) == 0)
    def _():
        mine[0], mine[1] = sorted_halves(flag[0], x_ref[...])

    out = dot(mine[0], own_ref[...], ((1,), (0,))) + dot(mine[1], other_ref[...], ((1,), (0,)))
    out_ref[...] = out.astype(BF16)


def project(order, core, x, w, column, count):
    rows, width = x.shape
    waits = order.take()
    w_spec = pl.BlockSpec((width // 2, width), lambda j, f: (0, j + column))
    out = pl.pallas_call(
        project_kernel,
        grid_spec=pltpu.PrefetchScalarGridSpec(
            num_scalar_prefetch=1,
            grid=(count,),
            in_specs=[pl.BlockSpec((rows, width), lambda j, f: (0, 0)), w_spec, w_spec]
            + [pl.BlockSpec(memory_space=pl.ANY)] * len(waits),
            out_specs=pl.BlockSpec((rows, width), lambda j, f: (0, j)),
            scratch_shapes=[pltpu.VMEM((2, rows, width // 2), BF16)],
        ),
        out_shape=jax.ShapeDtypeStruct((rows, count * width), BF16),
        compiler_params=params(),
        cost_estimate=cost(order.long()),
    )(core.reshape(1), x, *w, *waits)
    return order.after(out)


def forward_norm_kernel(flag, x_ref, own_ref, other_ref, b_ref, g_ref, *refs):
    h_ref, a_ref = refs[-2:]
    mine, yours = sorted_halves(flag[0], x_ref[...])
    h_ref[...] = dot(mine, own_ref[...], ((1,), (0,))) + dot(
        yours, other_ref[...], ((1,), (0,))
    )
    gain = g_ref[...]
    rows, chunk = h_ref.shape[0], 144

    @pl.loop(0, rows // chunk)
    def _(i):
        at = pl.ds(pl.multiple_of(i * chunk, chunk), chunk)
        value = h_ref[at, :] + b_ref[at, :].astype(F32)
        h_ref[at, :] = value
        factor = lax.rsqrt(jnp.mean(value * value, axis=-1, keepdims=True) + EPSILON)
        a_ref[at, :] = (value * factor * gain).astype(BF16)


def forward_norm(order, core, x, w, column, base, gain):
    rows, width = x.shape
    waits = order.take()
    whole = pl.BlockSpec((rows, width), lambda j, f: (0, 0))
    w_spec = pl.BlockSpec((width // 2, width), lambda j, f: (0, column))
    out = pl.pallas_call(
        forward_norm_kernel,
        grid_spec=pltpu.PrefetchScalarGridSpec(
            num_scalar_prefetch=1,
            grid=(1,),
            in_specs=[
                whole,
                w_spec,
                w_spec,
                whole,
                pl.BlockSpec((1, width), lambda j, f: (0, 0)),
            ]
            + [pl.BlockSpec(memory_space=pl.ANY)] * len(waits),
            out_specs=[whole, whole],
        ),
        out_shape=[
            jax.ShapeDtypeStruct((rows, width), F32),
            jax.ShapeDtypeStruct((rows, width), BF16),
        ],
        compiler_params=params(),
        cost_estimate=cost(order.long()),
    )(core.reshape(1), x, *w, base, gain.reshape(1, width), *waits)
    order.after(out[1])
    return out


def forward_out_kernel(steps, waits, x_ref, w_ref, b_ref, *refs):
    o_ref, acc = refs[waits:]
    step = pl.program_id(0)
    partial = dot(x_ref[...], w_ref[...], ((1,), (0,)))

    @pl.when(step == 0)
    def _():
        acc[...] = partial + b_ref[...]

    @pl.when(step > 0)
    def _():
        acc[...] += partial

    @pl.when(step == steps - 1)
    def _():
        o_ref[...] = acc[...].astype(BF16)


def forward_out(order, x, w, base):
    rows, width = base.shape
    tile = next(t for t in (1408, 1024) if w.shape[0] % t == 0)
    steps = w.shape[0] // tile
    whole = pl.BlockSpec((rows, width), lambda k: (0, 0))
    waits = order.take()
    out = pl.pallas_call(
        functools.partial(forward_out_kernel, steps, len(waits)),
        grid=(steps,),
        in_specs=[
            pl.BlockSpec((rows, tile), lambda k: (0, k)),
            pl.BlockSpec((tile, width), lambda k: (k, 0)),
            whole,
        ]
        + [pl.BlockSpec(memory_space=pl.ANY)] * len(waits),
        out_specs=whole,
        out_shape=jax.ShapeDtypeStruct((rows, width), BF16),
        scratch_shapes=[pltpu.VMEM((rows, width), F32)],
        compiler_params=params(),
        cost_estimate=cost(order.long()),
    )(x, w, base, *waits)
    return order.after(out)


def back_product_kernel(flag, x_ref, own_ref, other_ref, *refs):
    w = interleaved(flag[0], own_ref[...], other_ref[...])
    refs[-1][...] = dot(x_ref[...], w, ((1,), (1,)))


def back_product(order, core, x, w):
    rows, depth = x.shape
    half = w[0].shape[0]
    waits = order.take()
    w_spec = pl.BlockSpec((128, depth), lambda j, f: (j, 0))
    out = pl.pallas_call(
        back_product_kernel,
        grid_spec=pltpu.PrefetchScalarGridSpec(
            num_scalar_prefetch=1,
            grid=(half // 128,),
            in_specs=[pl.BlockSpec((rows, depth), lambda j, f: (0, 0)), w_spec, w_spec]
            + [pl.BlockSpec(memory_space=pl.ANY)] * len(waits),
            out_specs=pl.BlockSpec((rows, 256), lambda j, f: (0, j)),
        ),
        out_shape=jax.ShapeDtypeStruct((rows, 2 * half), F32),
        compiler_params=params(),
        cost_estimate=cost(order.long()),
    )(core.reshape(1), x, *w, *waits)
    return order.after(out)


def bit_of(spot, bit):
    return (spot // bit) % 2


class Sum:
    def __init__(self, order, spot, axis, product, first, second):
        self.order, self.axis, self.product = order, axis, product
        self.first, self.second = first, second
        self.bits = bit_of(spot, 1), bit_of(spot, first), bit_of(spot, second)
        core, one, _ = self.bits
        (give,) = product(jnp.stack([1 - core, one]))
        self.flight = swap(give, 1)

    def core(self):
        core, one, _ = self.bits
        give, self.keep = self.product(jnp.stack([core, one]), self.flight)
        self.flight = swap(give, self.first)


class Part:
    def __init__(self, spot, first, second):
        self.first, self.second, self.axis = first, second, 0
        self.bits = bit_of(spot, 1), bit_of(spot, first), bit_of(spot, second)


class Pair:
    def __init__(self, order, spot, pairs):
        self.product = functools.partial(grad_rows, order, pairs)
        self.parts = [Part(spot, 2, 4), Part(spot, 4, 2)]
        self.flags = [bit_of(spot, b) for b in (1, 2, 4)]
        core, one, two = self.flags
        (give,) = self.product(jnp.stack([1 - core, one, two]))
        self.flight = swap(give, 1)

    def core(self):
        core, one, two = self.flags
        out = self.product(jnp.stack([core, one, two]), self.flight)
        for i, part in enumerate(self.parts):
            part.keep = out[2 * i + 1]
            part.flight = swap(out[2 * i], part.first)
        return self.parts


def region(axis, first, cross):
    return (first, cross) if axis == 0 else (cross, first)


def either(flag, put, one, two):
    pl.when(flag == 0)(lambda: put(one, two))
    pl.when(flag > 0)(lambda: put(two, one))


def cut_kernel(axis, z_ref, *refs):
    a_ref, b_ref = refs[-2:]
    half = z_ref.shape[2 - axis] // 2
    a_ref[0] = z_ref.at[0][region(axis, slice(None), slice(0, half))]
    b_ref[0] = z_ref.at[0][region(axis, slice(None), slice(half, None))]


def cut(order, value, axis, column, columns):
    waits = order.take()
    z, n, _ = value.shape
    shape = (z, n, columns // 2) if axis == 0 else (z, n // 2, columns)
    out = pl.pallas_call(
        functools.partial(cut_kernel, axis),
        grid=(z,),
        in_specs=[pl.BlockSpec((1, n, columns), lambda j: (j, 0, column))]
        + [pl.BlockSpec(memory_space=pl.ANY)] * len(waits),
        out_specs=[pl.BlockSpec((1, *shape[1:]), lambda j: (j, 0, 0))] * 2,
        out_shape=[jax.ShapeDtypeStruct(shape, BF16)] * 2,
        compiler_params=params(),
        cost_estimate=cost(order.long()),
    )(value, *waits)
    order.after(out[0])
    return out


def pack_kernel(tall, place, *refs):
    refs = list(refs)
    if tall:
        last_in, last_out = refs.pop(len(refs) - 3), refs.pop()
        last_out[...] = last_in[...]
    column = 0
    for ref in refs[:-1]:
        refs[-1][:, column : column + ref.shape[1]] = ref[...]
        column += ref.shape[1]


def pack(shards, seats, pieces, last=None, tall=None):
    n = shards[0].shape[0] // pieces
    specs = [
        pl.BlockSpec((n, w.shape[1]), lambda j, f, i=i: (f[i % len(seats)], 0))
        for i, w in enumerate(shards)
    ]
    total = sum(w.shape[1] for w in shards)
    operands = list(shards)
    if last is not None:
        specs.append(pl.BlockSpec(last.shape, lambda j, f: (0, 0)))
        operands.append(last)
        total += last.shape[1]
    outs, shapes = [pl.BlockSpec((n, total), lambda j, f: (0, 0))], [(n, total)]
    if tall is not None:
        piece = (tall.shape[0], tall.shape[1] // 8)
        specs.append(pl.BlockSpec(piece, lambda j, f: (0, f[0])))
        operands.append(tall)
        outs.append(pl.BlockSpec(piece, lambda j, f: (0, 0)))
        shapes.append(piece)
    return pl.pallas_call(
        functools.partial(pack_kernel, tall is not None),
        grid_spec=pltpu.PrefetchScalarGridSpec(
            num_scalar_prefetch=1, grid=(1,), in_specs=specs, out_specs=outs
        ),
        out_shape=[jax.ShapeDtypeStruct(shape, BF16) for shape in shapes],
        compiler_params=params(),
        cost_estimate=cost(1),
    )(jnp.stack(seats), *operands)


def pairs_kernel(axis, flags, *refs):
    ins, outs = refs[:4], refs[-2:]
    for i in range(2):
        size = ins[2 * i].shape[1 + axis]

        def put(low, high, out=outs[i], size=size):
            out.at[0][region(axis, slice(0, size), slice(None))] = low[0]
            out.at[0][region(axis, slice(size, None), slice(None))] = high[0]

        either(flags[i], put, ins[2 * i], ins[2 * i + 1])


def quads_kernel(axis, flags, *refs):
    a_own, a_got, b_own, b_got = refs[:4]
    out = refs[-1].at[0]
    two, half = a_own.shape[1 + axis], a_own.shape[2 - axis]
    n = two // 2

    def put_a(low, high):
        out[region(axis, slice(0, two), slice(0, half))] = low[0]
        out[region(axis, slice(two, None), slice(0, half))] = high[0]

    def put_b(low, high):
        for y in range(2):
            for x, ref in enumerate((low, high)):
                at = (2 * y + x) * n
                out[region(axis, slice(at, at + n), slice(half, None))] = ref.at[0][
                    region(axis, slice(y * n, y * n + n), slice(None))
                ]

    either(flags[1], put_a, a_own, a_got)
    either(flags[0], put_b, b_own, b_got)


def sides_kernel(axis, flags, *refs):
    a_own, a_got, b_own, b_got = refs[:4]
    out = refs[-1].at[0]
    n, half = a_own.shape[1], a_own.shape[2]

    def put_in(columns):
        def put(low, high):
            out[:n, columns] = low[0]
            out[n:, columns] = high[0]

        return put

    either(flags[0], put_in(slice(0, half)), a_own, a_got)
    either(flags[1], put_in(slice(half, None)), b_own, b_got)


def cores_kernel(axis, flags, own_ref, got_ref, *refs):
    out = refs[-1].at[0]
    size = own_ref.shape[1 + axis]

    def put(low, high):
        out[region(axis, slice(0, size), slice(None))] = low[0]
        out[region(axis, slice(size, None), slice(None))] = high[0]

    either(flags[2], put, own_ref, got_ref)


def by_shard(order, kernel, axis, flags, operands, shapes):
    waits = order.take()
    block = lambda shape: pl.BlockSpec((1, *shape[1:]), lambda j, *f: (j, 0, 0))
    out = pl.pallas_call(
        functools.partial(kernel, axis),
        grid_spec=pltpu.PrefetchScalarGridSpec(
            num_scalar_prefetch=len(flags),
            grid=(operands[0].shape[0],),
            in_specs=[block(v.shape) for v in operands]
            + [pl.BlockSpec(memory_space=pl.ANY)] * len(waits),
            out_specs=[block(shape) for shape in shapes],
        ),
        out_shape=[jax.ShapeDtypeStruct(shape, BF16) for shape in shapes],
        compiler_params=params(),
        cost_estimate=cost(order.long()),
    )(*flags, *operands, *waits)
    order.after(out[0])
    return out


class Gather:
    def __init__(self, order, spot, value, axis, column=0, columns=None):
        self.order, self.axis = order, axis
        self.flags = [jnp.stack([bit_of(spot, b) for b in (2, 4, 1)])]
        self.value, self.place = value, (column, columns or value.shape[2])

    def scaled(self, shape, along, across):
        shape = list(shape)
        shape[1 + self.axis] = shape[1 + self.axis] * along
        shape[2 - self.axis] = shape[2 - self.axis] * across // 2
        return tuple(shape)

    def run(self, kernel, flags, operands, shapes):
        return by_shard(self.order, kernel, self.axis, flags, operands, shapes)

    def one(self):
        self.a, self.b = cut(self.order, self.value, self.axis, *self.place)
        self.got = swap(self.a, 2), swap(self.b, 4)

    def two(self):
        shape = self.scaled(self.a.shape, 2, 2)
        self.a, self.b = self.run(
            pairs_kernel, self.flags, [self.a, self.got[0], self.b, self.got[1]], [shape] * 2
        )
        self.got = swap(self.a, 4), swap(self.b, 2)

    def three(self):
        shape = self.scaled(self.a.shape, 2, 4)
        (self.half,) = self.run(
            quads_kernel, self.flags, [self.a, self.got[0], self.b, self.got[1]], [shape]
        )
        self.got = swap(self.half, 1)

    def side(self):
        shape = self.scaled(self.a.shape, 2, 4)
        (self.half,) = self.run(
            sides_kernel, self.flags, [self.a, self.got[0], self.b, self.got[1]], [shape]
        )
        self.got = swap(self.half, 1)

    def halves(self):
        flat = lambda value: value.reshape(-1, value.shape[-1])
        return flat(self.half), flat(self.got)

    def four(self):
        shape = self.scaled(self.half.shape, 2, 2)
        (whole,) = self.run(cores_kernel, self.flags, [self.half, self.got], [shape])
        return whole.reshape(-1, whole.shape[-1])


def land_first(order, *sums):
    out = land_sums(
        order, [(s.keep, s.flight) for s in sums], [s.bits[2] for s in sums], sums[0].axis
    )
    for i, s in enumerate(sums):
        s.keep = out[2 * i + 1]
        s.flight = swap(out[2 * i], s.second)


def land_second(order, *sums):
    (out,) = land_sums(
        order, [(s.keep, s.flight) for s in sums], [s.bits[2] for s in sums], None
    )
    return out.reshape(-1, out.shape[-1])


def over_shards(value):
    value = lax.psum_scatter(value, "fsdp", scatter_dimension=0, tiled=True)
    return across_groups(value)


def across_groups(value):
    size = lax.axis_size("group")
    ring = [(i, (i + 1) % size) for i in range(size)]
    total = step = value
    for _ in range(size - 1):
        step = lax.ppermute(step, "group", ring)
        total = total + step
    return total


class Spread:
    def __init__(self, order, spot, value, parts, turned, axis=0):
        self.order, self.spot, self.axis = order, spot, axis
        self.value, self.parts, self.turned = value, parts, turned
        self.bits = [4, 2, 1]
        self.send()

    def send(self):
        self.flight = swap(self.value, self.bits[0])

    def land(self):
        bit = self.bits.pop(0)
        last = not self.bits
        out = land_join(
            self.order,
            self.value,
            self.flight,
            bit_of(self.spot, bit),
            self.axis,
            self.parts if last else [self.value.shape[1]],
            self.turned if last else [False],
            F32 if last else BF16,
        )
        if last:
            self.values = out
        else:
            self.value = out[0]
            self.send()


def on_device(
    text,
    memory,
    text_lengths,
    memory_mask,
    grad_out,
    self_gain,
    self_query,
    self_key,
    self_value,
    self_output,
    cross_gain,
    cross_query,
    cross_key,
    cross_value,
    cross_output,
    mlp_gain,
    mlp_gate,
    mlp_up,
    mlp_down,
):
    items, rows, width = text.shape
    keys = memory.shape[1]
    spot = 4 * lax.axis_index("y") + 2 * lax.axis_index("x") + lax.axis_index("core")

    order = Order()
    gather = lambda value: lax.all_gather(value, "fsdp", axis=0)
    own = self_gain.shape[0]
    lines = jnp.stack([self_gain, cross_gain, mlp_gain]).reshape(-1, 128)
    squares = [
        self_query,
        self_key,
        self_value,
        self_output,
        cross_key,
        cross_value,
        cross_query,
        cross_output,
    ]
    lines = jnp.pad(lines, ((0, width // 32 - lines.shape[0]), (0, 0)))
    x_bit, y_bit, core = (bit_of(spot, b) for b in (2, 4, 1))
    seat = 4 * core + 2 * y_bit + x_bit
    piece, piece_down = pack(squares, [seat], 8, lines, mlp_down)
    both = gather(piece)
    g_down = Gather(order, spot, gather(piece_down), 1)
    g_self = Gather(order, spot, both, 0, 0, 4 * width)
    g_cross = Gather(order, spot, both, 0, 1, 4 * width)
    shards = both.shape[0]
    gains = both[:, : 3 * own // 128, 8 * width :].reshape(shards, 3, own)
    gains = gains.transpose(1, 0, 2).reshape(3, width).astype(F32)
    g_wide = Gather(order, spot, gather(*pack([mlp_gate, mlp_up], [2 * core + x_bit, 2 * core + y_bit], 4)), 0)
    hidden = mlp_gate.shape[1]

    x = text.reshape(-1, width).astype(F32)
    flat_memory = memory.reshape(-1, width)
    e3 = grad_out.reshape(-1, width)
    mask = memory_mask[:, None, :]

    g_down.one()
    g_down.two()
    g_self.one()
    g_cross.one()
    order.micros = C_LONG
    g_down.three()
    g_self.two()
    g_cross.two()
    order.micros = C_LONG
    w_down = g_down.four()
    g_self.three()
    w_self = g_self.halves()
    c1 = factor_of(x)
    a1 = (x * c1 * gains[0]).astype(BF16)
    qkv = project(order, core, a1, w_self, 0, 3).reshape(items, rows, 3 * width)
    o1, p1 = self_forward(qkv, text_lengths)
    o1 = order.after(o1).reshape(-1, width)
    g_wide.one()
    g_cross.three()
    w_cross = g_cross.halves()
    order.micros = C_LONG
    h1, a2 = forward_norm(order, core, o1, w_self, 3, x, gains[1])
    kv = project(order, core, flat_memory, w_cross, 0, 2).reshape(items, keys, 2 * width)
    q2 = project(order, core, a2, w_cross, 2, 1).reshape(items, rows, width)
    o2, p2 = cross_forward(q2, kv, mask)
    o2 = order.after(o2).reshape(-1, width)
    g_wide.side()
    h2, a3 = forward_norm(order, core, o2, w_cross, 3, h1, gains[2])
    w_wide = g_wide.halves()
    inner, d_wide = mlp(order, core, a3, e3, *w_wide, w_down)
    order.take()

    s_wide = Pair(order, spot, [(a3, d_wide, 0, hidden), (a3, d_wide, 1, hidden)])
    s_down = Sum(order, spot, 1, functools.partial(grad_columns, order, inner, e3), 2, 4)
    wide = s_wide.core()
    s_down.core()
    order.micros = C_LONG
    d_h2, gg3, e2, d_o2 = segment(
        order, core, d_wide, w_wide, 0, hidden, h2, e3, gains[2], (w_cross, 3)
    )
    d_q2, d_kv = cross_backward(order, q2, kv, p2, d_o2.reshape(text.shape), mask)
    d_q2 = d_q2.reshape(-1, width)
    d_kv = d_kv.reshape(-1, 2 * width)
    s_cross = Pair(
        order,
        spot,
        [
            (flat_memory, d_kv, 0, 2 * width),
            (a2, d_q2, 0, width),
            (o2, e2, 0, width),
        ],
    )
    land_first(order, *wide)
    order.micros = C_SEG2
    d_h1, gg2, e1, d_o1 = segment(
        order, core, d_q2, w_cross, 2, width, h1, d_h2, gains[1], (w_self, 3)
    )
    land_first(order, s_down)
    order.micros = C_LONG
    z_wide = land_second(order, *wide)
    cross = s_cross.core()
    z_down = land_second(order, s_down)
    order.micros = C_LONG
    d_qkv = self_backward(order, qkv, p1, d_o1.reshape(text.shape)).reshape(-1, 3 * width)
    s_self = Pair(
        order,
        spot,
        [
            (a1, d_qkv, 0, 2 * width),
            (a1, d_qkv, 2, width),
            (o1, e1, 0, width),
        ],
    )
    land_first(order, *cross)
    z_wide = over_shards(z_wide)
    order.micros = C_LONG
    grad_text, gg1 = segment(order, core, d_qkv, w_self, 0, width, x, d_h1, gains[0])
    z_wide = hold(order, z_wide)
    z_down = over_shards(z_down)
    t_wide = Spread(order, spot, z_wide, [hidden, hidden], [False, True])
    both = s_self.core()
    z_cross = land_second(order, *cross)
    order.micros = C_LONG
    grad_memory = back_product(order, core, d_kv, w_cross)
    z_down = hold(order, z_down)
    z_cross = over_shards(z_cross)
    land_first(order, *both)
    lines = jnp.concatenate([gg1, gg2, gg3]).reshape(3, shards, own).transpose(1, 0, 2)
    lines = lines.reshape(shards, -1, 128)
    lines = jnp.pad(lines, ((0, 0), (0, width // 32 - lines.shape[1]), (0, 0)))
    lines = order.after(lines.astype(BF16).reshape(-1, 128))
    z_self = land_second(order, *both)
    z_self = order.after(jnp.concatenate([z_self, lines], axis=1))
    z_cross = hold(order, z_cross)
    z_self = over_shards(z_self)
    squares = [width] * 4
    t_wide.land()
    t_down = Spread(order, spot, z_down, [width], [False], 1)
    t_cross = Spread(order, spot, z_cross, squares, [False, False, True, True])
    block_out = forward_out(order, inner, w_down, h2)
    t_down.land()
    t_cross.land()
    t_wide.land()
    z_self = hold(order, z_self)
    t_self = Spread(
        order, spot, z_self, [*squares, 128], [False, False, True, True, False]
    )
    t_down.land()
    t_wide.land()
    t_cross.land()
    t_self.land()
    t_down.land()
    t_self.land()
    t_cross.land()
    t_self.land()
    g_gate, g_up = t_wide.values
    (g_down,) = t_down.values
    g_ck, g_cv, g_cq, g_co = t_cross.values
    g_sq, g_sk, g_sv, g_so, lines = t_self.values
    lines = jnp.sum(lines.reshape(8, -1, 128), axis=0)
    gg = lines[: 3 * own // 128].reshape(3, own)

    return (
        block_out.reshape(text.shape),
        grad_text.reshape(text.shape),
        grad_memory.reshape(memory.shape),
        gg[0],
        g_sq,
        g_sk,
        g_sv,
        g_so,
        gg[1],
        g_cq,
        g_ck,
        g_cv,
        g_co,
        gg[2],
        g_gate,
        g_up,
        g_down,
    )


def solution(mesh):
    shape = mesh.devices.shape
    mesh = jax.sharding.Mesh(
        mesh.devices.reshape(shape[0] // 8, 2, 2, 2, shape[1]),
        ("group", "y", "x", "core", "fsdp"),
    )
    every = ("group", "y", "x", "core", "fsdp")
    rows = P(every, None, None)
    gain, weight = P("fsdp"), P("fsdp", None)
    weights = (gain, weight, weight, weight, weight) * 2 + (gain, weight, weight, weight)
    return jax.shard_map(
        on_device,
        mesh=mesh,
        in_specs=(rows, rows, P(every), P(every, None), rows) + weights,
        out_specs=(rows, rows, rows) + weights,
        check_vma=False,
    )
```

```python
import functools

import jax
import jax.numpy as jnp
from jax import lax
from jax.experimental import pallas as pl
from jax.experimental.pallas import tpu as pltpu
from jax.sharding import PartitionSpec as P

HEAD_DIM = 64
QUAD = 4
WIDE = HEAD_DIM * QUAD
EPSILON = 1e-06
MASKED = -1e30
SCALE = 0.125
VMEM_LIMIT = 48 * 1024 * 1024

C_LONG = 100
MLP_TILE = 1408
C_SEG2 = 11
C_MID = 8

BF16 = jnp.bfloat16
F32 = jnp.float32


def params():
    return pltpu.CompilerParams(vmem_limit_bytes=VMEM_LIMIT)


def dot(a, b, dims):
    return lax.dot_general(a, b, (dims, ((), ())), preferred_element_type=F32)


def stack_heads(value):
    lane = lax.broadcasted_iota(jnp.int32, value.shape, 1) // HEAD_DIM
    zero = jnp.zeros_like(value)
    return jnp.concatenate([jnp.where(lane == j, value, zero) for j in range(QUAD)], axis=0)


def join_heads(stacked):
    rows = stacked.shape[0] // QUAD
    lane = lax.broadcasted_iota(jnp.int32, (rows, WIDE), 1) // HEAD_DIM
    out = stacked[:rows]
    for j in range(1, QUAD):
        out = jnp.where(lane == j, stacked[j * rows : (j + 1) * rows], out)
    return out


def causal_mask(rows, keys, length):
    t = lax.broadcasted_iota(jnp.int32, (rows, keys), 0)
    u = lax.broadcasted_iota(jnp.int32, (rows, keys), 1)
    one = (u <= t) & (u < length)
    return jnp.concatenate([one] * QUAD, axis=0)


def forward_quad(q, k, v, allowed):
    stacked = stack_heads(q)
    scores = dot(stacked, k, ((1,), (1,))) * SCALE
    scores = jnp.where(allowed, scores, MASKED)
    top = jnp.max(scores, axis=-1, keepdims=True)
    lifted = jnp.exp(scores - top)
    total = jnp.sum(lifted, axis=-1, keepdims=True)
    probs = (lifted / total).astype(BF16)
    mixed = join_heads(dot(probs, v, ((1,), (0,))))
    return probs, mixed.astype(BF16)


def backward_quad(q, k, v, probs, grad, allowed):
    q_stack = stack_heads(q)
    g_stack = stack_heads(grad)
    grad_v = dot(probs, g_stack, ((0,), (0,)))
    grad_p = dot(g_stack, v, ((1,), (1,)))
    p = probs.astype(F32)
    inner = jnp.sum(grad_p * p, axis=-1, keepdims=True)
    grad_s = p * (grad_p - inner)
    if allowed is not None:
        grad_s = jnp.where(allowed, grad_s, 0.0)
    grad_s = grad_s.astype(BF16)
    grad_q = join_heads(dot(grad_s, k, ((1,), (0,)))) * SCALE
    grad_k = dot(grad_s, q_stack, ((0,), (0,))) * SCALE
    return grad_q.astype(BF16), grad_k.astype(BF16), grad_v.astype(BF16)


def self_forward_kernel(lengths, qkv_ref, o_ref, p_ref):
    rows, width = o_ref.shape[1], o_ref.shape[2]
    allowed = causal_mask(rows, rows, lengths[pl.program_id(0)])
    for h in range(width // WIDE):
        c = h * WIDE
        probs, mixed = forward_quad(
            qkv_ref[0, :, c : c + WIDE],
            qkv_ref[0, :, width + c : width + c + WIDE],
            qkv_ref[0, :, 2 * width + c : 2 * width + c + WIDE],
            allowed,
        )
        o_ref[0, :, c : c + WIDE] = mixed
        p_ref[0, h] = probs


def self_forward(qkv, lengths):
    items, rows, width3 = qkv.shape
    width = width3 // 3
    quads = width // WIDE
    return pl.pallas_call(
        self_forward_kernel,
        grid_spec=pltpu.PrefetchScalarGridSpec(
            num_scalar_prefetch=1,
            grid=(items,),
            in_specs=[pl.BlockSpec((1, rows, width3), lambda i, s: (i, 0, 0))],
            out_specs=[
                pl.BlockSpec((1, rows, width), lambda i, s: (i, 0, 0)),
                pl.BlockSpec((1, quads, QUAD * rows, rows), lambda i, s: (i, 0, 0, 0)),
            ],
        ),
        out_shape=[
            jax.ShapeDtypeStruct((items, rows, width), BF16),
            jax.ShapeDtypeStruct((items, quads, QUAD * rows, rows), BF16),
        ],
        compiler_params=params(),
        cost_estimate=cost(0.1),
    )(lengths, qkv)


def self_backward_kernel(qkv_ref, p_ref, g_ref, *refs):
    d_ref = refs[-1]
    width = g_ref.shape[2]
    for h in range(width // WIDE):
        c = h * WIDE
        grad_q, grad_k, grad_v = backward_quad(
            qkv_ref[0, :, c : c + WIDE],
            qkv_ref[0, :, width + c : width + c + WIDE],
            qkv_ref[0, :, 2 * width + c : 2 * width + c + WIDE],
            p_ref[0, h],
            g_ref[0, :, c : c + WIDE],
            None,
        )
        d_ref[0, :, c : c + WIDE] = grad_q
        d_ref[0, :, width + c : width + c + WIDE] = grad_k
        d_ref[0, :, 2 * width + c : 2 * width + c + WIDE] = grad_v


def self_backward(order, qkv, probs, grad):
    items, rows, width3 = qkv.shape
    width = width3 // 3
    quads = width // WIDE
    waits = order.take()
    out = pl.pallas_call(
        self_backward_kernel,
        grid=(items,),
        in_specs=[
            pl.BlockSpec((1, rows, width3), lambda i: (i, 0, 0)),
            pl.BlockSpec((1, quads, QUAD * rows, rows), lambda i: (i, 0, 0, 0)),
            pl.BlockSpec((1, rows, width), lambda i: (i, 0, 0)),
        ]
        + [pl.BlockSpec(memory_space=pl.ANY)] * len(waits),
        out_specs=pl.BlockSpec((1, rows, width3), lambda i: (i, 0, 0)),
        out_shape=jax.ShapeDtypeStruct((items, rows, width3), BF16),
        compiler_params=params(),
        cost_estimate=cost(order.long()),
    )(qkv, probs, grad, *waits)
    return order.after(out)


def cross_forward_kernel(q_ref, kv_ref, m_ref, o_ref, p_ref):
    rows, width = o_ref.shape[1], o_ref.shape[2]
    allowed = m_ref[0] > 0
    for h in range(width // WIDE):
        c = h * WIDE
        probs, mixed = forward_quad(
            q_ref[0, :, c : c + WIDE],
            kv_ref[0, :, c : c + WIDE],
            kv_ref[0, :, width + c : width + c + WIDE],
            allowed,
        )
        o_ref[0, :, c : c + WIDE] = mixed
        p_ref[0, h] = probs


def cross_forward(q, kv, mask):
    items, rows, width = q.shape
    keys = kv.shape[1]
    quads = width // WIDE
    return pl.pallas_call(
        cross_forward_kernel,
        grid=(items,),
        in_specs=[
            pl.BlockSpec((1, rows, width), lambda i: (i, 0, 0)),
            pl.BlockSpec((1, keys, 2 * width), lambda i: (i, 0, 0)),
            pl.BlockSpec((1, 1, keys), lambda i: (i, 0, 0)),
        ],
        out_specs=[
            pl.BlockSpec((1, rows, width), lambda i: (i, 0, 0)),
            pl.BlockSpec((1, quads, QUAD * rows, keys), lambda i: (i, 0, 0, 0)),
        ],
        out_shape=[
            jax.ShapeDtypeStruct((items, rows, width), BF16),
            jax.ShapeDtypeStruct((items, quads, QUAD * rows, keys), BF16),
        ],
        compiler_params=params(),
        cost_estimate=cost(0.1),
    )(q, kv, mask)


def cross_backward_kernel(q_ref, kv_ref, p_ref, g_ref, m_ref, *refs):
    dq_ref, dkv_ref = refs[-2:]
    width = g_ref.shape[2]
    allowed = m_ref[0] > 0
    for h in range(width // WIDE):
        c = h * WIDE
        grad_q, grad_k, grad_v = backward_quad(
            q_ref[0, :, c : c + WIDE],
            kv_ref[0, :, c : c + WIDE],
            kv_ref[0, :, width + c : width + c + WIDE],
            p_ref[0, h],
            g_ref[0, :, c : c + WIDE],
            allowed,
        )
        dq_ref[0, :, c : c + WIDE] = grad_q
        dkv_ref[0, :, c : c + WIDE] = grad_k
        dkv_ref[0, :, width + c : width + c + WIDE] = grad_v


def cross_backward(order, q, kv, probs, grad, mask):
    items, rows, width = q.shape
    keys = kv.shape[1]
    quads = width // WIDE
    waits = order.take()
    out = pl.pallas_call(
        cross_backward_kernel,
        grid=(items,),
        in_specs=[
            pl.BlockSpec((1, rows, width), lambda i: (i, 0, 0)),
            pl.BlockSpec((1, keys, 2 * width), lambda i: (i, 0, 0)),
            pl.BlockSpec((1, quads, QUAD * rows, keys), lambda i: (i, 0, 0, 0)),
            pl.BlockSpec((1, rows, width), lambda i: (i, 0, 0)),
            pl.BlockSpec((1, 1, keys), lambda i: (i, 0, 0)),
        ]
        + [pl.BlockSpec(memory_space=pl.ANY)] * len(waits),
        out_specs=[
            pl.BlockSpec((1, rows, width), lambda i: (i, 0, 0)),
            pl.BlockSpec((1, keys, 2 * width), lambda i: (i, 0, 0)),
        ],
        out_shape=[
            jax.ShapeDtypeStruct((items, rows, width), BF16),
            jax.ShapeDtypeStruct((items, keys, 2 * width), BF16),
        ],
        compiler_params=params(),
        cost_estimate=cost(order.long()),
    )(q, kv, probs, grad, mask, *waits)
    order.after(out[0])
    return out


def factor_of(value):
    return lax.rsqrt(jnp.mean(value * value, axis=-1, keepdims=True) + EPSILON)


AXES = {1: "core", 2: "x", 4: "y"}


def swap(value, bit):
    return lax.ppermute(value, AXES[bit], [(0, 1), (1, 0)])


class Order:
    def __init__(self):
        self.waits, self.micros = [], 0.1

    def long(self):
        micros, self.micros = self.micros, 0.1
        return micros

    def take(self):
        waits, self.waits = self.waits, []
        return waits

    def after(self, array):
        self.waits.append(array)
        return array


def hold_kernel(*refs):
    pass


def hold(order, array):
    whole = pl.BlockSpec(memory_space=pl.ANY)
    waits = order.take()
    out = pl.pallas_call(
        hold_kernel,
        in_specs=[whole] * (1 + len(waits)),
        out_specs=whole,
        out_shape=jax.ShapeDtypeStruct(array.shape, array.dtype),
        input_output_aliases={0: 0},
        compiler_params=pltpu.CompilerParams(vmem_limit_bytes=1024 * 1024),
        cost_estimate=cost(order.long()),
    )(array, *waits)
    return order.after(out)


def cost(micros):
    return pl.CostEstimate(
        flops=int(micros * 1.15e9), bytes_accessed=int(micros * 3.6e6), transcendentals=0
    )


def put_split(value, flag, axis, give_ref, keep_ref):
    half = value.shape[axis] // 2
    low, high = (value[:half], value[half:]) if axis == 0 else (value[:, :half], value[:, half:])

    @pl.when(flag == 0)
    def _():
        keep_ref[...] = low
        give_ref[...] = high

    @pl.when(flag > 0)
    def _():
        keep_ref[...] = high
        give_ref[...] = low


def product_kernel(jobs, has_add, axis, halves, flags, *refs):
    outs = refs[-halves * 2 :] if has_add else refs[-1:]
    add_ref = refs[sum(count + 1 for count, _, _ in jobs)]
    at = 0
    total = sum(steps for _, _, steps in jobs)
    for count, start, steps in jobs:
        lefts, right = refs[at : at + count], refs[at + count]
        at += count + 1

        def work(lefts=lefts, right=right, start=start):
            left = jnp.concatenate([r[...] for r in lefts], axis=1)
            value = right[0] if len(right.shape) == 3 else right[...]
            out = dot(left, value, ((0,), (0,)))
            if not has_add:
                outs[0][...] = out.astype(BF16)
                return
            out = (out + add_ref[...].astype(F32)).astype(BF16)
            if axis == 1:
                put_split(out, flags[1], 1, *outs)
                return
            which = 2 * start // total if halves > 1 else 0
            give, keep = outs[2 * which : 2 * which + 2]
            for z in range(give.shape[0]):
                part = out[128 * z : 128 * z + 128]
                put_split(part, flags[1 + which], 0, give.at[z], keep.at[z])

        if len(jobs) == 1:
            work()
        else:
            step = pl.program_id(0)
            pl.when((step >= start) & (step < start + steps))(work)


def call_product(order, axis, grid, jobs, flags, specs, operands, out_specs, out_shapes):
    waits = order.take()
    has_add = len(out_shapes) > 1
    out = pl.pallas_call(
        functools.partial(product_kernel, jobs, has_add, axis, len(out_shapes) // 2),
        grid_spec=pltpu.PrefetchScalarGridSpec(
            num_scalar_prefetch=1,
            grid=grid,
            in_specs=specs + [pl.BlockSpec(memory_space=pl.ANY)] * len(waits),
            out_specs=out_specs,
        ),
        out_shape=out_shapes,
        compiler_params=params(),
        cost_estimate=cost(order.long()),
    )(flags, *operands, *waits)
    order.after(out[0])
    return out


def grad_rows(order, pairs, flags, add=None):
    count = pairs[0][0].shape[1] // 256
    total = sum(columns for _, _, _, columns in pairs)
    tile = next(t for t in (1408, 1024) if all(c % t == 0 for _, _, _, c in pairs))
    specs, operands, jobs, start = [], [], [], 0
    for left, right, place, columns in pairs:
        rows, steps = left.shape[0], columns // tile
        specs += [
            pl.BlockSpec((rows, 128), lambda j, f, z=z: (0, 2 * z + f[0])) for z in range(count)
        ]
        block = lambda j, f, start=start, steps=steps: jnp.clip(j - start, 0, steps - 1)
        if right.ndim == 3:
            specs.append(
                pl.BlockSpec((1, rows, tile), lambda j, f, b=block, p=place: (p, 0, b(j, f)))
            )
        else:
            specs.append(
                pl.BlockSpec((rows, tile), lambda j, f, b=block, p=place: (0, p + b(j, f)))
            )
        operands += [left] * count + [right]
        jobs.append((count, start, steps))
        start += steps
    block = pl.BlockSpec((count * 128, tile), lambda j, f: (0, j))
    if add is None:
        shapes, outs = [jax.ShapeDtypeStruct((count * 128, total), BF16)], [block]
    else:
        specs.append(block)
        operands.append(add)
        halves = flags.shape[0] - 1
        shapes = [jax.ShapeDtypeStruct((count, 64, total // halves), BF16)] * (2 * halves)
        outs, most = [], start // halves
        for i in range(halves):
            place = lambda j, f, i=i: (0, 0, jnp.clip(j - i * most, 0, most - 1))
            outs += [pl.BlockSpec((count, 64, tile), place)] * 2
    return call_product(order, 0, (start,), jobs, flags, specs, operands, outs, shapes)


def grad_columns(order, left, right, flags, add=None):
    rows, width = left.shape
    half = right.shape[1] // 2
    tile = next(t for t in (1408, 1024) if width % t == 0)
    block = lambda columns: pl.BlockSpec((tile, columns), lambda j, f: (j, 0))
    specs = [
        pl.BlockSpec((rows, tile), lambda j, f: (0, j)),
        pl.BlockSpec((rows, half), lambda j, f: (0, f[0])),
    ]
    operands = [left, right]
    if add is None:
        shapes, outs = [jax.ShapeDtypeStruct((width, half), BF16)], [block(half)]
    else:
        specs.append(block(half))
        operands.append(add)
        shapes = [jax.ShapeDtypeStruct((width, half // 2), BF16)] * 2
        outs = [block(half // 2)] * 2
    steps = width // tile
    return call_product(
        order, 1, (steps,), [(1, 0, steps)], flags, specs, operands, outs, shapes
    )


def land_kernel(count, axis, flags, *refs):
    outs = refs[len(refs) - (2 * count if axis is not None else 1) :]
    column = 0
    for i in range(count):
        total = refs[2 * i][...] + refs[2 * i + 1][...]
        if axis is None:
            columns = total.shape[-1]
            outs[0][..., column : column + columns] = total
            column += columns
        elif axis == 1:
            put_split(total, flags[i], 1, *outs[2 * i : 2 * i + 2])
        else:
            for z in range(total.shape[0]):
                put_split(
                    total[z], flags[i], 0, outs[2 * i].at[z], outs[2 * i + 1].at[z]
                )


def land_sums(order, pairs, flags, axis):
    waits = order.take()
    steps = 2
    block = lambda shape: pl.BlockSpec(
        (shape[0] // steps, *shape[1:]), lambda j, f: (j,) + (0,) * (len(shape) - 1)
    )
    specs, operands, shapes = [], [], []
    for keep, got in pairs:
        specs += [block(keep.shape)] * 2
        operands += [keep, got]
        shape = list(keep.shape)
        if axis is not None:
            shape[-2 if axis == 0 else -1] //= 2
            shapes += [tuple(shape)] * 2
    if axis is None:
        total = sum(keep.shape[-1] for keep, _ in pairs)
        shapes = [(*pairs[0][0].shape[:-1], total)]
    out = pl.pallas_call(
        functools.partial(land_kernel, len(pairs), axis),
        grid_spec=pltpu.PrefetchScalarGridSpec(
            num_scalar_prefetch=1,
            grid=(steps,),
            in_specs=specs + [pl.BlockSpec(memory_space=pl.ANY)] * len(waits),
            out_specs=[block(shape) for shape in shapes],
        ),
        out_shape=[jax.ShapeDtypeStruct(shape, BF16) for shape in shapes],
        compiler_params=params(),
        cost_estimate=cost(order.long()),
    )(jnp.stack(flags), *operands, *waits)
    order.after(out[0])
    return out


def join_kernel(axis, parts, turned, flag, own_ref, got_ref, *refs):
    outs = refs[len(refs) - len(parts) :]
    half = own_ref.shape[axis]

    def put(low, high):
        column = 0
        for out, columns, turn in zip(outs, parts, turned):
            at = slice(column, column + columns)
            column += columns
            for start, ref in ((0, low), (half, high)):
                value = ref[:, at].astype(out.dtype)
                if axis == 1:
                    out[:, start : start + half] = value
                elif turn:
                    n = half // 4
                    for i, j in enumerate((0, 2, 1, 3)):
                        out[start + j * n : start + (j + 1) * n] = value[i * n : (i + 1) * n]
                else:
                    out[start : start + half] = value

    either(flag[0], put, own_ref, got_ref)


def land_join(order, own, got, flag, axis, parts, turned, kind):
    waits = order.take()
    whole = lambda shape: pl.BlockSpec(shape, lambda j, f: (0, 0))
    n, c = own.shape
    shapes = [(2 * n, columns) for columns in parts] if axis == 0 else [(n, 2 * c)]
    out = pl.pallas_call(
        functools.partial(join_kernel, axis, parts, turned),
        grid_spec=pltpu.PrefetchScalarGridSpec(
            num_scalar_prefetch=1,
            grid=(1,),
            in_specs=[whole(own.shape)] * 2 + [pl.BlockSpec(memory_space=pl.ANY)] * len(waits),
            out_specs=[whole(shape) for shape in shapes],
        ),
        out_shape=[jax.ShapeDtypeStruct(shape, kind) for shape in shapes],
        compiler_params=params(),
        cost_estimate=cost(order.long()),
    )(flag.reshape(1), own, got, *waits)
    order.after(out[0])
    return out


def segment_kernel(steps, has_next, split, waits, flag, *refs):
    x_ref, w_ref, v_ref, b_ref, g_ref = refs[:5]
    n_refs = refs[5 : 5 + 2 * has_next]
    u_ref = refs[5 + 2 * has_next] if split else None
    refs = refs[5 + 2 * has_next + split + waits :]
    if has_next:
        d_ref, gg_ref, e_ref, o_ref, acc = refs
    else:
        d_ref, gg_ref, acc = refs
    step = pl.program_id(0)
    x = x_ref[0] if len(x_ref.shape) == 3 else x_ref[...]
    size = w_ref.shape[0]
    for at, ref in ((0, w_ref), (size, u_ref)):
        if ref is None:
            continue
        partial = dot(x, ref[...], ((1,), (1,)))

        @pl.when(step == 0)
        def _(at=at, partial=partial):
            acc[:, at : at + size] = partial

        @pl.when(step > 0)
        def _(at=at, partial=partial):
            acc[:, at : at + size] += partial

    @pl.when(step == steps - 1)
    def _():
        gain = g_ref[...]
        rows, chunk = acc.shape[0], 144
        gg_ref[...] = jnp.zeros_like(gg_ref)

        @pl.loop(0, rows // chunk)
        def _(i):
            at = pl.ds(pl.multiple_of(i * chunk, chunk), chunk)
            grad = acc[at, :]
            if split:
                own, other = grad[:, :size], grad[:, size:]
                low, high = jnp.where(flag[0] == 0, own, other), jnp.where(flag[0] == 0, other, own)
                blocks = []
                for k in range(0, size, 128):
                    blocks += [low[:, k : k + 128], high[:, k : k + 128]]
                grad = jnp.concatenate(blocks, axis=1)
            value = v_ref[at, :].astype(F32)
            factor = lax.rsqrt(jnp.mean(value * value, axis=-1, keepdims=True) + EPSILON)
            scaled = gain * grad
            along = jnp.mean(scaled * value, axis=-1, keepdims=True)
            back = factor * scaled - value * (factor * factor * factor * along)
            gg_ref[...] += jnp.sum(grad * value * factor, axis=0, keepdims=True)
            total = b_ref[at, :].astype(F32) + back
            d_ref[at, :] = total
            if has_next:
                e_ref[at, :] = total.astype(BF16)

        if has_next:
            matrix = interleaved(flag[0], n_refs[0][...], n_refs[1][...])
            o_ref[...] = dot(e_ref[...], matrix, ((1,), (1,))).astype(BF16)


def segment(order, core, x, w, column, tile, value, base, gain, after=None):
    rows, width = value.shape
    steps = x.shape[-1] * (x.shape[0] if x.ndim == 3 else 1) // tile
    if x.ndim == 3:
        per = x.shape[-1] // tile
        x_spec = pl.BlockSpec((1, rows, tile), lambda k, f: (k // per, 0, k % per))
    else:
        x_spec = pl.BlockSpec((rows, tile), lambda k, f: (0, k))
    whole = pl.BlockSpec((rows, width), lambda k, f: (0, 0))
    line = pl.BlockSpec((1, width), lambda k, f: (0, 0))
    split = isinstance(w, tuple)
    w = w if split else (w,)
    w_spec = pl.BlockSpec((w[0].shape[0], tile), lambda k, f: (0, k + column))
    specs = [x_spec, w_spec, whole, whole, line]
    operands = [x, w[0], value, base, gain.reshape(1, width)]
    shapes = [
        jax.ShapeDtypeStruct((rows, width), F32),
        jax.ShapeDtypeStruct((1, width), F32),
    ]
    outs = [whole, line]
    if after is not None:
        matrix, at = after
        specs += [pl.BlockSpec((width // 2, width), lambda k, f: (0, at))] * 2
        operands += matrix
        shapes += [jax.ShapeDtypeStruct((rows, width), BF16)] * 2
        outs += [whole, whole]
    if split:
        specs.append(w_spec)
        operands.append(w[1])
    waits = order.take()
    out = pl.pallas_call(
        functools.partial(segment_kernel, steps, after is not None, split, len(waits)),
        grid_spec=pltpu.PrefetchScalarGridSpec(
            num_scalar_prefetch=1,
            grid=(steps,),
            in_specs=specs + [pl.BlockSpec(memory_space=pl.ANY)] * len(waits),
            out_specs=outs,
            scratch_shapes=[pltpu.VMEM((rows, width), F32)],
        ),
        out_shape=shapes,
        compiler_params=params(),
        cost_estimate=cost(order.long()),
    )(core.reshape(1), *operands, *waits)
    order.after(out[1])
    return out


def halves_of(value):
    starts = range(0, value.shape[1], 256)
    return [
        jnp.concatenate([value[:, k + j : k + j + 128] for k in starts], axis=1)
        for j in (0, 128)
    ]


def mlp_kernel(flag, a_ref, e_ref, wg_ref, wu_ref, vg_ref, vu_ref, wd_ref, i_ref, d_ref, mine):
    @pl.when(pl.program_id(0) == 0)
    def _():
        def put(own, other):
            mine[0] = own
            mine[1] = other

        either(flag[0], put, *halves_of(a_ref[...]))

    grad = dot(e_ref[...], wd_ref[...], ((1,), (1,)))
    product = lambda w, v: dot(mine[0], w[...], ((1,), (0,))) + dot(mine[1], v[...], ((1,), (0,)))
    gate, up = product(wg_ref, vg_ref), product(wu_ref, vu_ref)
    slope, cubic = 0.7978845608028654, 0.044715
    square = gate * gate
    bend = jnp.tanh(slope * gate * (1.0 + cubic * square))
    half = 0.5 * (1.0 + bend)
    act = gate * half
    turn = half + 0.5 * gate * (1.0 - bend * bend) * slope * (1.0 + 3.0 * cubic * square)
    i_ref[...] = (act * up).astype(BF16)
    d_ref[0] = (grad * up * turn).astype(BF16)
    d_ref[1] = (grad * act).astype(BF16)


def mlp(order, core, a3, e3, own, other, w_down):
    rows, width = a3.shape
    hidden = w_down.shape[0]
    tile = MLP_TILE
    count = hidden // tile
    whole = pl.BlockSpec((rows, width), lambda j, f: (0, 0))
    gate = pl.BlockSpec((width // 2, tile), lambda j, f: (0, j))
    up = pl.BlockSpec((width // 2, tile), lambda j, f: (0, count + j))
    return pl.pallas_call(
        mlp_kernel,
        grid_spec=pltpu.PrefetchScalarGridSpec(
            num_scalar_prefetch=1,
            grid=(count,),
            in_specs=[
                whole,
                whole,
                gate,
                up,
                gate,
                up,
                pl.BlockSpec((tile, width), lambda j, f: (j, 0)),
            ],
            out_specs=[
                pl.BlockSpec((rows, tile), lambda j, f: (0, j)),
                pl.BlockSpec((2, rows, tile), lambda j, f: (0, 0, j)),
            ],
            scratch_shapes=[pltpu.VMEM((2, rows, width // 2), BF16)],
        ),
        out_shape=[
            jax.ShapeDtypeStruct((rows, hidden), BF16),
            jax.ShapeDtypeStruct((2, rows, hidden), BF16),
        ],
        compiler_params=params(),
        cost_estimate=cost(order.long()),
    )(core.reshape(1), a3, e3, own, own, other, other, w_down)


def sorted_halves(flag, value):
    low, high = halves_of(value)
    return jnp.where(flag == 0, low, high), jnp.where(flag == 0, high, low)


def interleaved(flag, own, other):
    low, high = jnp.where(flag == 0, own, other), jnp.where(flag == 0, other, own)
    blocks = []
    for k in range(0, own.shape[0], 128):
        blocks += [low[k : k + 128], high[k : k + 128]]
    return jnp.concatenate(blocks, axis=0)


def project_kernel(flag, x_ref, own_ref, other_ref, *refs):
    out_ref, mine = refs[-2:]

    @pl.when(pl.program_id(0) == 0)
    def _():
        mine[0], mine[1] = sorted_halves(flag[0], x_ref[...])

    out = dot(mine[0], own_ref[...], ((1,), (0,))) + dot(mine[1], other_ref[...], ((1,), (0,)))
    out_ref[...] = out.astype(BF16)


def project(order, core, x, w, column, count):
    rows, width = x.shape
    waits = order.take()
    w_spec = pl.BlockSpec((width // 2, width), lambda j, f: (0, j + column))
    out = pl.pallas_call(
        project_kernel,
        grid_spec=pltpu.PrefetchScalarGridSpec(
            num_scalar_prefetch=1,
            grid=(count,),
            in_specs=[pl.BlockSpec((rows, width), lambda j, f: (0, 0)), w_spec, w_spec]
            + [pl.BlockSpec(memory_space=pl.ANY)] * len(waits),
            out_specs=pl.BlockSpec((rows, width), lambda j, f: (0, j)),
            scratch_shapes=[pltpu.VMEM((2, rows, width // 2), BF16)],
        ),
        out_shape=jax.ShapeDtypeStruct((rows, count * width), BF16),
        compiler_params=params(),
        cost_estimate=cost(order.long()),
    )(core.reshape(1), x, *w, *waits)
    return order.after(out)


def forward_norm_kernel(flag, x_ref, own_ref, other_ref, b_ref, g_ref, *refs):
    h_ref, a_ref = refs[-2:]
    mine, yours = sorted_halves(flag[0], x_ref[...])
    h_ref[...] = dot(mine, own_ref[...], ((1,), (0,))) + dot(
        yours, other_ref[...], ((1,), (0,))
    )
    gain = g_ref[...]
    rows, chunk = h_ref.shape[0], 144

    @pl.loop(0, rows // chunk)
    def _(i):
        at = pl.ds(pl.multiple_of(i * chunk, chunk), chunk)
        value = h_ref[at, :] + b_ref[at, :].astype(F32)
        h_ref[at, :] = value
        factor = lax.rsqrt(jnp.mean(value * value, axis=-1, keepdims=True) + EPSILON)
        a_ref[at, :] = (value * factor * gain).astype(BF16)


def forward_norm(order, core, x, w, column, base, gain):
    rows, width = x.shape
    waits = order.take()
    whole = pl.BlockSpec((rows, width), lambda j, f: (0, 0))
    w_spec = pl.BlockSpec((width // 2, width), lambda j, f: (0, column))
    out = pl.pallas_call(
        forward_norm_kernel,
        grid_spec=pltpu.PrefetchScalarGridSpec(
            num_scalar_prefetch=1,
            grid=(1,),
            in_specs=[
                whole,
                w_spec,
                w_spec,
                whole,
                pl.BlockSpec((1, width), lambda j, f: (0, 0)),
            ]
            + [pl.BlockSpec(memory_space=pl.ANY)] * len(waits),
            out_specs=[whole, whole],
        ),
        out_shape=[
            jax.ShapeDtypeStruct((rows, width), F32),
            jax.ShapeDtypeStruct((rows, width), BF16),
        ],
        compiler_params=params(),
        cost_estimate=cost(order.long()),
    )(core.reshape(1), x, *w, base, gain.reshape(1, width), *waits)
    order.after(out[1])
    return out


def forward_out_kernel(steps, waits, x_ref, w_ref, b_ref, *refs):
    o_ref, acc = refs[waits:]
    step = pl.program_id(0)
    partial = dot(x_ref[...], w_ref[...], ((1,), (0,)))

    @pl.when(step == 0)
    def _():
        acc[...] = partial + b_ref[...]

    @pl.when(step > 0)
    def _():
        acc[...] += partial

    @pl.when(step == steps - 1)
    def _():
        o_ref[...] = acc[...].astype(BF16)


def forward_out(order, x, w, base):
    rows, width = base.shape
    tile = next(t for t in (1408, 1024) if w.shape[0] % t == 0)
    steps = w.shape[0] // tile
    whole = pl.BlockSpec((rows, width), lambda k: (0, 0))
    waits = order.take()
    out = pl.pallas_call(
        functools.partial(forward_out_kernel, steps, len(waits)),
        grid=(steps,),
        in_specs=[
            pl.BlockSpec((rows, tile), lambda k: (0, k)),
            pl.BlockSpec((tile, width), lambda k: (k, 0)),
            whole,
        ]
        + [pl.BlockSpec(memory_space=pl.ANY)] * len(waits),
        out_specs=whole,
        out_shape=jax.ShapeDtypeStruct((rows, width), BF16),
        scratch_shapes=[pltpu.VMEM((rows, width), F32)],
        compiler_params=params(),
        cost_estimate=cost(order.long()),
    )(x, w, base, *waits)
    return order.after(out)


def back_product_kernel(flag, x_ref, own_ref, other_ref, *refs):
    w = interleaved(flag[0], own_ref[...], other_ref[...])
    refs[-1][...] = dot(x_ref[...], w, ((1,), (1,)))


def back_product(order, core, x, w):
    rows, depth = x.shape
    half = w[0].shape[0]
    waits = order.take()
    w_spec = pl.BlockSpec((128, depth), lambda j, f: (j, 0))
    out = pl.pallas_call(
        back_product_kernel,
        grid_spec=pltpu.PrefetchScalarGridSpec(
            num_scalar_prefetch=1,
            grid=(half // 128,),
            in_specs=[pl.BlockSpec((rows, depth), lambda j, f: (0, 0)), w_spec, w_spec]
            + [pl.BlockSpec(memory_space=pl.ANY)] * len(waits),
            out_specs=pl.BlockSpec((rows, 256), lambda j, f: (0, j)),
        ),
        out_shape=jax.ShapeDtypeStruct((rows, 2 * half), F32),
        compiler_params=params(),
        cost_estimate=cost(order.long()),
    )(core.reshape(1), x, *w, *waits)
    return order.after(out)


def bit_of(spot, bit):
    return (spot // bit) % 2


class Sum:
    def __init__(self, order, spot, axis, product, first, second):
        self.order, self.axis, self.product = order, axis, product
        self.first, self.second = first, second
        self.bits = bit_of(spot, 1), bit_of(spot, first), bit_of(spot, second)
        core, one, _ = self.bits
        (give,) = product(jnp.stack([1 - core, one]))
        self.flight = swap(give, 1)

    def core(self):
        core, one, _ = self.bits
        give, self.keep = self.product(jnp.stack([core, one]), self.flight)
        self.flight = swap(give, self.first)


class Part:
    def __init__(self, spot, first, second):
        self.first, self.second, self.axis = first, second, 0
        self.bits = bit_of(spot, 1), bit_of(spot, first), bit_of(spot, second)


class Pair:
    def __init__(self, order, spot, pairs):
        self.product = functools.partial(grad_rows, order, pairs)
        self.parts = [Part(spot, 2, 4), Part(spot, 4, 2)]
        self.flags = [bit_of(spot, b) for b in (1, 2, 4)]
        core, one, two = self.flags
        (give,) = self.product(jnp.stack([1 - core, one, two]))
        self.flight = swap(give, 1)

    def core(self):
        core, one, two = self.flags
        out = self.product(jnp.stack([core, one, two]), self.flight)
        for i, part in enumerate(self.parts):
            part.keep = out[2 * i + 1]
            part.flight = swap(out[2 * i], part.first)
        return self.parts


def region(axis, first, cross):
    return (first, cross) if axis == 0 else (cross, first)


def either(flag, put, one, two):
    pl.when(flag == 0)(lambda: put(one, two))
    pl.when(flag > 0)(lambda: put(two, one))


def cut_kernel(axis, z_ref, *refs):
    a_ref, b_ref = refs[-2:]
    half = z_ref.shape[2 - axis] // 2
    a_ref[0] = z_ref.at[0][region(axis, slice(None), slice(0, half))]
    b_ref[0] = z_ref.at[0][region(axis, slice(None), slice(half, None))]


def cut(order, value, axis, column, columns):
    waits = order.take()
    z, n, _ = value.shape
    shape = (z, n, columns // 2) if axis == 0 else (z, n // 2, columns)
    out = pl.pallas_call(
        functools.partial(cut_kernel, axis),
        grid=(z,),
        in_specs=[pl.BlockSpec((1, n, columns), lambda j: (j, 0, column))]
        + [pl.BlockSpec(memory_space=pl.ANY)] * len(waits),
        out_specs=[pl.BlockSpec((1, *shape[1:]), lambda j: (j, 0, 0))] * 2,
        out_shape=[jax.ShapeDtypeStruct(shape, BF16)] * 2,
        compiler_params=params(),
        cost_estimate=cost(order.long()),
    )(value, *waits)
    order.after(out[0])
    return out


def pack_kernel(tall, place, *refs):
    refs = list(refs)
    if tall:
        last_in, last_out = refs.pop(len(refs) - 3), refs.pop()
        last_out[...] = last_in[...]
    column = 0
    for ref in refs[:-1]:
        refs[-1][:, column : column + ref.shape[1]] = ref[...]
        column += ref.shape[1]


def pack(shards, seats, pieces, last=None, tall=None):
    n = shards[0].shape[0] // pieces
    specs = [
        pl.BlockSpec((n, w.shape[1]), lambda j, f, i=i: (f[i % len(seats)], 0))
        for i, w in enumerate(shards)
    ]
    total = sum(w.shape[1] for w in shards)
    operands = list(shards)
    if last is not None:
        specs.append(pl.BlockSpec(last.shape, lambda j, f: (0, 0)))
        operands.append(last)
        total += last.shape[1]
    outs, shapes = [pl.BlockSpec((n, total), lambda j, f: (0, 0))], [(n, total)]
    if tall is not None:
        piece = (tall.shape[0], tall.shape[1] // 8)
        specs.append(pl.BlockSpec(piece, lambda j, f: (0, f[0])))
        operands.append(tall)
        outs.append(pl.BlockSpec(piece, lambda j, f: (0, 0)))
        shapes.append(piece)
    return pl.pallas_call(
        functools.partial(pack_kernel, tall is not None),
        grid_spec=pltpu.PrefetchScalarGridSpec(
            num_scalar_prefetch=1, grid=(1,), in_specs=specs, out_specs=outs
        ),
        out_shape=[jax.ShapeDtypeStruct(shape, BF16) for shape in shapes],
        compiler_params=params(),
        cost_estimate=cost(1),
    )(jnp.stack(seats), *operands)


def pairs_kernel(axis, flags, *refs):
    ins, outs = refs[:4], refs[-2:]
    for i in range(2):
        size = ins[2 * i].shape[1 + axis]

        def put(low, high, out=outs[i], size=size):
            out.at[0][region(axis, slice(0, size), slice(None))] = low[0]
            out.at[0][region(axis, slice(size, None), slice(None))] = high[0]

        either(flags[i], put, ins[2 * i], ins[2 * i + 1])


def quads_kernel(axis, flags, *refs):
    a_own, a_got, b_own, b_got = refs[:4]
    out = refs[-1].at[0]
    two, half = a_own.shape[1 + axis], a_own.shape[2 - axis]
    n = two // 2

    def put_a(low, high):
        out[region(axis, slice(0, two), slice(0, half))] = low[0]
        out[region(axis, slice(two, None), slice(0, half))] = high[0]

    def put_b(low, high):
        for y in range(2):
            for x, ref in enumerate((low, high)):
                at = (2 * y + x) * n
                out[region(axis, slice(at, at + n), slice(half, None))] = ref.at[0][
                    region(axis, slice(y * n, y * n + n), slice(None))
                ]

    either(flags[1], put_a, a_own, a_got)
    either(flags[0], put_b, b_own, b_got)


def sides_kernel(axis, flags, *refs):
    a_own, a_got, b_own, b_got = refs[:4]
    out = refs[-1].at[0]
    n, half = a_own.shape[1], a_own.shape[2]

    def put_in(columns):
        def put(low, high):
            out[:n, columns] = low[0]
            out[n:, columns] = high[0]

        return put

    either(flags[0], put_in(slice(0, half)), a_own, a_got)
    either(flags[1], put_in(slice(half, None)), b_own, b_got)


def cores_kernel(axis, flags, own_ref, got_ref, *refs):
    out = refs[-1].at[0]
    size = own_ref.shape[1 + axis]

    def put(low, high):
        out[region(axis, slice(0, size), slice(None))] = low[0]
        out[region(axis, slice(size, None), slice(None))] = high[0]

    either(flags[2], put, own_ref, got_ref)


def by_shard(order, kernel, axis, flags, operands, shapes):
    waits = order.take()
    block = lambda shape: pl.BlockSpec((1, *shape[1:]), lambda j, *f: (j, 0, 0))
    out = pl.pallas_call(
        functools.partial(kernel, axis),
        grid_spec=pltpu.PrefetchScalarGridSpec(
            num_scalar_prefetch=len(flags),
            grid=(operands[0].shape[0],),
            in_specs=[block(v.shape) for v in operands]
            + [pl.BlockSpec(memory_space=pl.ANY)] * len(waits),
            out_specs=[block(shape) for shape in shapes],
        ),
        out_shape=[jax.ShapeDtypeStruct(shape, BF16) for shape in shapes],
        compiler_params=params(),
        cost_estimate=cost(order.long()),
    )(*flags, *operands, *waits)
    order.after(out[0])
    return out


class Gather:
    def __init__(self, order, spot, value, axis, column=0, columns=None):
        self.order, self.axis = order, axis
        self.flags = [jnp.stack([bit_of(spot, b) for b in (2, 4, 1)])]
        self.value, self.place = value, (column, columns or value.shape[2])

    def scaled(self, shape, along, across):
        shape = list(shape)
        shape[1 + self.axis] = shape[1 + self.axis] * along
        shape[2 - self.axis] = shape[2 - self.axis] * across // 2
        return tuple(shape)

    def run(self, kernel, flags, operands, shapes):
        return by_shard(self.order, kernel, self.axis, flags, operands, shapes)

    def one(self):
        self.a, self.b = cut(self.order, self.value, self.axis, *self.place)
        self.got = swap(self.a, 2), swap(self.b, 4)

    def two(self):
        shape = self.scaled(self.a.shape, 2, 2)
        self.a, self.b = self.run(
            pairs_kernel, self.flags, [self.a, self.got[0], self.b, self.got[1]], [shape] * 2
        )
        self.got = swap(self.a, 4), swap(self.b, 2)

    def three(self):
        shape = self.scaled(self.a.shape, 2, 4)
        (self.half,) = self.run(
            quads_kernel, self.flags, [self.a, self.got[0], self.b, self.got[1]], [shape]
        )
        self.got = swap(self.half, 1)

    def side(self):
        shape = self.scaled(self.a.shape, 2, 4)
        (self.half,) = self.run(
            sides_kernel, self.flags, [self.a, self.got[0], self.b, self.got[1]], [shape]
        )
        self.got = swap(self.half, 1)

    def halves(self):
        flat = lambda value: value.reshape(-1, value.shape[-1])
        return flat(self.half), flat(self.got)

    def four(self):
        shape = self.scaled(self.half.shape, 2, 2)
        (whole,) = self.run(cores_kernel, self.flags, [self.half, self.got], [shape])
        return whole.reshape(-1, whole.shape[-1])


def land_first(order, *sums):
    out = land_sums(
        order, [(s.keep, s.flight) for s in sums], [s.bits[2] for s in sums], sums[0].axis
    )
    for i, s in enumerate(sums):
        s.keep = out[2 * i + 1]
        s.flight = swap(out[2 * i], s.second)


def land_second(order, *sums):
    (out,) = land_sums(
        order, [(s.keep, s.flight) for s in sums], [s.bits[2] for s in sums], None
    )
    return out.reshape(-1, out.shape[-1])


def over_shards(value):
    value = lax.psum_scatter(value, "fsdp", scatter_dimension=0, tiled=True)
    return across_groups(value)


def across_groups(value):
    size = lax.axis_size("group")
    ring = [(i, (i + 1) % size) for i in range(size)]
    total = step = value
    for _ in range(size - 1):
        step = lax.ppermute(step, "group", ring)
        total = total + step
    return total


class Spread:
    def __init__(self, order, spot, value, parts, turned, axis=0):
        self.order, self.spot, self.axis = order, spot, axis
        self.value, self.parts, self.turned = value, parts, turned
        self.bits = [4, 2, 1]
        self.send()

    def send(self):
        self.flight = swap(self.value, self.bits[0])

    def land(self):
        bit = self.bits.pop(0)
        last = not self.bits
        out = land_join(
            self.order,
            self.value,
            self.flight,
            bit_of(self.spot, bit),
            self.axis,
            self.parts if last else [self.value.shape[1]],
            self.turned if last else [False],
            F32 if last else BF16,
        )
        if last:
            self.values = out
        else:
            self.value = out[0]
            self.send()


def on_device(
    text,
    memory,
    text_lengths,
    memory_mask,
    grad_out,
    self_gain,
    self_query,
    self_key,
    self_value,
    self_output,
    cross_gain,
    cross_query,
    cross_key,
    cross_value,
    cross_output,
    mlp_gain,
    mlp_gate,
    mlp_up,
    mlp_down,
):
    items, rows, width = text.shape
    keys = memory.shape[1]
    spot = 4 * lax.axis_index("y") + 2 * lax.axis_index("x") + lax.axis_index("core")

    order = Order()
    gather = lambda value: lax.all_gather(value, "fsdp", axis=0)
    own = self_gain.shape[0]
    lines = jnp.stack([self_gain, cross_gain, mlp_gain]).reshape(-1, 128)
    squares = [
        self_query,
        self_key,
        self_value,
        self_output,
        cross_key,
        cross_value,
        cross_query,
        cross_output,
    ]
    lines = jnp.pad(lines, ((0, width // 32 - lines.shape[0]), (0, 0)))
    x_bit, y_bit, core = (bit_of(spot, b) for b in (2, 4, 1))
    seat = 4 * core + 2 * y_bit + x_bit
    piece, piece_down = pack(squares, [seat], 8, lines, mlp_down)
    both = gather(piece)
    g_down = Gather(order, spot, gather(piece_down), 1)
    g_self = Gather(order, spot, both, 0, 0, 4 * width)
    g_cross = Gather(order, spot, both, 0, 1, 4 * width)
    shards = both.shape[0]
    gains = both[:, : 3 * own // 128, 8 * width :].reshape(shards, 3, own)
    gains = gains.transpose(1, 0, 2).reshape(3, width).astype(F32)
    g_wide = Gather(order, spot, gather(*pack([mlp_gate, mlp_up], [2 * core + x_bit, 2 * core + y_bit], 4)), 0)
    hidden = mlp_gate.shape[1]

    x = text.reshape(-1, width).astype(F32)
    flat_memory = memory.reshape(-1, width)
    e3 = grad_out.reshape(-1, width)
    mask = memory_mask[:, None, :]

    g_down.one()
    g_down.two()
    g_self.one()
    g_cross.one()
    order.micros = C_LONG
    g_down.three()
    g_self.two()
    g_cross.two()
    order.micros = C_LONG
    w_down = g_down.four()
    g_self.three()
    w_self = g_self.halves()
    c1 = factor_of(x)
    a1 = (x * c1 * gains[0]).astype(BF16)
    qkv = project(order, core, a1, w_self, 0, 3).reshape(items, rows, 3 * width)
    o1, p1 = self_forward(qkv, text_lengths)
    o1 = order.after(o1).reshape(-1, width)
    g_wide.one()
    g_cross.three()
    w_cross = g_cross.halves()
    order.micros = C_LONG
    h1, a2 = forward_norm(order, core, o1, w_self, 3, x, gains[1])
    kv = project(order, core, flat_memory, w_cross, 0, 2).reshape(items, keys, 2 * width)
    q2 = project(order, core, a2, w_cross, 2, 1).reshape(items, rows, width)
    o2, p2 = cross_forward(q2, kv, mask)
    o2 = order.after(o2).reshape(-1, width)
    g_wide.side()
    h2, a3 = forward_norm(order, core, o2, w_cross, 3, h1, gains[2])
    w_wide = g_wide.halves()
    inner, d_wide = mlp(order, core, a3, e3, *w_wide, w_down)
    order.take()

    s_wide = Pair(order, spot, [(a3, d_wide, 0, hidden), (a3, d_wide, 1, hidden)])
    s_down = Sum(order, spot, 1, functools.partial(grad_columns, order, inner, e3), 2, 4)
    wide = s_wide.core()
    s_down.core()
    order.micros = C_LONG
    d_h2, gg3, e2, d_o2 = segment(
        order, core, d_wide, w_wide, 0, hidden, h2, e3, gains[2], (w_cross, 3)
    )
    d_q2, d_kv = cross_backward(order, q2, kv, p2, d_o2.reshape(text.shape), mask)
    d_q2 = d_q2.reshape(-1, width)
    d_kv = d_kv.reshape(-1, 2 * width)
    s_cross = Pair(
        order,
        spot,
        [
            (flat_memory, d_kv, 0, 2 * width),
            (a2, d_q2, 0, width),
            (o2, e2, 0, width),
        ],
    )
    land_first(order, *wide)
    order.micros = C_SEG2
    d_h1, gg2, e1, d_o1 = segment(
        order, core, d_q2, w_cross, 2, width, h1, d_h2, gains[1], (w_self, 3)
    )
    land_first(order, s_down)
    order.micros = C_LONG
    z_wide = land_second(order, *wide)
    cross = s_cross.core()
    z_down = land_second(order, s_down)
    order.micros = C_LONG
    d_qkv = self_backward(order, qkv, p1, d_o1.reshape(text.shape)).reshape(-1, 3 * width)
    s_self = Pair(
        order,
        spot,
        [
            (a1, d_qkv, 0, 2 * width),
            (a1, d_qkv, 2, width),
            (o1, e1, 0, width),
        ],
    )
    land_first(order, *cross)
    z_wide = over_shards(z_wide)
    order.micros = C_LONG
    grad_text, gg1 = segment(order, core, d_qkv, w_self, 0, width, x, d_h1, gains[0])
    z_wide = hold(order, z_wide)
    z_down = over_shards(z_down)
    t_wide = Spread(order, spot, z_wide, [hidden, hidden], [False, True])
    both = s_self.core()
    z_cross = land_second(order, *cross)
    order.micros = C_LONG
    grad_memory = back_product(order, core, d_kv, w_cross)
    z_down = hold(order, z_down)
    z_cross = over_shards(z_cross)
    land_first(order, *both)
    lines = jnp.concatenate([gg1, gg2, gg3]).reshape(3, shards, own).transpose(1, 0, 2)
    lines = lines.reshape(shards, -1, 128)
    lines = jnp.pad(lines, ((0, 0), (0, width // 32 - lines.shape[1]), (0, 0)))
    lines = order.after(lines.astype(BF16).reshape(-1, 128))
    z_self = land_second(order, *both)
    z_self = order.after(jnp.concatenate([z_self, lines], axis=1))
    z_cross = hold(order, z_cross)
    z_self = over_shards(z_self)
    squares = [width] * 4
    t_wide.land()
    t_down = Spread(order, spot, z_down, [width], [False], 1)
    t_cross = Spread(order, spot, z_cross, squares, [False, False, True, True])
    block_out = forward_out(order, inner, w_down, h2)
    t_down.land()
    t_cross.land()
    t_wide.land()
    z_self = hold(order, z_self)
    t_self = Spread(
        order, spot, z_self, [*squares, 128], [False, False, True, True, False]
    )
    t_down.land()
    t_wide.land()
    t_cross.land()
    t_self.land()
    t_down.land()
    t_self.land()
    t_cross.land()
    t_self.land()
    g_gate, g_up = t_wide.values
    (g_down,) = t_down.values
    g_ck, g_cv, g_cq, g_co = t_cross.values
    g_sq, g_sk, g_sv, g_so, lines = t_self.values
    lines = jnp.sum(lines.reshape(8, -1, 128), axis=0)
    gg = lines[: 3 * own // 128].reshape(3, own)

    return (
        block_out.reshape(text.shape),
        grad_text.reshape(text.shape),
        grad_memory.reshape(memory.shape),
        gg[0],
        g_sq,
        g_sk,
        g_sv,
        g_so,
        gg[1],
        g_cq,
        g_ck,
        g_cv,
        g_co,
        gg[2],
        g_gate,
        g_up,
        g_down,
    )


def solution(mesh):
    shape = mesh.devices.shape
    mesh = jax.sharding.Mesh(
        mesh.devices.reshape(shape[0] // 8, 2, 2, 2, shape[1]),
        ("group", "y", "x", "core", "fsdp"),
    )
    every = ("group", "y", "x", "core", "fsdp")
    rows = P(every, None, None)
    gain, weight = P("fsdp"), P("fsdp", None)
    weights = (gain, weight, weight, weight, weight) * 2 + (gain, weight, weight, weight)
    return jax.shard_map(
        on_device,
        mesh=mesh,
        in_specs=(rows, rows, P(every), P(every, None), rows) + weights,
        out_specs=(rows, rows, rows) + weights,
        check_vma=False,
    )
```

```python
import functools

import jax
import jax.numpy as jnp
from jax import lax
from jax.experimental import pallas as pl
from jax.experimental.pallas import tpu as pltpu
from jax.sharding import PartitionSpec as P

HEAD_DIM = 64
QUAD = 4
WIDE = HEAD_DIM * QUAD
EPSILON = 1e-06
MASKED = -1e30
SCALE = 0.125
VMEM_LIMIT = 50 * 1024 * 1024

C_LONG = 100
MLP_TILE = 1408
C_SEG2 = 11
C_MID = 8

BF16 = jnp.bfloat16
F32 = jnp.float32


def params():
    return pltpu.CompilerParams(vmem_limit_bytes=VMEM_LIMIT)


def dot(a, b, dims):
    return lax.dot_general(a, b, (dims, ((), ())), preferred_element_type=F32)


def stack_heads(value):
    lane = lax.broadcasted_iota(jnp.int32, value.shape, 1) // HEAD_DIM
    zero = jnp.zeros_like(value)
    return jnp.concatenate([jnp.where(lane == j, value, zero) for j in range(QUAD)], axis=0)


def join_heads(stacked):
    rows = stacked.shape[0] // QUAD
    lane = lax.broadcasted_iota(jnp.int32, (rows, WIDE), 1) // HEAD_DIM
    out = stacked[:rows]
    for j in range(1, QUAD):
        out = jnp.where(lane == j, stacked[j * rows : (j + 1) * rows], out)
    return out


def causal_mask(rows, keys, length):
    t = lax.broadcasted_iota(jnp.int32, (rows, keys), 0)
    u = lax.broadcasted_iota(jnp.int32, (rows, keys), 1)
    one = (u <= t) & (u < length)
    return jnp.concatenate([one] * QUAD, axis=0)


def forward_quad(q, k, v, allowed):
    stacked = stack_heads(q)
    scores = dot(stacked, k, ((1,), (1,))) * SCALE
    scores = jnp.where(allowed, scores, MASKED)
    top = jnp.max(scores, axis=-1, keepdims=True)
    lifted = jnp.exp(scores - top)
    total = jnp.sum(lifted, axis=-1, keepdims=True)
    probs = (lifted / total).astype(BF16)
    mixed = join_heads(dot(probs, v, ((1,), (0,))))
    return probs, mixed.astype(BF16)


def backward_quad(q, k, v, probs, grad, allowed):
    q_stack = stack_heads(q)
    g_stack = stack_heads(grad)
    grad_v = dot(probs, g_stack, ((0,), (0,)))
    grad_p = dot(g_stack, v, ((1,), (1,)))
    p = probs.astype(F32)
    inner = jnp.sum(grad_p * p, axis=-1, keepdims=True)
    grad_s = p * (grad_p - inner)
    if allowed is not None:
        grad_s = jnp.where(allowed, grad_s, 0.0)
    grad_s = grad_s.astype(BF16)
    grad_q = join_heads(dot(grad_s, k, ((1,), (0,)))) * SCALE
    grad_k = dot(grad_s, q_stack, ((0,), (0,))) * SCALE
    return grad_q.astype(BF16), grad_k.astype(BF16), grad_v.astype(BF16)


def self_forward_kernel(lengths, qkv_ref, o_ref, p_ref):
    rows, width = o_ref.shape[1], o_ref.shape[2]
    allowed = causal_mask(rows, rows, lengths[pl.program_id(0)])
    for h in range(width // WIDE):
        c = h * WIDE
        probs, mixed = forward_quad(
            qkv_ref[0, :, c : c + WIDE],
            qkv_ref[0, :, width + c : width + c + WIDE],
            qkv_ref[0, :, 2 * width + c : 2 * width + c + WIDE],
            allowed,
        )
        o_ref[0, :, c : c + WIDE] = mixed
        p_ref[0, h] = probs


def self_forward(qkv, lengths):
    items, rows, width3 = qkv.shape
    width = width3 // 3
    quads = width // WIDE
    return pl.pallas_call(
        self_forward_kernel,
        grid_spec=pltpu.PrefetchScalarGridSpec(
            num_scalar_prefetch=1,
            grid=(items,),
            in_specs=[pl.BlockSpec((1, rows, width3), lambda i, s: (i, 0, 0))],
            out_specs=[
                pl.BlockSpec((1, rows, width), lambda i, s: (i, 0, 0)),
                pl.BlockSpec((1, quads, QUAD * rows, rows), lambda i, s: (i, 0, 0, 0)),
            ],
        ),
        out_shape=[
            jax.ShapeDtypeStruct((items, rows, width), BF16),
            jax.ShapeDtypeStruct((items, quads, QUAD * rows, rows), BF16),
        ],
        compiler_params=params(),
        cost_estimate=cost(0.1),
    )(lengths, qkv)


def self_backward_kernel(qkv_ref, p_ref, g_ref, *refs):
    d_ref = refs[-1]
    width = g_ref.shape[2]
    for h in range(width // WIDE):
        c = h * WIDE
        grad_q, grad_k, grad_v = backward_quad(
            qkv_ref[0, :, c : c + WIDE],
            qkv_ref[0, :, width + c : width + c + WIDE],
            qkv_ref[0, :, 2 * width + c : 2 * width + c + WIDE],
            p_ref[0, h],
            g_ref[0, :, c : c + WIDE],
            None,
        )
        d_ref[0, :, c : c + WIDE] = grad_q
        d_ref[0, :, width + c : width + c + WIDE] = grad_k
        d_ref[0, :, 2 * width + c : 2 * width + c + WIDE] = grad_v


def self_backward(order, qkv, probs, grad):
    items, rows, width3 = qkv.shape
    width = width3 // 3
    quads = width // WIDE
    waits = order.take()
    out = pl.pallas_call(
        self_backward_kernel,
        grid=(items,),
        in_specs=[
            pl.BlockSpec((1, rows, width3), lambda i: (i, 0, 0)),
            pl.BlockSpec((1, quads, QUAD * rows, rows), lambda i: (i, 0, 0, 0)),
            pl.BlockSpec((1, rows, width), lambda i: (i, 0, 0)),
        ]
        + [pl.BlockSpec(memory_space=pl.ANY)] * len(waits),
        out_specs=pl.BlockSpec((1, rows, width3), lambda i: (i, 0, 0)),
        out_shape=jax.ShapeDtypeStruct((items, rows, width3), BF16),
        compiler_params=params(),
        cost_estimate=cost(order.long()),
    )(qkv, probs, grad, *waits)
    return order.after(out)


def cross_forward_kernel(q_ref, kv_ref, m_ref, o_ref, p_ref):
    rows, width = o_ref.shape[1], o_ref.shape[2]
    allowed = m_ref[0] > 0
    for h in range(width // WIDE):
        c = h * WIDE
        probs, mixed = forward_quad(
            q_ref[0, :, c : c + WIDE],
            kv_ref[0, :, c : c + WIDE],
            kv_ref[0, :, width + c : width + c + WIDE],
            allowed,
        )
        o_ref[0, :, c : c + WIDE] = mixed
        p_ref[0, h] = probs


def cross_forward(q, kv, mask):
    items, rows, width = q.shape
    keys = kv.shape[1]
    quads = width // WIDE
    return pl.pallas_call(
        cross_forward_kernel,
        grid=(items,),
        in_specs=[
            pl.BlockSpec((1, rows, width), lambda i: (i, 0, 0)),
            pl.BlockSpec((1, keys, 2 * width), lambda i: (i, 0, 0)),
            pl.BlockSpec((1, 1, keys), lambda i: (i, 0, 0)),
        ],
        out_specs=[
            pl.BlockSpec((1, rows, width), lambda i: (i, 0, 0)),
            pl.BlockSpec((1, quads, QUAD * rows, keys), lambda i: (i, 0, 0, 0)),
        ],
        out_shape=[
            jax.ShapeDtypeStruct((items, rows, width), BF16),
            jax.ShapeDtypeStruct((items, quads, QUAD * rows, keys), BF16),
        ],
        compiler_params=params(),
        cost_estimate=cost(0.1),
    )(q, kv, mask)


def cross_backward_kernel(q_ref, kv_ref, p_ref, g_ref, m_ref, *refs):
    dq_ref, dkv_ref = refs[-2:]
    width = g_ref.shape[2]
    allowed = m_ref[0] > 0
    for h in range(width // WIDE):
        c = h * WIDE
        grad_q, grad_k, grad_v = backward_quad(
            q_ref[0, :, c : c + WIDE],
            kv_ref[0, :, c : c + WIDE],
            kv_ref[0, :, width + c : width + c + WIDE],
            p_ref[0, h],
            g_ref[0, :, c : c + WIDE],
            allowed,
        )
        dq_ref[0, :, c : c + WIDE] = grad_q
        dkv_ref[0, :, c : c + WIDE] = grad_k
        dkv_ref[0, :, width + c : width + c + WIDE] = grad_v


def cross_backward(order, q, kv, probs, grad, mask):
    items, rows, width = q.shape
    keys = kv.shape[1]
    quads = width // WIDE
    waits = order.take()
    out = pl.pallas_call(
        cross_backward_kernel,
        grid=(items,),
        in_specs=[
            pl.BlockSpec((1, rows, width), lambda i: (i, 0, 0)),
            pl.BlockSpec((1, keys, 2 * width), lambda i: (i, 0, 0)),
            pl.BlockSpec((1, quads, QUAD * rows, keys), lambda i: (i, 0, 0, 0)),
            pl.BlockSpec((1, rows, width), lambda i: (i, 0, 0)),
            pl.BlockSpec((1, 1, keys), lambda i: (i, 0, 0)),
        ]
        + [pl.BlockSpec(memory_space=pl.ANY)] * len(waits),
        out_specs=[
            pl.BlockSpec((1, rows, width), lambda i: (i, 0, 0)),
            pl.BlockSpec((1, keys, 2 * width), lambda i: (i, 0, 0)),
        ],
        out_shape=[
            jax.ShapeDtypeStruct((items, rows, width), BF16),
            jax.ShapeDtypeStruct((items, keys, 2 * width), BF16),
        ],
        compiler_params=params(),
        cost_estimate=cost(order.long()),
    )(q, kv, probs, grad, mask, *waits)
    order.after(out[0])
    return out


def factor_of(value):
    return lax.rsqrt(jnp.mean(value * value, axis=-1, keepdims=True) + EPSILON)


AXES = {1: "core", 2: "x", 4: "y"}


def swap(value, bit):
    return lax.ppermute(value, AXES[bit], [(0, 1), (1, 0)])


class Order:
    def __init__(self):
        self.waits, self.micros = [], 0.1

    def long(self):
        micros, self.micros = self.micros, 0.1
        return micros

    def take(self):
        waits, self.waits = self.waits, []
        return waits

    def after(self, array):
        self.waits.append(array)
        return array


def hold_kernel(*refs):
    pass


def hold(order, array):
    whole = pl.BlockSpec(memory_space=pl.ANY)
    waits = order.take()
    out = pl.pallas_call(
        hold_kernel,
        in_specs=[whole] * (1 + len(waits)),
        out_specs=whole,
        out_shape=jax.ShapeDtypeStruct(array.shape, array.dtype),
        input_output_aliases={0: 0},
        compiler_params=pltpu.CompilerParams(vmem_limit_bytes=1024 * 1024),
        cost_estimate=cost(order.long()),
    )(array, *waits)
    return order.after(out)


def cost(micros):
    return pl.CostEstimate(
        flops=int(micros * 1.15e9), bytes_accessed=int(micros * 3.6e6), transcendentals=0
    )


def put_split(value, flag, axis, give_ref, keep_ref):
    half = value.shape[axis] // 2
    low, high = (value[:half], value[half:]) if axis == 0 else (value[:, :half], value[:, half:])

    @pl.when(flag == 0)
    def _():
        keep_ref[...] = low
        give_ref[...] = high

    @pl.when(flag > 0)
    def _():
        keep_ref[...] = high
        give_ref[...] = low


def product_kernel(jobs, has_add, axis, halves, flags, *refs):
    outs = refs[-halves * 2 :] if has_add else refs[-1:]
    add_ref = refs[sum(count + 1 for count, _, _ in jobs)]
    at = 0
    total = sum(steps for _, _, steps in jobs)
    for count, start, steps in jobs:
        lefts, right = refs[at : at + count], refs[at + count]
        at += count + 1

        def work(lefts=lefts, right=right, start=start):
            left = jnp.concatenate([r[...] for r in lefts], axis=1)
            value = right[0] if len(right.shape) == 3 else right[...]
            out = dot(left, value, ((0,), (0,)))
            if not has_add:
                outs[0][...] = out.astype(BF16)
                return
            out = (out + add_ref[...].astype(F32)).astype(BF16)
            if axis == 1:
                put_split(out, flags[1], 1, *outs)
                return
            which = 2 * start // total if halves > 1 else 0
            give, keep = outs[2 * which : 2 * which + 2]
            for z in range(give.shape[0]):
                part = out[128 * z : 128 * z + 128]
                put_split(part, flags[1 + which], 0, give.at[z], keep.at[z])

        if len(jobs) == 1:
            work()
        else:
            step = pl.program_id(0)
            pl.when((step >= start) & (step < start + steps))(work)


def call_product(order, axis, grid, jobs, flags, specs, operands, out_specs, out_shapes):
    waits = order.take()
    has_add = len(out_shapes) > 1
    out = pl.pallas_call(
        functools.partial(product_kernel, jobs, has_add, axis, len(out_shapes) // 2),
        grid_spec=pltpu.PrefetchScalarGridSpec(
            num_scalar_prefetch=1,
            grid=grid,
            in_specs=specs + [pl.BlockSpec(memory_space=pl.ANY)] * len(waits),
            out_specs=out_specs,
        ),
        out_shape=out_shapes,
        compiler_params=params(),
        cost_estimate=cost(order.long()),
    )(flags, *operands, *waits)
    order.after(out[0])
    return out


def grad_rows(order, pairs, flags, add=None):
    count = pairs[0][0].shape[1] // 256
    total = sum(columns for _, _, _, columns in pairs)
    tile = next(t for t in (1408, 1024) if all(c % t == 0 for _, _, _, c in pairs))
    specs, operands, jobs, start = [], [], [], 0
    for left, right, place, columns in pairs:
        rows, steps = left.shape[0], columns // tile
        specs += [
            pl.BlockSpec((rows, 128), lambda j, f, z=z: (0, 2 * z + f[0])) for z in range(count)
        ]
        block = lambda j, f, start=start, steps=steps: jnp.clip(j - start, 0, steps - 1)
        if right.ndim == 3:
            specs.append(
                pl.BlockSpec((1, rows, tile), lambda j, f, b=block, p=place: (p, 0, b(j, f)))
            )
        else:
            specs.append(
                pl.BlockSpec((rows, tile), lambda j, f, b=block, p=place: (0, p + b(j, f)))
            )
        operands += [left] * count + [right]
        jobs.append((count, start, steps))
        start += steps
    block = pl.BlockSpec((count * 128, tile), lambda j, f: (0, j))
    if add is None:
        shapes, outs = [jax.ShapeDtypeStruct((count * 128, total), BF16)], [block]
    else:
        specs.append(block)
        operands.append(add)
        halves = flags.shape[0] - 1
        shapes = [jax.ShapeDtypeStruct((count, 64, total // halves), BF16)] * (2 * halves)
        outs, most = [], start // halves
        for i in range(halves):
            place = lambda j, f, i=i: (0, 0, jnp.clip(j - i * most, 0, most - 1))
            outs += [pl.BlockSpec((count, 64, tile), place)] * 2
    return call_product(order, 0, (start,), jobs, flags, specs, operands, outs, shapes)


def grad_columns(order, left, right, flags, add=None):
    rows, width = left.shape
    half = right.shape[1] // 2
    tile = next(t for t in (1408, 1024) if width % t == 0)
    block = lambda columns: pl.BlockSpec((tile, columns), lambda j, f: (j, 0))
    specs = [
        pl.BlockSpec((rows, tile), lambda j, f: (0, j)),
        pl.BlockSpec((rows, half), lambda j, f: (0, f[0])),
    ]
    operands = [left, right]
    if add is None:
        shapes, outs = [jax.ShapeDtypeStruct((width, half), BF16)], [block(half)]
    else:
        specs.append(block(half))
        operands.append(add)
        shapes = [jax.ShapeDtypeStruct((width, half // 2), BF16)] * 2
        outs = [block(half // 2)] * 2
    steps = width // tile
    return call_product(
        order, 1, (steps,), [(1, 0, steps)], flags, specs, operands, outs, shapes
    )


def land_kernel(count, axis, flags, *refs):
    outs = refs[len(refs) - (2 * count if axis is not None else 1) :]
    column = 0
    for i in range(count):
        total = refs[2 * i][...] + refs[2 * i + 1][...]
        if axis is None:
            columns = total.shape[-1]
            outs[0][..., column : column + columns] = total
            column += columns
        elif axis == 1:
            put_split(total, flags[i], 1, *outs[2 * i : 2 * i + 2])
        else:
            for z in range(total.shape[0]):
                put_split(
                    total[z], flags[i], 0, outs[2 * i].at[z], outs[2 * i + 1].at[z]
                )


def land_sums(order, pairs, flags, axis):
    waits = order.take()
    steps = 2
    block = lambda shape: pl.BlockSpec(
        (shape[0] // steps, *shape[1:]), lambda j, f: (j,) + (0,) * (len(shape) - 1)
    )
    specs, operands, shapes = [], [], []
    for keep, got in pairs:
        specs += [block(keep.shape)] * 2
        operands += [keep, got]
        shape = list(keep.shape)
        if axis is not None:
            shape[-2 if axis == 0 else -1] //= 2
            shapes += [tuple(shape)] * 2
    if axis is None:
        total = sum(keep.shape[-1] for keep, _ in pairs)
        shapes = [(*pairs[0][0].shape[:-1], total)]
    out = pl.pallas_call(
        functools.partial(land_kernel, len(pairs), axis),
        grid_spec=pltpu.PrefetchScalarGridSpec(
            num_scalar_prefetch=1,
            grid=(steps,),
            in_specs=specs + [pl.BlockSpec(memory_space=pl.ANY)] * len(waits),
            out_specs=[block(shape) for shape in shapes],
        ),
        out_shape=[jax.ShapeDtypeStruct(shape, BF16) for shape in shapes],
        compiler_params=params(),
        cost_estimate=cost(order.long()),
    )(jnp.stack(flags), *operands, *waits)
    order.after(out[0])
    return out


def join_kernel(axis, parts, turned, flag, own_ref, got_ref, *refs):
    outs = refs[len(refs) - len(parts) :]
    half = own_ref.shape[axis]

    def put(low, high):
        column = 0
        for out, columns, turn in zip(outs, parts, turned):
            at = slice(column, column + columns)
            column += columns
            for start, ref in ((0, low), (half, high)):
                value = ref[:, at].astype(out.dtype)
                if axis == 1:
                    out[:, start : start + half] = value
                elif turn:
                    n = half // 4
                    for i, j in enumerate((0, 2, 1, 3)):
                        out[start + j * n : start + (j + 1) * n] = value[i * n : (i + 1) * n]
                else:
                    out[start : start + half] = value

    either(flag[0], put, own_ref, got_ref)


def land_join(order, own, got, flag, axis, parts, turned, kind):
    waits = order.take()
    whole = lambda shape: pl.BlockSpec(shape, lambda j, f: (0, 0))
    n, c = own.shape
    shapes = [(2 * n, columns) for columns in parts] if axis == 0 else [(n, 2 * c)]
    out = pl.pallas_call(
        functools.partial(join_kernel, axis, parts, turned),
        grid_spec=pltpu.PrefetchScalarGridSpec(
            num_scalar_prefetch=1,
            grid=(1,),
            in_specs=[whole(own.shape)] * 2 + [pl.BlockSpec(memory_space=pl.ANY)] * len(waits),
            out_specs=[whole(shape) for shape in shapes],
        ),
        out_shape=[jax.ShapeDtypeStruct(shape, kind) for shape in shapes],
        compiler_params=params(),
        cost_estimate=cost(order.long()),
    )(flag.reshape(1), own, got, *waits)
    order.after(out[0])
    return out


def segment_kernel(steps, has_next, split, waits, flag, *refs):
    x_ref, w_ref, v_ref, b_ref, g_ref = refs[:5]
    n_refs = refs[5 : 5 + 2 * has_next]
    u_ref = refs[5 + 2 * has_next] if split else None
    refs = refs[5 + 2 * has_next + split + waits :]
    if has_next:
        d_ref, gg_ref, e_ref, o_ref, acc = refs
    else:
        d_ref, gg_ref, acc = refs
    step = pl.program_id(0)
    x = x_ref[0] if len(x_ref.shape) == 3 else x_ref[...]
    size = w_ref.shape[0]
    for at, ref in ((0, w_ref), (size, u_ref)):
        if ref is None:
            continue
        partial = dot(x, ref[...], ((1,), (1,)))

        @pl.when(step == 0)
        def _(at=at, partial=partial):
            acc[:, at : at + size] = partial

        @pl.when(step > 0)
        def _(at=at, partial=partial):
            acc[:, at : at + size] += partial

    @pl.when(step == steps - 1)
    def _():
        gain = g_ref[...]
        rows, chunk = acc.shape[0], 144
        gg_ref[...] = jnp.zeros_like(gg_ref)

        @pl.loop(0, rows // chunk)
        def _(i):
            at = pl.ds(pl.multiple_of(i * chunk, chunk), chunk)
            grad = acc[at, :]
            if split:
                own, other = grad[:, :size], grad[:, size:]
                low, high = jnp.where(flag[0] == 0, own, other), jnp.where(flag[0] == 0, other, own)
                blocks = []
                for k in range(0, size, 128):
                    blocks += [low[:, k : k + 128], high[:, k : k + 128]]
                grad = jnp.concatenate(blocks, axis=1)
            value = v_ref[at, :].astype(F32)
            factor = lax.rsqrt(jnp.mean(value * value, axis=-1, keepdims=True) + EPSILON)
            scaled = gain * grad
            along = jnp.mean(scaled * value, axis=-1, keepdims=True)
            back = factor * scaled - value * (factor * factor * factor * along)
            gg_ref[...] += jnp.sum(grad * value * factor, axis=0, keepdims=True)
            total = b_ref[at, :].astype(F32) + back
            d_ref[at, :] = total
            if has_next:
                e_ref[at, :] = total.astype(BF16)

        if has_next:
            matrix = interleaved(flag[0], n_refs[0][...], n_refs[1][...])
            o_ref[...] = dot(e_ref[...], matrix, ((1,), (1,))).astype(BF16)


def segment(order, core, x, w, column, tile, value, base, gain, after=None):
    rows, width = value.shape
    steps = x.shape[-1] * (x.shape[0] if x.ndim == 3 else 1) // tile
    if x.ndim == 3:
        per = x.shape[-1] // tile
        x_spec = pl.BlockSpec((1, rows, tile), lambda k, f: (k // per, 0, k % per))
    else:
        x_spec = pl.BlockSpec((rows, tile), lambda k, f: (0, k))
    whole = pl.BlockSpec((rows, width), lambda k, f: (0, 0))
    line = pl.BlockSpec((1, width), lambda k, f: (0, 0))
    split = isinstance(w, tuple)
    w = w if split else (w,)
    w_spec = pl.BlockSpec((w[0].shape[0], tile), lambda k, f: (0, k + column))
    specs = [x_spec, w_spec, whole, whole, line]
    operands = [x, w[0], value, base, gain.reshape(1, width)]
    shapes = [
        jax.ShapeDtypeStruct((rows, width), F32),
        jax.ShapeDtypeStruct((1, width), F32),
    ]
    outs = [whole, line]
    if after is not None:
        matrix, at = after
        specs += [pl.BlockSpec((width // 2, width), lambda k, f: (0, at))] * 2
        operands += matrix
        shapes += [jax.ShapeDtypeStruct((rows, width), BF16)] * 2
        outs += [whole, whole]
    if split:
        specs.append(w_spec)
        operands.append(w[1])
    waits = order.take()
    out = pl.pallas_call(
        functools.partial(segment_kernel, steps, after is not None, split, len(waits)),
        grid_spec=pltpu.PrefetchScalarGridSpec(
            num_scalar_prefetch=1,
            grid=(steps,),
            in_specs=specs + [pl.BlockSpec(memory_space=pl.ANY)] * len(waits),
            out_specs=outs,
            scratch_shapes=[pltpu.VMEM((rows, width), F32)],
        ),
        out_shape=shapes,
        compiler_params=params(),
        cost_estimate=cost(order.long()),
    )(core.reshape(1), *operands, *waits)
    order.after(out[1])
    return out


def halves_of(value):
    starts = range(0, value.shape[1], 256)
    return [
        jnp.concatenate([value[:, k + j : k + j + 128] for k in starts], axis=1)
        for j in (0, 128)
    ]


def mlp_kernel(flag, a_ref, e_ref, wg_ref, wu_ref, vg_ref, vu_ref, wd_ref, i_ref, d_ref, mine):
    @pl.when(pl.program_id(0) == 0)
    def _():
        def put(own, other):
            mine[0] = own
            mine[1] = other

        either(flag[0], put, *halves_of(a_ref[...]))

    grad = dot(e_ref[...], wd_ref[...], ((1,), (1,)))
    product = lambda w, v: dot(mine[0], w[...], ((1,), (0,))) + dot(mine[1], v[...], ((1,), (0,)))
    gate, up = product(wg_ref, vg_ref), product(wu_ref, vu_ref)
    slope, cubic = 0.7978845608028654, 0.044715
    square = gate * gate
    bend = jnp.tanh(slope * gate * (1.0 + cubic * square))
    half = 0.5 * (1.0 + bend)
    act = gate * half
    turn = half + 0.5 * gate * (1.0 - bend * bend) * slope * (1.0 + 3.0 * cubic * square)
    i_ref[...] = (act * up).astype(BF16)
    d_ref[0] = (grad * up * turn).astype(BF16)
    d_ref[1] = (grad * act).astype(BF16)


def mlp(order, core, a3, e3, own, other, w_down):
    rows, width = a3.shape
    hidden = w_down.shape[0]
    tile = MLP_TILE
    count = hidden // tile
    whole = pl.BlockSpec((rows, width), lambda j, f: (0, 0))
    gate = pl.BlockSpec((width // 2, tile), lambda j, f: (0, j))
    up = pl.BlockSpec((width // 2, tile), lambda j, f: (0, count + j))
    return pl.pallas_call(
        mlp_kernel,
        grid_spec=pltpu.PrefetchScalarGridSpec(
            num_scalar_prefetch=1,
            grid=(count,),
            in_specs=[
                whole,
                whole,
                gate,
                up,
                gate,
                up,
                pl.BlockSpec((tile, width), lambda j, f: (j, 0)),
            ],
            out_specs=[
                pl.BlockSpec((rows, tile), lambda j, f: (0, j)),
                pl.BlockSpec((2, rows, tile), lambda j, f: (0, 0, j)),
            ],
            scratch_shapes=[pltpu.VMEM((2, rows, width // 2), BF16)],
        ),
        out_shape=[
            jax.ShapeDtypeStruct((rows, hidden), BF16),
            jax.ShapeDtypeStruct((2, rows, hidden), BF16),
        ],
        compiler_params=params(),
        cost_estimate=cost(order.long()),
    )(core.reshape(1), a3, e3, own, own, other, other, w_down)


def sorted_halves(flag, value):
    low, high = halves_of(value)
    return jnp.where(flag == 0, low, high), jnp.where(flag == 0, high, low)


def interleaved(flag, own, other):
    low, high = jnp.where(flag == 0, own, other), jnp.where(flag == 0, other, own)
    blocks = []
    for k in range(0, own.shape[0], 128):
        blocks += [low[k : k + 128], high[k : k + 128]]
    return jnp.concatenate(blocks, axis=0)


def project_kernel(flag, x_ref, own_ref, other_ref, *refs):
    out_ref, mine = refs[-2:]

    @pl.when(pl.program_id(0) == 0)
    def _():
        mine[0], mine[1] = sorted_halves(flag[0], x_ref[...])

    out = dot(mine[0], own_ref[...], ((1,), (0,))) + dot(mine[1], other_ref[...], ((1,), (0,)))
    out_ref[...] = out.astype(BF16)


def project(order, core, x, w, column, count):
    rows, width = x.shape
    waits = order.take()
    w_spec = pl.BlockSpec((width // 2, width), lambda j, f: (0, j + column))
    out = pl.pallas_call(
        project_kernel,
        grid_spec=pltpu.PrefetchScalarGridSpec(
            num_scalar_prefetch=1,
            grid=(count,),
            in_specs=[pl.BlockSpec((rows, width), lambda j, f: (0, 0)), w_spec, w_spec]
            + [pl.BlockSpec(memory_space=pl.ANY)] * len(waits),
            out_specs=pl.BlockSpec((rows, width), lambda j, f: (0, j)),
            scratch_shapes=[pltpu.VMEM((2, rows, width // 2), BF16)],
        ),
        out_shape=jax.ShapeDtypeStruct((rows, count * width), BF16),
        compiler_params=params(),
        cost_estimate=cost(order.long()),
    )(core.reshape(1), x, *w, *waits)
    return order.after(out)


def forward_norm_kernel(flag, x_ref, own_ref, other_ref, b_ref, g_ref, *refs):
    h_ref, a_ref = refs[-2:]
    mine, yours = sorted_halves(flag[0], x_ref[...])
    h_ref[...] = dot(mine, own_ref[...], ((1,), (0,))) + dot(
        yours, other_ref[...], ((1,), (0,))
    )
    gain = g_ref[...]
    rows, chunk = h_ref.shape[0], 144

    @pl.loop(0, rows // chunk)
    def _(i):
        at = pl.ds(pl.multiple_of(i * chunk, chunk), chunk)
        value = h_ref[at, :] + b_ref[at, :].astype(F32)
        h_ref[at, :] = value
        factor = lax.rsqrt(jnp.mean(value * value, axis=-1, keepdims=True) + EPSILON)
        a_ref[at, :] = (value * factor * gain).astype(BF16)


def forward_norm(order, core, x, w, column, base, gain):
    rows, width = x.shape
    waits = order.take()
    whole = pl.BlockSpec((rows, width), lambda j, f: (0, 0))
    w_spec = pl.BlockSpec((width // 2, width), lambda j, f: (0, column))
    out = pl.pallas_call(
        forward_norm_kernel,
        grid_spec=pltpu.PrefetchScalarGridSpec(
            num_scalar_prefetch=1,
            grid=(1,),
            in_specs=[
                whole,
                w_spec,
                w_spec,
                whole,
                pl.BlockSpec((1, width), lambda j, f: (0, 0)),
            ]
            + [pl.BlockSpec(memory_space=pl.ANY)] * len(waits),
            out_specs=[whole, whole],
        ),
        out_shape=[
            jax.ShapeDtypeStruct((rows, width), F32),
            jax.ShapeDtypeStruct((rows, width), BF16),
        ],
        compiler_params=params(),
        cost_estimate=cost(order.long()),
    )(core.reshape(1), x, *w, base, gain.reshape(1, width), *waits)
    order.after(out[1])
    return out


def forward_out_kernel(steps, waits, x_ref, w_ref, b_ref, *refs):
    o_ref, acc = refs[waits:]
    step = pl.program_id(0)
    partial = dot(x_ref[...], w_ref[...], ((1,), (0,)))

    @pl.when(step == 0)
    def _():
        acc[...] = partial + b_ref[...]

    @pl.when(step > 0)
    def _():
        acc[...] += partial

    @pl.when(step == steps - 1)
    def _():
        o_ref[...] = acc[...].astype(BF16)


def forward_out(order, x, w, base):
    rows, width = base.shape
    tile = next(t for t in (1408, 1024) if w.shape[0] % t == 0)
    steps = w.shape[0] // tile
    whole = pl.BlockSpec((rows, width), lambda k: (0, 0))
    waits = order.take()
    out = pl.pallas_call(
        functools.partial(forward_out_kernel, steps, len(waits)),
        grid=(steps,),
        in_specs=[
            pl.BlockSpec((rows, tile), lambda k: (0, k)),
            pl.BlockSpec((tile, width), lambda k: (k, 0)),
            whole,
        ]
        + [pl.BlockSpec(memory_space=pl.ANY)] * len(waits),
        out_specs=whole,
        out_shape=jax.ShapeDtypeStruct((rows, width), BF16),
        scratch_shapes=[pltpu.VMEM((rows, width), F32)],
        compiler_params=params(),
        cost_estimate=cost(order.long()),
    )(x, w, base, *waits)
    return order.after(out)


def back_product_kernel(flag, x_ref, own_ref, other_ref, *refs):
    w = interleaved(flag[0], own_ref[...], other_ref[...])
    refs[-1][...] = dot(x_ref[...], w, ((1,), (1,)))


def back_product(order, core, x, w):
    rows, depth = x.shape
    half = w[0].shape[0]
    waits = order.take()
    w_spec = pl.BlockSpec((128, depth), lambda j, f: (j, 0))
    out = pl.pallas_call(
        back_product_kernel,
        grid_spec=pltpu.PrefetchScalarGridSpec(
            num_scalar_prefetch=1,
            grid=(half // 128,),
            in_specs=[pl.BlockSpec((rows, depth), lambda j, f: (0, 0)), w_spec, w_spec]
            + [pl.BlockSpec(memory_space=pl.ANY)] * len(waits),
            out_specs=pl.BlockSpec((rows, 256), lambda j, f: (0, j)),
        ),
        out_shape=jax.ShapeDtypeStruct((rows, 2 * half), F32),
        compiler_params=params(),
        cost_estimate=cost(order.long()),
    )(core.reshape(1), x, *w, *waits)
    return order.after(out)


def bit_of(spot, bit):
    return (spot // bit) % 2


class Sum:
    def __init__(self, order, spot, axis, product, first, second):
        self.order, self.axis, self.product = order, axis, product
        self.first, self.second = first, second
        self.bits = bit_of(spot, 1), bit_of(spot, first), bit_of(spot, second)
        core, one, _ = self.bits
        (give,) = product(jnp.stack([1 - core, one]))
        self.flight = swap(give, 1)

    def core(self):
        core, one, _ = self.bits
        give, self.keep = self.product(jnp.stack([core, one]), self.flight)
        self.flight = swap(give, self.first)


class Part:
    def __init__(self, spot, first, second):
        self.first, self.second, self.axis = first, second, 0
        self.bits = bit_of(spot, 1), bit_of(spot, first), bit_of(spot, second)


class Pair:
    def __init__(self, order, spot, pairs):
        self.product = functools.partial(grad_rows, order, pairs)
        self.parts = [Part(spot, 2, 4), Part(spot, 4, 2)]
        self.flags = [bit_of(spot, b) for b in (1, 2, 4)]
        core, one, two = self.flags
        (give,) = self.product(jnp.stack([1 - core, one, two]))
        self.flight = swap(give, 1)

    def core(self):
        core, one, two = self.flags
        out = self.product(jnp.stack([core, one, two]), self.flight)
        for i, part in enumerate(self.parts):
            part.keep = out[2 * i + 1]
            part.flight = swap(out[2 * i], part.first)
        return self.parts


def region(axis, first, cross):
    return (first, cross) if axis == 0 else (cross, first)


def either(flag, put, one, two):
    pl.when(flag == 0)(lambda: put(one, two))
    pl.when(flag > 0)(lambda: put(two, one))


def cut_kernel(axis, z_ref, *refs):
    a_ref, b_ref = refs[-2:]
    half = z_ref.shape[2 - axis] // 2
    a_ref[0] = z_ref.at[0][region(axis, slice(None), slice(0, half))]
    b_ref[0] = z_ref.at[0][region(axis, slice(None), slice(half, None))]


def cut(order, value, axis, column, columns):
    waits = order.take()
    z, n, _ = value.shape
    shape = (z, n, columns // 2) if axis == 0 else (z, n // 2, columns)
    out = pl.pallas_call(
        functools.partial(cut_kernel, axis),
        grid=(z,),
        in_specs=[pl.BlockSpec((1, n, columns), lambda j: (j, 0, column))]
        + [pl.BlockSpec(memory_space=pl.ANY)] * len(waits),
        out_specs=[pl.BlockSpec((1, *shape[1:]), lambda j: (j, 0, 0))] * 2,
        out_shape=[jax.ShapeDtypeStruct(shape, BF16)] * 2,
        compiler_params=params(),
        cost_estimate=cost(order.long()),
    )(value, *waits)
    order.after(out[0])
    return out


def pack_kernel(tall, place, *refs):
    refs = list(refs)
    if tall:
        last_in, last_out = refs.pop(len(refs) - 3), refs.pop()
        last_out[...] = last_in[...]
    column = 0
    for ref in refs[:-1]:
        refs[-1][:, column : column + ref.shape[1]] = ref[...]
        column += ref.shape[1]


def pack(shards, seats, pieces, last=None, tall=None):
    n = shards[0].shape[0] // pieces
    specs = [
        pl.BlockSpec((n, w.shape[1]), lambda j, f, i=i: (f[i % len(seats)], 0))
        for i, w in enumerate(shards)
    ]
    total = sum(w.shape[1] for w in shards)
    operands = list(shards)
    if last is not None:
        specs.append(pl.BlockSpec(last.shape, lambda j, f: (0, 0)))
        operands.append(last)
        total += last.shape[1]
    outs, shapes = [pl.BlockSpec((n, total), lambda j, f: (0, 0))], [(n, total)]
    if tall is not None:
        piece = (tall.shape[0], tall.shape[1] // 8)
        specs.append(pl.BlockSpec(piece, lambda j, f: (0, f[0])))
        operands.append(tall)
        outs.append(pl.BlockSpec(piece, lambda j, f: (0, 0)))
        shapes.append(piece)
    return pl.pallas_call(
        functools.partial(pack_kernel, tall is not None),
        grid_spec=pltpu.PrefetchScalarGridSpec(
            num_scalar_prefetch=1, grid=(1,), in_specs=specs, out_specs=outs
        ),
        out_shape=[jax.ShapeDtypeStruct(shape, BF16) for shape in shapes],
        compiler_params=params(),
        cost_estimate=cost(1),
    )(jnp.stack(seats), *operands)


def pairs_kernel(axis, flags, *refs):
    ins, outs = refs[:4], refs[-2:]
    for i in range(2):
        size = ins[2 * i].shape[1 + axis]

        def put(low, high, out=outs[i], size=size):
            out.at[0][region(axis, slice(0, size), slice(None))] = low[0]
            out.at[0][region(axis, slice(size, None), slice(None))] = high[0]

        either(flags[i], put, ins[2 * i], ins[2 * i + 1])


def quads_kernel(axis, flags, *refs):
    a_own, a_got, b_own, b_got = refs[:4]
    out = refs[-1].at[0]
    two, half = a_own.shape[1 + axis], a_own.shape[2 - axis]
    n = two // 2

    def put_a(low, high):
        out[region(axis, slice(0, two), slice(0, half))] = low[0]
        out[region(axis, slice(two, None), slice(0, half))] = high[0]

    def put_b(low, high):
        for y in range(2):
            for x, ref in enumerate((low, high)):
                at = (2 * y + x) * n
                out[region(axis, slice(at, at + n), slice(half, None))] = ref.at[0][
                    region(axis, slice(y * n, y * n + n), slice(None))
                ]

    either(flags[1], put_a, a_own, a_got)
    either(flags[0], put_b, b_own, b_got)


def sides_kernel(axis, flags, *refs):
    a_own, a_got, b_own, b_got = refs[:4]
    out = refs[-1].at[0]
    n, half = a_own.shape[1], a_own.shape[2]

    def put_in(columns):
        def put(low, high):
            out[:n, columns] = low[0]
            out[n:, columns] = high[0]

        return put

    either(flags[0], put_in(slice(0, half)), a_own, a_got)
    either(flags[1], put_in(slice(half, None)), b_own, b_got)


def cores_kernel(axis, flags, own_ref, got_ref, *refs):
    out = refs[-1].at[0]
    size = own_ref.shape[1 + axis]

    def put(low, high):
        out[region(axis, slice(0, size), slice(None))] = low[0]
        out[region(axis, slice(size, None), slice(None))] = high[0]

    either(flags[2], put, own_ref, got_ref)


def by_shard(order, kernel, axis, flags, operands, shapes):
    waits = order.take()
    block = lambda shape: pl.BlockSpec((1, *shape[1:]), lambda j, *f: (j, 0, 0))
    out = pl.pallas_call(
        functools.partial(kernel, axis),
        grid_spec=pltpu.PrefetchScalarGridSpec(
            num_scalar_prefetch=len(flags),
            grid=(operands[0].shape[0],),
            in_specs=[block(v.shape) for v in operands]
            + [pl.BlockSpec(memory_space=pl.ANY)] * len(waits),
            out_specs=[block(shape) for shape in shapes],
        ),
        out_shape=[jax.ShapeDtypeStruct(shape, BF16) for shape in shapes],
        compiler_params=params(),
        cost_estimate=cost(order.long()),
    )(*flags, *operands, *waits)
    order.after(out[0])
    return out


class Gather:
    def __init__(self, order, spot, value, axis, column=0, columns=None):
        self.order, self.axis = order, axis
        self.flags = [jnp.stack([bit_of(spot, b) for b in (2, 4, 1)])]
        self.value, self.place = value, (column, columns or value.shape[2])

    def scaled(self, shape, along, across):
        shape = list(shape)
        shape[1 + self.axis] = shape[1 + self.axis] * along
        shape[2 - self.axis] = shape[2 - self.axis] * across // 2
        return tuple(shape)

    def run(self, kernel, flags, operands, shapes):
        return by_shard(self.order, kernel, self.axis, flags, operands, shapes)

    def one(self):
        self.a, self.b = cut(self.order, self.value, self.axis, *self.place)
        self.got = swap(self.a, 2), swap(self.b, 4)

    def two(self):
        shape = self.scaled(self.a.shape, 2, 2)
        self.a, self.b = self.run(
            pairs_kernel, self.flags, [self.a, self.got[0], self.b, self.got[1]], [shape] * 2
        )
        self.got = swap(self.a, 4), swap(self.b, 2)

    def three(self):
        shape = self.scaled(self.a.shape, 2, 4)
        (self.half,) = self.run(
            quads_kernel, self.flags, [self.a, self.got[0], self.b, self.got[1]], [shape]
        )
        self.got = swap(self.half, 1)

    def side(self):
        shape = self.scaled(self.a.shape, 2, 4)
        (self.half,) = self.run(
            sides_kernel, self.flags, [self.a, self.got[0], self.b, self.got[1]], [shape]
        )
        self.got = swap(self.half, 1)

    def halves(self):
        flat = lambda value: value.reshape(-1, value.shape[-1])
        return flat(self.half), flat(self.got)

    def four(self):
        shape = self.scaled(self.half.shape, 2, 2)
        (whole,) = self.run(cores_kernel, self.flags, [self.half, self.got], [shape])
        return whole.reshape(-1, whole.shape[-1])


def land_first(order, *sums):
    out = land_sums(
        order, [(s.keep, s.flight) for s in sums], [s.bits[2] for s in sums], sums[0].axis
    )
    for i, s in enumerate(sums):
        s.keep = out[2 * i + 1]
        s.flight = swap(out[2 * i], s.second)


def land_second(order, *sums):
    (out,) = land_sums(
        order, [(s.keep, s.flight) for s in sums], [s.bits[2] for s in sums], None
    )
    return out.reshape(-1, out.shape[-1])


def over_shards(value):
    value = lax.psum_scatter(value, "fsdp", scatter_dimension=0, tiled=True)
    return across_groups(value)


def across_groups(value):
    size = lax.axis_size("group")
    ring = [(i, (i + 1) % size) for i in range(size)]
    total = step = value
    for _ in range(size - 1):
        step = lax.ppermute(step, "group", ring)
        total = total + step
    return total


class Spread:
    def __init__(self, order, spot, value, parts, turned, axis=0):
        self.order, self.spot, self.axis = order, spot, axis
        self.value, self.parts, self.turned = value, parts, turned
        self.bits = [4, 2, 1]
        self.send()

    def send(self):
        self.flight = swap(self.value, self.bits[0])

    def land(self):
        bit = self.bits.pop(0)
        last = not self.bits
        out = land_join(
            self.order,
            self.value,
            self.flight,
            bit_of(self.spot, bit),
            self.axis,
            self.parts if last else [self.value.shape[1]],
            self.turned if last else [False],
            F32 if last else BF16,
        )
        if last:
            self.values = out
        else:
            self.value = out[0]
            self.send()


def on_device(
    text,
    memory,
    text_lengths,
    memory_mask,
    grad_out,
    self_gain,
    self_query,
    self_key,
    self_value,
    self_output,
    cross_gain,
    cross_query,
    cross_key,
    cross_value,
    cross_output,
    mlp_gain,
    mlp_gate,
    mlp_up,
    mlp_down,
):
    items, rows, width = text.shape
    keys = memory.shape[1]
    spot = 4 * lax.axis_index("y") + 2 * lax.axis_index("x") + lax.axis_index("core")

    order = Order()
    gather = lambda value: lax.all_gather(value, "fsdp", axis=0)
    own = self_gain.shape[0]
    lines = jnp.stack([self_gain, cross_gain, mlp_gain]).reshape(-1, 128)
    squares = [
        self_query,
        self_key,
        self_value,
        self_output,
        cross_key,
        cross_value,
        cross_query,
        cross_output,
    ]
    lines = jnp.pad(lines, ((0, width // 32 - lines.shape[0]), (0, 0)))
    x_bit, y_bit, core = (bit_of(spot, b) for b in (2, 4, 1))
    seat = 4 * core + 2 * y_bit + x_bit
    piece, piece_down = pack(squares, [seat], 8, lines, mlp_down)
    both = gather(piece)
    g_down = Gather(order, spot, gather(piece_down), 1)
    g_self = Gather(order, spot, both, 0, 0, 4 * width)
    g_cross = Gather(order, spot, both, 0, 1, 4 * width)
    shards = both.shape[0]
    gains = both[:, : 3 * own // 128, 8 * width :].reshape(shards, 3, own)
    gains = gains.transpose(1, 0, 2).reshape(3, width).astype(F32)
    g_wide = Gather(order, spot, gather(*pack([mlp_gate, mlp_up], [2 * core + x_bit, 2 * core + y_bit], 4)), 0)
    hidden = mlp_gate.shape[1]

    x = text.reshape(-1, width).astype(F32)
    flat_memory = memory.reshape(-1, width)
    e3 = grad_out.reshape(-1, width)
    mask = memory_mask[:, None, :]

    g_down.one()
    g_down.two()
    g_self.one()
    g_cross.one()
    order.micros = C_LONG
    g_down.three()
    g_self.two()
    g_cross.two()
    order.micros = C_LONG
    w_down = g_down.four()
    g_self.three()
    w_self = g_self.halves()
    c1 = factor_of(x)
    a1 = (x * c1 * gains[0]).astype(BF16)
    qkv = project(order, core, a1, w_self, 0, 3).reshape(items, rows, 3 * width)
    o1, p1 = self_forward(qkv, text_lengths)
    o1 = order.after(o1).reshape(-1, width)
    g_wide.one()
    g_cross.three()
    w_cross = g_cross.halves()
    order.micros = C_LONG
    h1, a2 = forward_norm(order, core, o1, w_self, 3, x, gains[1])
    kv = project(order, core, flat_memory, w_cross, 0, 2).reshape(items, keys, 2 * width)
    q2 = project(order, core, a2, w_cross, 2, 1).reshape(items, rows, width)
    o2, p2 = cross_forward(q2, kv, mask)
    o2 = order.after(o2).reshape(-1, width)
    g_wide.side()
    h2, a3 = forward_norm(order, core, o2, w_cross, 3, h1, gains[2])
    w_wide = g_wide.halves()
    inner, d_wide = mlp(order, core, a3, e3, *w_wide, w_down)
    order.take()

    s_wide = Pair(order, spot, [(a3, d_wide, 0, hidden), (a3, d_wide, 1, hidden)])
    s_down = Sum(order, spot, 1, functools.partial(grad_columns, order, inner, e3), 2, 4)
    wide = s_wide.core()
    s_down.core()
    order.micros = C_LONG
    d_h2, gg3, e2, d_o2 = segment(
        order, core, d_wide, w_wide, 0, hidden, h2, e3, gains[2], (w_cross, 3)
    )
    d_q2, d_kv = cross_backward(order, q2, kv, p2, d_o2.reshape(text.shape), mask)
    d_q2 = d_q2.reshape(-1, width)
    d_kv = d_kv.reshape(-1, 2 * width)
    s_cross = Pair(
        order,
        spot,
        [
            (flat_memory, d_kv, 0, 2 * width),
            (a2, d_q2, 0, width),
            (o2, e2, 0, width),
        ],
    )
    land_first(order, *wide)
    order.micros = C_SEG2
    d_h1, gg2, e1, d_o1 = segment(
        order, core, d_q2, w_cross, 2, width, h1, d_h2, gains[1], (w_self, 3)
    )
    land_first(order, s_down)
    order.micros = C_LONG
    z_wide = land_second(order, *wide)
    cross = s_cross.core()
    z_down = land_second(order, s_down)
    order.micros = C_LONG
    d_qkv = self_backward(order, qkv, p1, d_o1.reshape(text.shape)).reshape(-1, 3 * width)
    s_self = Pair(
        order,
        spot,
        [
            (a1, d_qkv, 0, 2 * width),
            (a1, d_qkv, 2, width),
            (o1, e1, 0, width),
        ],
    )
    land_first(order, *cross)
    z_wide = over_shards(z_wide)
    order.micros = C_LONG
    grad_text, gg1 = segment(order, core, d_qkv, w_self, 0, width, x, d_h1, gains[0])
    z_wide = hold(order, z_wide)
    z_down = over_shards(z_down)
    t_wide = Spread(order, spot, z_wide, [hidden, hidden], [False, True])
    both = s_self.core()
    z_cross = land_second(order, *cross)
    order.micros = C_LONG
    grad_memory = back_product(order, core, d_kv, w_cross)
    z_down = hold(order, z_down)
    z_cross = over_shards(z_cross)
    land_first(order, *both)
    lines = jnp.concatenate([gg1, gg2, gg3]).reshape(3, shards, own).transpose(1, 0, 2)
    lines = lines.reshape(shards, -1, 128)
    lines = jnp.pad(lines, ((0, 0), (0, width // 32 - lines.shape[1]), (0, 0)))
    lines = order.after(lines.astype(BF16).reshape(-1, 128))
    z_self = land_second(order, *both)
    z_self = order.after(jnp.concatenate([z_self, lines], axis=1))
    z_cross = hold(order, z_cross)
    z_self = over_shards(z_self)
    squares = [width] * 4
    t_wide.land()
    t_down = Spread(order, spot, z_down, [width], [False], 1)
    t_cross = Spread(order, spot, z_cross, squares, [False, False, True, True])
    block_out = forward_out(order, inner, w_down, h2)
    t_down.land()
    t_cross.land()
    t_wide.land()
    z_self = hold(order, z_self)
    t_self = Spread(
        order, spot, z_self, [*squares, 128], [False, False, True, True, False]
    )
    t_down.land()
    t_wide.land()
    t_cross.land()
    t_self.land()
    t_down.land()
    t_self.land()
    t_cross.land()
    t_self.land()
    g_gate, g_up = t_wide.values
    (g_down,) = t_down.values
    g_ck, g_cv, g_cq, g_co = t_cross.values
    g_sq, g_sk, g_sv, g_so, lines = t_self.values
    lines = jnp.sum(lines.reshape(8, -1, 128), axis=0)
    gg = lines[: 3 * own // 128].reshape(3, own)

    return (
        block_out.reshape(text.shape),
        grad_text.reshape(text.shape),
        grad_memory.reshape(memory.shape),
        gg[0],
        g_sq,
        g_sk,
        g_sv,
        g_so,
        gg[1],
        g_cq,
        g_ck,
        g_cv,
        g_co,
        gg[2],
        g_gate,
        g_up,
        g_down,
    )


def solution(mesh):
    shape = mesh.devices.shape
    mesh = jax.sharding.Mesh(
        mesh.devices.reshape(shape[0] // 8, 2, 2, 2, shape[1]),
        ("group", "y", "x", "core", "fsdp"),
    )
    every = ("group", "y", "x", "core", "fsdp")
    rows = P(every, None, None)
    gain, weight = P("fsdp"), P("fsdp", None)
    weights = (gain, weight, weight, weight, weight) * 2 + (gain, weight, weight, weight)
    return jax.shard_map(
        on_device,
        mesh=mesh,
        in_specs=(rows, rows, P(every), P(every, None), rows) + weights,
        out_specs=(rows, rows, rows) + weights,
        check_vma=False,
    )
```
